1024 devices in a mesh: gx: 8 (over y), gy: 16 (over z), gz: 8 (over x, core).
Axes of the slice: x: 4, y: 8, z: 16, core: 2. Of those that a mesh axis runs over, the one named last changes fastest.
Arguments:
- right_side: float32 [32, 32, 4096], P('gx', 'gy', 'gz'), may hold values from -24 to 24
- element_class: int32 [32, 32, 64], P('gx', 'gy', 'gz'), may hold values from 0 to 15
- class_blocks: float32 [16, 64, 64], replicated, may hold values from -0.05 to 11, as said below
- class_shift: float32 [16], replicated, may hold values from 0.5 to 4
- face_weights: float32 [3], replicated, may hold values from 0.4 to 0.9
Outputs:
- solution_field: float32 [32, 32, 4096], P('gx', 'gy', 'gz')
- residual: float32 [32, 32, 4096], P('gx', 'gy', 'gz')
The draws below stay inside these ranges and needn't reach their ends.
Inputs may be any that keep to these rules, and one draw needn't show every extreme that they name: `class_blocks`: each block is symmetric, and each diagonal entry exceeds the sum of magnitudes of the other entries of its row by 3 or more.
All inputs are finite; a program needn't handle non-finite values.
Results may differ from the reference program's by a relative error of at most 0.00027.
Values sent between devices are 32-bit elements; how exact they have to be, the bound alone decides.
No kernel may reach another device: no remote copies, remote signals or barrier semaphores. Data moves between devices by JAX's collectives and lax.ppermute only.
A program may use at most 32 MiB of HBM per device.

```python
import math
import jax
import jax.numpy as jnp
from jax import lax

CX = 4
CY = 2
CZ = 8
P_SIZE = 64
K = 16
SWEEPS = 4
NX = 32
NY = 32
NZ = 64
N_GX = 8
N_GY = 16
N_GZ = 8


def draw_class_blocks(key, part):
    key = jax.random.fold_in(key, 11)
    first_key, second_key = jax.random.split(key)
    raw_entries = jax.random.uniform(first_key, (K, P_SIZE, P_SIZE), jnp.float32, -0.05, 0.05)
    symmetric = 0.5 * (raw_entries + jnp.swapaxes(raw_entries, 1, 2))
    identity = jnp.eye(P_SIZE, dtype=jnp.float32)
    margin = jax.random.uniform(second_key, (K, P_SIZE), jnp.float32, 1.0, 4.0)
    diagonal = 0.05 * (P_SIZE - 1) + 3.0 + margin
    return symmetric * (1.0 - identity) + identity * diagonal[:, :, None]


def plant(entries, rng, least, largest):
    longest = entries.shape.index(max(entries.shape))
    spots = []
    for shift in (0, 1):
        where = [jax.random.randint(jax.random.fold_in(rng, axis), (), 0, length) for axis, length in enumerate(entries.shape)]
        where[longest] = (where[longest] + shift) % entries.shape[longest]
        spots.append(tuple(where))
    return entries.at[spots[0]].set(least).at[spots[1]].set(largest)


def block_levels(own_key, dims, cuts, low, top_value):
    gain, own = 1.0, jax.random.fold_in(own_key, 6)
    for axis_at, shards_of in cuts:
        steps = jnp.exp(jax.random.uniform(jax.random.fold_in(own, axis_at), (shards_of,), jnp.float32, low / len(cuts), top_value / len(cuts)))
        gain = gain * jnp.repeat(steps, dims[axis_at] // shards_of).reshape([-1 if axis == axis_at else 1 for axis in range(len(dims))])
    return gain


def noise(key, shape, scale, bound, pieces=(), kind=jnp.bfloat16):
    array = jax.random.normal(key, shape, jnp.float32) * scale
    if len(pieces) > 0:
        array = block_levels(key, shape, pieces, -0.22, 0.18) * array
    return jnp.clip(array, min=-bound, max=bound).astype(kind)


def setup_inputs(seed: int = 0) -> dict:
    keys = jax.random.split(jax.random.key(seed), 6)
    return {
        "right_side": noise(keys[0], (NX, NY, NZ * P_SIZE), 4.0, 24.0, ((0, 8), (1, 16), (2, 8)), jnp.float32),
        "element_class": plant(jax.random.randint(keys[1], (NX, NY, NZ), 0, K), jax.random.fold_in(keys[1], 1), 0, K - 1).astype(jnp.int32),
        "class_blocks": draw_class_blocks(jax.random.fold_in(keys[5], 71), 0),
        "class_shift": jnp.clip(jnp.exp(jax.random.uniform(keys[3], (K,), jnp.float32, math.log(0.5), math.log(4.0))), 0.5, 4.0),
        "face_weights": jnp.clip(jax.random.uniform(keys[4], (3,), jnp.float32, 0.4, 0.9), 0.4, 0.9),
    }


highest = lax.Precision.HIGHEST
relax_weight = 0.6


def couple(padded, face_weights):
    middle = padded[1:-1, 1:-1, 1:-1]
    result = jnp.zeros(middle.shape, jnp.float32)
    result = result.at[:, :, :, 3].add(face_weights[0] * padded[2:, 1:-1, 1:-1, 0])
    result = result.at[:, :, :, 0].add(face_weights[0] * padded[:-2, 1:-1, 1:-1, 3])
    result = result.at[:, :, :, :, 3].add(face_weights[1] * padded[1:-1, 2:, 1:-1, :, 0])
    result = result.at[:, :, :, :, 0].add(face_weights[1] * padded[1:-1, :-2, 1:-1, :, 3])
    result = result.at[:, :, :, :, :, 3].add(face_weights[2] * padded[1:-1, 1:-1, 2:, :, :, 0])
    result = result.at[:, :, :, :, :, 0].add(face_weights[2] * padded[1:-1, 1:-1, :-2, :, :, 3])
    return result


def coarsen(values):
    size_x, size_y, size_z = values.shape
    return values.reshape(size_x // 2, 2, size_y // 2, 2, size_z // 2, 2).sum(axis=(1, 3, 5))


def refine(values):
    return jnp.repeat(jnp.repeat(jnp.repeat(values, 2, axis=0), 2, axis=1), 2, axis=2)


def section_apply(values, shift, extent):
    size_x, size_y, size_z = values.shape
    ext_x, ext_y, ext_z = extent
    blocked = values.reshape(size_x // ext_x, ext_x, size_y // ext_y, ext_y, size_z // ext_z, ext_z)
    padded = jnp.pad(blocked, ((0, 0), (1, 1), (0, 0), (1, 1), (0, 0), (1, 1)))
    beside = padded[:, 2:, :, 1:-1, :, 1:-1] + padded[:, :-2, :, 1:-1, :, 1:-1]
    beside = beside + padded[:, 1:-1, :, 2:, :, 1:-1] + padded[:, 1:-1, :, :-2, :, 1:-1]
    beside = beside + padded[:, 1:-1, :, 1:-1, :, 2:] + padded[:, 1:-1, :, 1:-1, :, :-2]
    return (6.0 + shift) * values - beside.reshape(size_x, size_y, size_z)


def extents(depth):
    factor = 2 ** depth
    return (CX * min(N_GX, factor) // factor, CY * min(N_GY, factor) // factor, CZ * min(N_GZ, factor) // factor)


def fine_apply(field, element_class, class_blocks, face_weights):
    elements = field.reshape(NX, NY, NZ, P_SIZE)

    def one_slab(pair):
        slab, marks = pair
        chosen = class_blocks[marks]
        return jnp.einsum("yznm,yzm->yzn", chosen, slab, precision=highest)

    local_part = lax.map(one_slab, (elements, element_class))
    padded = jnp.pad(elements.reshape(NX, NY, NZ, 4, 4, 4), ((1, 1), (1, 1), (1, 1), (0, 0), (0, 0), (0, 0)))
    nearby = couple(padded, face_weights).reshape(NX, NY, NZ, P_SIZE)
    return (local_part - nearby).reshape(NX, NY, NZ * P_SIZE)


def section_cycle(source, shift, depth):
    extent = extents(depth)
    diagonal = 6.0 + shift
    if depth == 3:
        iterate = jnp.zeros_like(source)
        for sweep_index in range(SWEEPS):
            iterate = iterate + relax_weight * (source - section_apply(iterate, shift, extent)) / diagonal
        return iterate
    iterate = relax_weight * source / diagonal
    remainder = source - section_apply(iterate, shift, extent)
    coarse = section_cycle(0.25 * coarsen(remainder), 0.125 * coarsen(shift), depth + 1)
    iterate = iterate + refine(coarse)
    return iterate + relax_weight * (source - section_apply(iterate, shift, extent)) / diagonal


def precondition(source, element_class, class_blocks, face_weights, fine_diagonal, shift_cells):
    iterate = relax_weight * source / fine_diagonal
    remainder = source - fine_apply(iterate, element_class, class_blocks, face_weights)
    sums = remainder.reshape(NX, NY, NZ, P_SIZE).sum(axis=3)
    coarse = section_cycle(coarsen(sums) / float(P_SIZE), 0.125 * coarsen(shift_cells), 1)
    iterate = iterate + jnp.repeat(refine(coarse), P_SIZE, axis=2)
    update = source - fine_apply(iterate, element_class, class_blocks, face_weights)
    return iterate + relax_weight * update / fine_diagonal


def reference(right_side, element_class, class_blocks, class_shift, face_weights):
    table = jnp.diagonal(class_blocks, axis1=1, axis2=2)
    fine_diagonal = table[element_class].reshape(NX, NY, NZ * P_SIZE)
    shift_cells = class_shift[element_class]
    residual = right_side
    smoothed = precondition(residual, element_class, class_blocks, face_weights, fine_diagonal, shift_cells)
    gamma_now = jnp.sum(residual * smoothed)
    direction = smoothed
    image = fine_apply(direction, element_class, class_blocks, face_weights)
    step_size = gamma_now / jnp.sum(direction * image)
    solution_field = step_size * direction
    residual = residual - step_size * image
    smoothed = precondition(residual, element_class, class_blocks, face_weights, fine_diagonal, shift_cells)
    gamma_next = jnp.sum(residual * smoothed)
    direction = smoothed + (gamma_next / gamma_now) * direction
    image = fine_apply(direction, element_class, class_blocks, face_weights)
    step_size = gamma_next / jnp.sum(direction * image)
    solution_field = solution_field + step_size * direction
    residual = residual - step_size * image
    return solution_field, residual
```

```python
import functools

import jax
import jax.numpy as jnp
from jax import lax
from jax.experimental import pallas as pl
from jax.experimental.pallas import tpu as pltpu
from jax.sharding import PartitionSpec as P

NODES = 64
CLASSES = 16
SLABS = 16
RELAX = 0.6
F32 = jnp.float32
HIGHEST = lax.Precision.HIGHEST
AXES = ("gx", "gy", "gz")


def dot(left, right):
    return jnp.dot(left, right, precision=HIGHEST, preferred_element_type=F32)


def iota(shape, dim):
    return lax.broadcasted_iota(jnp.int32, shape, dim)


def roll(values, shift, axis):
    return pltpu.roll(values, shift % values.shape[axis], axis)


def lane_places(shape):
    lane = iota(shape, len(shape) - 1)
    yd = (lane * 171) >> 12
    rest = lane - 24 * yd
    return rest >> 1, yd, rest & 1


def beside_1(v, lane, sub):
    a, b, gy = lane >> 6, (lane >> 4) & 3, lane & 15
    swapped = [roll(x, 64, 1) for x in v]
    result = []
    for gx in range(8):
        x = v[gx]
        total = swapped[gx] + jnp.where((gy & 1) == 0, roll(x, -1, 1), roll(x, 1, 1))
        if gx % 2 == 0:
            total = total + jnp.where(a == 1, swapped[gx + 1], 0.0)
        else:
            total = total + jnp.where(a == 0, swapped[gx - 1], 0.0)
        after = jnp.where((sub & 1) == 0, roll(roll(x, -1, 0), 48, 1), 0.0)
        before = jnp.where((sub & 1) == 1, roll(roll(x, 1, 0), -48, 1), 0.0)
        total = total + jnp.where(b < 3, roll(x, -16, 1), after)
        total = total + jnp.where(b > 0, roll(x, 16, 1), before)
        result.append(total)
    return result


def beside_2(v, lane, sub):
    b, gy = (lane >> 4) & 3, lane & 15
    result = []
    for gx in range(8):
        x = v[gx]
        total = jnp.where((gy & 2) == 0, roll(x, -2, 1), roll(x, 2, 1))
        if gx % 4 < 3:
            total = total + v[gx + 1]
        if gx % 4 > 0:
            total = total + v[gx - 1]
        after = jnp.where((sub & 3) < 3, roll(roll(x, -1, 0), 32, 1), 0.0)
        before = jnp.where((sub & 3) > 0, roll(roll(x, 1, 0), -32, 1), 0.0)
        total = total + jnp.where(b < 2, roll(x, -32, 1), after)
        total = total + jnp.where(b >= 2, roll(x, 32, 1), before)
        result.append(total)
    return result


def beside_3(v, lane, sub):
    gy = lane & 15
    result = []
    for gx in range(8):
        x = v[gx]
        total = jnp.where((gy & 4) == 0, roll(x, -4, 1), roll(x, 4, 1))
        if gx + 2 < 8:
            total = total + v[gx + 2]
        if gx - 2 >= 0:
            total = total + v[gx - 2]
        total = total + jnp.where(sub < 7, roll(x, -1, 0), 0.0)
        total = total + jnp.where(sub > 0, roll(x, 1, 0), 0.0)
        result.append(total)
    return result


def coarsen_1(v, lane):
    b, gy = (lane >> 4) & 3, lane & 15
    result = []
    for x in v:
        x = x + roll(x, 64, 1)
        x = x + jnp.where((b & 1) == 0, roll(x, -16, 1), roll(x, 16, 1))
        x = x + jnp.where((gy & 1) == 0, roll(x, -1, 1), roll(x, 1, 1))
        result.append(x)
    return result


def coarsen_2(v, lane):
    b, gy = (lane >> 4) & 3, lane & 15
    result = []
    for gx in range(8):
        x = v[gx] + v[gx ^ 1]
        x = x + jnp.where(b < 2, roll(x, -32, 1), roll(x, 32, 1))
        x = x + jnp.where((gy & 2) == 0, roll(x, -2, 1), roll(x, 2, 1))
        result.append(x)
    return result


def coarse_cycle(source, shift):
    lane, sub = iota((8, 128), 1), iota((8, 128), 0)
    eight = range(8)

    def remainder(beside, q, d, x):
        around = beside(x, lane, sub)
        return [q[i] - (d[i] * x[i] - around[i]) for i in eight]

    d1 = [6.0 + s for s in shift]
    shift2 = [0.125 * s for s in coarsen_1(shift, lane)]
    d2 = [6.0 + s for s in shift2]
    d3 = [6.0 + 0.125 * s for s in coarsen_2(shift2, lane)]
    w1 = [RELAX / d for d in d1]
    w2 = [RELAX / d for d in d2]
    w3 = [RELAX / d for d in d3]
    x1 = [w1[i] * source[i] for i in eight]
    q2 = [0.25 * t for t in coarsen_1(remainder(beside_1, source, d1, x1), lane)]
    x2 = [w2[i] * q2[i] for i in eight]
    q3 = [0.25 * t for t in coarsen_2(remainder(beside_2, q2, d2, x2), lane)]
    x3 = [w3[i] * q3[i] for i in eight]
    for _ in range(3):
        t3 = remainder(beside_3, q3, d3, x3)
        x3 = [x3[i] + w3[i] * t3[i] for i in eight]
    x2 = [x2[i] + x3[i] for i in eight]
    t2 = remainder(beside_2, q2, d2, x2)
    x2 = [x2[i] + w2[i] * t2[i] for i in eight]
    x1 = [x1[i] + x2[i] for i in eight]
    t1 = remainder(beside_1, source, d1, x1)
    return [x1[i] + w1[i] * t1[i] for i in eight]


def place_correction(coarse, place_ref, pad_ref, rows_ref, out_ref):
    gx0, gy0, gz0 = place_ref[0], place_ref[1], place_ref[2]
    pad_ref[...] = jnp.zeros_like(pad_ref)
    for gx in range(8):
        pad_ref[gx + 1, 8:16, :] = coarse[gx]
    rows_ref[...] = jnp.zeros_like(rows_ref)
    for e in range(3):
        for d in range(3):
            rows_ref[3 * e + d : 3 * e + d + 1, :] = pad_ref[gx0 + d, pl.ds(gz0 + 7 + e, 1), :]
    shape = (128, 512)
    source = iota(shape, 0)
    column = iota(shape, 1)
    target = column & 127
    yd = (target * 171) >> 12
    x = (target - 24 * yd) >> 1
    hit = ((source >> 4) & 3) == (column >> 7)
    hit = hit & ((source >> 6) == ((x >> 1) & 1))
    hit = hit & ((source & 15) == gy0 - 2 + yd) & (target < 120)
    spread = dot(rows_ref[...], jnp.where(hit, 1.0, 0.0))
    lane_x, _, _ = lane_places((1, 128))
    part = lane_x >> 2
    for t in range(8):
        e, b = (t + 2) // 4, (t + 2) % 4
        pieces = [spread[3 * e + d : 3 * e + d + 1, 128 * b : 128 * b + 128] for d in range(3)]
        row = jnp.where(part == 0, pieces[0], jnp.where(part == 1, pieces[1], pieces[2]))
        out_ref[2 * t : 2 * t + 1, :] = row
        out_ref[2 * t + 1 : 2 * t + 2, :] = row


def groups(values):
    return [values[8 * g : 8 * g + 8] for g in range(8)]


def next_y(values, yi):
    return jnp.where(yi == 0, roll(values, -1, 1), roll(values, -23, 1))


def previous_y(values, yi):
    return jnp.where(yi == 1, roll(values, 1, 1), roll(values, 23, 1))


def coupling(before, here, after, weights_ref):
    sub = iota((8, 128), 0)
    _, _, yi = lane_places((8, 128))
    wx, wy, wz = weights_ref[0], weights_ref[1], weights_ref[2]
    own, low, high = groups(here), groups(before), groups(after)
    wz_top = jnp.where((sub & 3) == 3, wz, 0.0)
    wz_bottom = jnp.where((sub & 3) == 0, wz, 0.0)
    wy_top = jnp.where(sub >= 4, wy, 0.0)
    wy_bottom = jnp.where(sub < 4, wy, 0.0)
    result = []
    for g in range(8):
        term = wz_top * roll(high[g], 3, 0) + wz_bottom * roll(low[g], -3, 0)
        if g % 2 == 1:
            term = term + wy_top * next_y(roll(own[g - 1], 4, 0), yi)
        else:
            term = term + wy_bottom * previous_y(roll(own[g + 1], 4, 0), yi)
        if g >= 6:
            term = term + wx * roll(own[g - 6], -2, 1)
        if g < 2:
            term = term + wx * roll(own[g + 6], 2, 1)
        result.append(term)
    return result


def apply_pair(field_ref, slab, packed_ref, class_ref, weights_ref, write):
    planes = [field_ref[slab + i] for i in (-1, 0, 1, 2)]
    u = jnp.concatenate([planes[1], planes[2]], axis=1)
    first = u.astype(jnp.bfloat16)
    rest = u - first.astype(F32)
    second = rest.astype(jnp.bfloat16)
    third = (rest - second.astype(F32)).astype(jnp.bfloat16)
    packed = jnp.concatenate([first, second, third, first, second, first], axis=0)
    products = jnp.dot(packed_ref[...], packed, preferred_element_type=F32)
    for half in range(2):
        marks = jnp.broadcast_to(class_ref[pl.ds(slab + half, 1), :], (8, 128))
        columns = slice(128 * half, 128 * half + 128)
        chosen = [products[8 * g : 8 * g + 8, columns] for g in range(8)]
        for k in range(1, CLASSES):
            hit = marks == k
            for g in range(8):
                row = 64 * k + 8 * g
                chosen[g] = jnp.where(hit, products[row : row + 8, columns], chosen[g])
        faces = coupling(planes[half], planes[half + 1], planes[half + 2], weights_ref)
        for g in range(8):
            write(slab + half, g, chosen[g] - faces[g])


def restrict(source_ref, inverse_ref, sums_ref, weights_ref, total_ref, all_ref, out_ref):
    sub = iota((8, 128), 0)
    _, _, yi = lane_places((8, 128))
    wx, wy, wz = weights_ref[0], weights_ref[1], weights_ref[2]

    def collect(s, carry):
        r, inv, cols = source_ref[s], inverse_ref[s], sums_ref[s]
        x = inv * r
        d = groups(r - cols * x)
        xs = groups(x)
        even = (xs[0] + xs[2]) + (xs[4] + xs[6])
        odd = (xs[1] + xs[3]) + (xs[5] + xs[7])
        local = ((d[0] + d[1]) + (d[2] + d[3])) + ((d[4] + d[5]) + (d[6] + d[7]))
        local = local + wx * (roll(xs[0] + xs[1], -2, 1) + roll(xs[6] + xs[7], 2, 1))
        local = local + jnp.where(sub < 4, wy, 0.0) * next_y(even, yi)
        local = local + jnp.where(sub >= 4, wy, 0.0) * previous_y(odd, yi)
        total_ref[s] = local
        all_ref[s] = even + odd
        return carry

    lax.fori_loop(3, 13, collect, 0)
    bottom = jnp.where((sub & 3) == 0, wz, 0.0)
    top = jnp.where((sub & 3) == 3, wz, 0.0)
    for z in range(8):
        s = z + 4
        value = total_ref[s] + bottom * all_ref[s + 1] + top * all_ref[s - 1]
        out_ref[z : z + 1, :] = jnp.sum(value, axis=0, keepdims=True)


def payload(cells, place_ref, scale):
    shape = (128, 128)
    source, target = iota(shape, 0), iota(shape, 1)
    hit = (source >= 56) & (source < 64) & (((source - 56) >> 2) == (target >> 6))
    hit = hit & ((target & 15) == place_ref[1])
    spread = dot(cells, jnp.where(hit, scale, 0.0))
    z, lane = iota((8, 128), 0), iota((8, 128), 1)
    return jnp.sum(jnp.where((z >> 1) == ((lane >> 4) & 3), spread, 0.0), axis=0, keepdims=True)


def compact(ref, out_ref):
    for pair in range(4):
        both = jnp.concatenate([ref[4 + 2 * pair], ref[5 + 2 * pair]], axis=0)
        out_ref[:, 128 * pair : 128 * pair + 128] = both.T[56:64]


def pack_kernel(blocks_ref, out_ref):
    w = blocks_ref[...]
    first = w.astype(jnp.bfloat16).astype(F32)
    rest = w - first
    second = rest.astype(jnp.bfloat16).astype(F32)
    third = rest - second
    column = iota(w.shape, 1)
    out_ref[...] = jnp.where(column < 192, first, jnp.where(column < 320, second, third)).astype(jnp.bfloat16)


def start_kernel(
    place_ref, weights_ref, class_shift_ref, middle_ref, low_ref, high_ref, table_ref,
    field_ref, class_ref, inverse_ref, sums_ref, payload_ref,
    total_ref, all_ref, cells_ref,
):
    rows = jnp.zeros((8, 128), F32)

    def turned(ref, block):
        return jnp.concatenate([ref[:, 128 * block : 128 * block + 128], rows], axis=0).T

    blocks = [turned(low_ref, 1), turned(low_ref, 2), turned(middle_ref, 0), turned(middle_ref, 1)]
    blocks += [turned(middle_ref, 3), turned(middle_ref, 4), turned(high_ref, 0), turned(high_ref, 1)]
    for pair, block in enumerate(blocks):
        field_ref[2 * pair] = block[:64]
        field_ref[2 * pair + 1] = block[64:]
    marks = jnp.concatenate(
        [turned(low_ref, 0)[0:8], turned(middle_ref, 2)[0:8], turned(high_ref, 2)[0:8]], axis=0
    )
    class_ref[...] = jnp.concatenate([marks[4:16], marks[16:20]], axis=0).astype(jnp.int32)

    gx0, gy0, gz0 = place_ref[0], place_ref[1], place_ref[2]
    x, yd, _ = lane_places((1, 128))
    gx, gy = gx0 - 1 + (x >> 2), gy0 - 2 + yd
    inside = (gx >= 0) & (gx < 8) & (gy >= 0) & (gy < 16) & (yd < 5)
    relax = jnp.where(inside, RELAX, 0.0)

    def coefficients(s, carry):
        row = class_ref[pl.ds(s, 1), :]
        onehot = jnp.where(jnp.broadcast_to(row, (CLASSES, 128)) == iota((CLASSES, 128), 0), 1.0, 0.0)
        both = dot(table_ref[...], onehot)
        gz = gz0 - 1 + ((s + 4) >> 3)
        valid = jnp.where((gz >= 0) & (gz < 8), 1.0, 0.0)
        inverse_ref[s] = (relax * valid) / both[:64]
        sums_ref[s] = both[64:]
        return carry

    lax.fori_loop(0, SLABS, coefficients, 0)
    restrict(field_ref, inverse_ref, sums_ref, weights_ref, total_ref, all_ref, cells_ref)
    own_marks = class_ref[4:12, :]
    shifts = jnp.zeros((8, 128), F32)
    for k in range(CLASSES):
        shifts = jnp.where(own_marks == k, class_shift_ref[k], shifts)
    payload_ref[:, 0:128] = payload(cells_ref[...], place_ref, 1.0 / NODES)
    payload_ref[:, 128:256] = payload(shifts, place_ref, 0.125)


def first_kernel(
    place_ref, weights_ref, gathered_ref, field_ref, class_ref, inverse_ref, sums_ref, packed_ref, right_ref,
    image_ref, own_direction_ref, own_image_ref, payload_ref,
    iterate_ref, smooth_ref, pad_ref, rows_ref, shift_ref, total_ref, all_ref, cells_ref,
):
    coarse = coarse_cycle(
        [gathered_ref[g, :, 0:128] for g in range(8)], [gathered_ref[g, :, 128:256] for g in range(8)]
    )
    place_correction(coarse, place_ref, pad_ref, rows_ref, shift_ref)

    def correct(s, carry):
        iterate_ref[s] = inverse_ref[s] * field_ref[s] + shift_ref[pl.ds(s, 1), :]
        return carry

    lax.fori_loop(0, SLABS, correct, 0)

    def smooth(s, g, value):
        at = (s, pl.ds(8 * g, 8))
        smooth_ref[at] = iterate_ref[at] + inverse_ref[at] * (field_ref[at] - value)

    def smooth_pair(i, carry):
        apply_pair(iterate_ref, 2 * i + 1, packed_ref, class_ref, weights_ref, smooth)
        return carry

    lax.fori_loop(0, 7, smooth_pair, 0)

    def store(s, g, value):
        image_ref[s, pl.ds(8 * g, 8)] = value

    def image_pair(i, carry):
        apply_pair(smooth_ref, 2 * i + 2, packed_ref, class_ref, weights_ref, store)
        return carry

    lax.fori_loop(0, 6, image_pair, 0)
    for s in (0, 1, 14, 15):
        image_ref[s] = jnp.zeros((64, 128), F32)
    restrict(image_ref, inverse_ref, sums_ref, weights_ref, total_ref, all_ref, cells_ref)
    payload_ref[:, 0:128] = payload(cells_ref[...], place_ref, 1.0 / NODES)
    compact(smooth_ref, own_direction_ref)
    compact(image_ref, own_image_ref)
    direction = own_direction_ref[...]
    gamma = jnp.sum(jnp.sum(right_ref[...] * direction, axis=0, keepdims=True), axis=1, keepdims=True)
    delta = jnp.sum(jnp.sum(direction * own_image_ref[...], axis=0, keepdims=True), axis=1, keepdims=True)
    lane = iota((1, 128), 1)
    payload_ref[:, 128:256] = jnp.where(lane == 0, gamma, jnp.where(lane == 1, delta, 0.0))


def second_kernel(
    place_ref, weights_ref, gathered_ref, shifts_ref, image_ref, class_ref, inverse_ref, packed_ref, right_ref,
    own_direction_ref, own_image_ref,
    residual_ref, smoothed_ref, applied_ref, known_ref, payload_ref,
    iterate_ref, smooth_ref, second_ref, pad_ref, rows_ref, shift_ref, turned_ref,
):
    coarse = coarse_cycle(
        [gathered_ref[g, :, 0:128] for g in range(8)], [shifts_ref[g, :, 128:256] for g in range(8)]
    )
    place_correction(coarse, place_ref, pad_ref, rows_ref, shift_ref)

    def correct(s, carry):
        iterate_ref[s] = inverse_ref[s] * image_ref[s] + shift_ref[pl.ds(s, 1), :]
        return carry

    lax.fori_loop(2, 14, correct, 0)

    def smooth(s, g, value):
        at = (s, pl.ds(8 * g, 8))
        smooth_ref[at] = iterate_ref[at] + inverse_ref[at] * (image_ref[at] - value)

    def smooth_pair(i, carry):
        apply_pair(iterate_ref, 2 * i + 3, packed_ref, class_ref, weights_ref, smooth)
        return carry

    lax.fori_loop(0, 5, smooth_pair, 0)

    def store(s, g, value):
        second_ref[s, pl.ds(8 * g, 8)] = value

    def second_pair(i, carry):
        apply_pair(smooth_ref, 2 * i + 4, packed_ref, class_ref, weights_ref, store)
        return carry

    lax.fori_loop(0, 4, second_pair, 0)

    sums = gathered_ref[0, :, 128:256]
    for g in range(1, 8):
        sums = sums + gathered_ref[g, :, 128:256]
    sums = jnp.sum(sums, axis=0, keepdims=True)
    known_ref[...] = sums
    step = sums[:, 0:1] / sums[:, 1:2]
    compact(smooth_ref, turned_ref)
    smoothed = own_direction_ref[...] - step * turned_ref[...]
    smoothed_ref[...] = smoothed
    compact(second_ref, turned_ref)
    applied = own_image_ref[...] - step * turned_ref[...]
    applied_ref[...] = applied
    residual = right_ref[...] - step * own_image_ref[...]
    residual_ref[...] = residual

    def total(values):
        return jnp.sum(jnp.sum(values, axis=0, keepdims=True), axis=1, keepdims=True)

    lane = iota((1, 128), 1)
    cross = own_direction_ref[...] * applied + own_image_ref[...] * smoothed
    row = jnp.where(lane == 0, total(residual * smoothed), 0.0)
    row = jnp.where(lane == 1, total(smoothed * applied), row)
    payload_ref[...] = jnp.where(lane == 2, total(cross), row)


VMEM = pl.BlockSpec(memory_space=pltpu.VMEM)
SMEM = pl.BlockSpec(memory_space=pltpu.SMEM)


def call(body, scalars, out_shape, scratch, *args):
    specs = [SMEM] * scalars + [VMEM] * (len(args) - scalars)
    shapes = [jax.ShapeDtypeStruct(shape, dtype) for shape, dtype in out_shape]
    return pl.pallas_call(
        body,
        out_shape=shapes,
        in_specs=specs,
        out_specs=[VMEM] * len(shapes),
        scratch_shapes=[pltpu.VMEM(shape, F32) for shape in scratch],
        compiler_params=pltpu.CompilerParams(vmem_limit_bytes=40 * 1024 * 1024),
    )(*args)


FIELD = (SLABS, NODES, 128)
COARSE_SCRATCH = [(10, 24, 128), (16, 128), (16, 128)]
SUM_SCRATCH = [(SLABS, 8, 128), (SLABS, 8, 128), (8, 128)]
OWN = (8, 512)


def start_call(*args):
    shapes = [(FIELD, F32), ((SLABS, 128), jnp.int32), (FIELD, F32), (FIELD, F32), ((1, 256), F32)]
    return call(start_kernel, 3, shapes, SUM_SCRATCH, *args)


def first_call(*args):
    shapes = [(FIELD, F32), (OWN, F32), (OWN, F32), ((1, 256), F32)]
    return call(first_kernel, 2, shapes, [FIELD, FIELD] + COARSE_SCRATCH + SUM_SCRATCH, *args)


def second_call(*args):
    shapes = [(OWN, F32), (OWN, F32), (OWN, F32), ((1, 128), F32), ((1, 128), F32)]
    return call(second_kernel, 2, shapes, [FIELD, FIELD, FIELD] + COARSE_SCRATCH + [OWN], *args)


def shifted(x, axis, step):
    size = lax.axis_size(axis)
    pairs = [(i, i + step) for i in range(size) if 0 <= i + step < size]
    return lax.ppermute(x, axis, pairs)


def extend(own):
    wide = jnp.concatenate([shifted(own, "gx", 1), own, shifted(own, "gx", -1)], axis=0)
    middle = jnp.concatenate(
        [
            shifted(wide, "gy", 2), shifted(wide, "gy", 1), wide, shifted(wide, "gy", -1), shifted(wide, "gy", -2),
        ],
        axis=0,
    )
    low = shifted(middle[:, 256:640], "gz", 1)
    high = shifted(middle[:, 0:384], "gz", -1)
    return middle, low, high


def gather_cells(row):
    parts = lax.all_to_all(jnp.broadcast_to(row[None], (128, 1, 256)), ("gy", "gz"), 0, 0, tiled=True)
    plane = parts.reshape(16, 8, 256).sum(axis=0)
    return lax.all_to_all(jnp.broadcast_to(plane[None], (8, 8, 256)), "gx", 0, 0, tiled=True)


def gather_sum(row):
    parts = lax.all_to_all(jnp.broadcast_to(row[None], (128, 1, 128)), ("gy", "gz"), 0, 0, tiled=True)
    part = parts.reshape(128, 128).sum(axis=0)
    parts = lax.all_to_all(jnp.broadcast_to(part[None, None], (8, 1, 128)), "gx", 0, 0, tiled=True)
    return parts.reshape(8, 128).sum(axis=0)


def per_device(right_side, element_class, class_blocks, class_shift, face_weights):
    place = jnp.stack([lax.axis_index(axis) for axis in AXES]).astype(jnp.int32)
    right = right_side.reshape(OWN)
    marks = jnp.pad(element_class.reshape(8, 8).astype(F32), ((0, 0), (0, 120)))
    own = jnp.concatenate([right[:, 0:256], marks, right[:, 256:512]], axis=1)
    middle, low, high = extend(own)

    blocks = class_blocks.reshape(CLASSES * NODES, NODES)
    packed = call(
        pack_kernel, 0, [((CLASSES * NODES, 384), jnp.bfloat16)], [], jnp.concatenate([blocks] * 6, axis=1)
    )[0]
    table = jnp.concatenate(
        [jnp.diagonal(class_blocks, axis1=1, axis2=2), class_blocks.sum(axis=1)], axis=1
    ).T

    field, classes, inverse, sums, row = start_call(place, face_weights, class_shift, middle, low, high, table)
    gathered = gather_cells(row)
    image, direction, own_image, row = first_call(
        place, face_weights, gathered, field, classes, inverse, sums, packed, right
    )
    again = gather_cells(row)
    residual, smoothed, applied, known, row = second_call(
        place, face_weights, again, gathered, image, classes, inverse, packed, right, direction, own_image
    )
    totals = gather_sum(row)
    gamma, delta = known[0, 0], known[0, 1]
    beta = totals[0] / gamma
    step = totals[0] / (totals[1] + beta * (totals[2] + beta * delta))
    solution_field = (gamma / delta) * direction + step * (smoothed + beta * direction)
    residual = residual - step * (applied + beta * own_image)
    return (solution_field.reshape(right_side.shape), residual.reshape(right_side.shape))


def solution(mesh):
    in_specs = (P("gx", "gy", "gz"), P("gx", "gy", "gz"), P(), P(), P())
    out_specs = (P("gx", "gy", "gz"), P("gx", "gy", "gz"))
    return jax.shard_map(
        per_device, mesh=mesh, in_specs=in_specs, out_specs=out_specs, check_vma=False
    )
```

```python
import functools

import jax
import jax.numpy as jnp
from jax import lax
from jax.experimental import pallas as pl
from jax.experimental.pallas import tpu as pltpu
from jax.sharding import PartitionSpec as P

NODES = 64
CLASSES = 16
SLABS = 16
RELAX = 0.6
F32 = jnp.float32
HIGHEST = lax.Precision.HIGHEST
AXES = ("gx", "gy", "gz")


def dot(left, right):
    return jnp.dot(left, right, precision=HIGHEST, preferred_element_type=F32)


def iota(shape, dim):
    return lax.broadcasted_iota(jnp.int32, shape, dim)


def roll(values, shift, axis):
    return pltpu.roll(values, shift % values.shape[axis], axis)


def lane_places(shape):
    lane = iota(shape, len(shape) - 1)
    yd = (lane * 171) >> 12
    rest = lane - 24 * yd
    return rest >> 1, yd, rest & 1


def beside_1(v, lane, sub):
    a, b, gy = lane >> 6, (lane >> 4) & 3, lane & 15
    swapped = [roll(x, 64, 1) for x in v]
    result = []
    for gx in range(8):
        x = v[gx]
        total = swapped[gx] + jnp.where((gy & 1) == 0, roll(x, -1, 1), roll(x, 1, 1))
        if gx % 2 == 0:
            total = total + jnp.where(a == 1, swapped[gx + 1], 0.0)
        else:
            total = total + jnp.where(a == 0, swapped[gx - 1], 0.0)
        after = jnp.where((sub & 1) == 0, roll(roll(x, -1, 0), 48, 1), 0.0)
        before = jnp.where((sub & 1) == 1, roll(roll(x, 1, 0), -48, 1), 0.0)
        total = total + jnp.where(b < 3, roll(x, -16, 1), after)
        total = total + jnp.where(b > 0, roll(x, 16, 1), before)
        result.append(total)
    return result


def beside_2(v, lane, sub):
    b, gy = (lane >> 4) & 3, lane & 15
    result = []
    for gx in range(8):
        x = v[gx]
        total = jnp.where((gy & 2) == 0, roll(x, -2, 1), roll(x, 2, 1))
        if gx % 4 < 3:
            total = total + v[gx + 1]
        if gx % 4 > 0:
            total = total + v[gx - 1]
        after = jnp.where((sub & 3) < 3, roll(roll(x, -1, 0), 32, 1), 0.0)
        before = jnp.where((sub & 3) > 0, roll(roll(x, 1, 0), -32, 1), 0.0)
        total = total + jnp.where(b < 2, roll(x, -32, 1), after)
        total = total + jnp.where(b >= 2, roll(x, 32, 1), before)
        result.append(total)
    return result


def beside_3(v, lane, sub):
    gy = lane & 15
    result = []
    for gx in range(8):
        x = v[gx]
        total = jnp.where((gy & 4) == 0, roll(x, -4, 1), roll(x, 4, 1))
        if gx + 2 < 8:
            total = total + v[gx + 2]
        if gx - 2 >= 0:
            total = total + v[gx - 2]
        total = total + jnp.where(sub < 7, roll(x, -1, 0), 0.0)
        total = total + jnp.where(sub > 0, roll(x, 1, 0), 0.0)
        result.append(total)
    return result


def coarsen_1(v, lane):
    b, gy = (lane >> 4) & 3, lane & 15
    result = []
    for x in v:
        x = x + roll(x, 64, 1)
        x = x + jnp.where((b & 1) == 0, roll(x, -16, 1), roll(x, 16, 1))
        x = x + jnp.where((gy & 1) == 0, roll(x, -1, 1), roll(x, 1, 1))
        result.append(x)
    return result


def coarsen_2(v, lane):
    b, gy = (lane >> 4) & 3, lane & 15
    result = []
    for gx in range(8):
        x = v[gx] + v[gx ^ 1]
        x = x + jnp.where(b < 2, roll(x, -32, 1), roll(x, 32, 1))
        x = x + jnp.where((gy & 2) == 0, roll(x, -2, 1), roll(x, 2, 1))
        result.append(x)
    return result


def coarse_cycle(source, shift):
    lane, sub = iota((8, 128), 1), iota((8, 128), 0)
    eight = range(8)

    def remainder(beside, q, d, x):
        around = beside(x, lane, sub)
        return [q[i] - (d[i] * x[i] - around[i]) for i in eight]

    d1 = [6.0 + s for s in shift]
    shift2 = [0.125 * s for s in coarsen_1(shift, lane)]
    d2 = [6.0 + s for s in shift2]
    d3 = [6.0 + 0.125 * s for s in coarsen_2(shift2, lane)]
    w1 = [RELAX / d for d in d1]
    w2 = [RELAX / d for d in d2]
    w3 = [RELAX / d for d in d3]
    x1 = [w1[i] * source[i] for i in eight]
    q2 = [0.25 * t for t in coarsen_1(remainder(beside_1, source, d1, x1), lane)]
    x2 = [w2[i] * q2[i] for i in eight]
    q3 = [0.25 * t for t in coarsen_2(remainder(beside_2, q2, d2, x2), lane)]
    x3 = [w3[i] * q3[i] for i in eight]
    for _ in range(3):
        t3 = remainder(beside_3, q3, d3, x3)
        x3 = [x3[i] + w3[i] * t3[i] for i in eight]
    x2 = [x2[i] + x3[i] for i in eight]
    t2 = remainder(beside_2, q2, d2, x2)
    x2 = [x2[i] + w2[i] * t2[i] for i in eight]
    x1 = [x1[i] + x2[i] for i in eight]
    t1 = remainder(beside_1, source, d1, x1)
    return [x1[i] + w1[i] * t1[i] for i in eight]


def place_correction(coarse, place_ref, pad_ref, rows_ref, out_ref):
    gx0, gy0, gz0 = place_ref[0], place_ref[1], place_ref[2]
    pad_ref[...] = jnp.zeros_like(pad_ref)
    for gx in range(8):
        pad_ref[gx + 1, 8:16, :] = coarse[gx]
    rows_ref[...] = jnp.zeros_like(rows_ref)
    for e in range(3):
        for d in range(3):
            rows_ref[3 * e + d : 3 * e + d + 1, :] = pad_ref[gx0 + d, pl.ds(gz0 + 7 + e, 1), :]
    shape = (128, 512)
    source = iota(shape, 0)
    column = iota(shape, 1)
    target = column & 127
    yd = (target * 171) >> 12
    x = (target - 24 * yd) >> 1
    hit = ((source >> 4) & 3) == (column >> 7)
    hit = hit & ((source >> 6) == ((x >> 1) & 1))
    hit = hit & ((source & 15) == gy0 - 2 + yd) & (target < 120)
    spread = dot(rows_ref[...], jnp.where(hit, 1.0, 0.0))
    lane_x, _, _ = lane_places((1, 128))
    part = lane_x >> 2
    for t in range(8):
        e, b = (t + 2) // 4, (t + 2) % 4
        pieces = [spread[3 * e + d : 3 * e + d + 1, 128 * b : 128 * b + 128] for d in range(3)]
        row = jnp.where(part == 0, pieces[0], jnp.where(part == 1, pieces[1], pieces[2]))
        out_ref[2 * t : 2 * t + 1, :] = row
        out_ref[2 * t + 1 : 2 * t + 2, :] = row


def groups(values):
    return [values[8 * g : 8 * g + 8] for g in range(8)]


def next_y(values, yi):
    return jnp.where(yi == 0, roll(values, -1, 1), roll(values, -23, 1))


def previous_y(values, yi):
    return jnp.where(yi == 1, roll(values, 1, 1), roll(values, 23, 1))


def coupling(before, here, after, weights_ref):
    sub = iota((8, 128), 0)
    _, _, yi = lane_places((8, 128))
    wx, wy, wz = weights_ref[0], weights_ref[1], weights_ref[2]
    own, low, high = groups(here), groups(before), groups(after)
    wz_top = jnp.where((sub & 3) == 3, wz, 0.0)
    wz_bottom = jnp.where((sub & 3) == 0, wz, 0.0)
    wy_top = jnp.where(sub >= 4, wy, 0.0)
    wy_bottom = jnp.where(sub < 4, wy, 0.0)
    result = []
    for g in range(8):
        term = wz_top * roll(high[g], 3, 0) + wz_bottom * roll(low[g], -3, 0)
        if g % 2 == 1:
            term = term + wy_top * next_y(roll(own[g - 1], 4, 0), yi)
        else:
            term = term + wy_bottom * previous_y(roll(own[g + 1], 4, 0), yi)
        if g >= 6:
            term = term + wx * roll(own[g - 6], -2, 1)
        if g < 2:
            term = term + wx * roll(own[g + 6], 2, 1)
        result.append(term)
    return result


def apply_pair(field_ref, slab, packed_ref, class_ref, weights_ref, write):
    planes = [field_ref[slab + i] for i in (-1, 0, 1, 2)]
    u = jnp.concatenate([planes[1], planes[2]], axis=1)
    first = u.astype(jnp.bfloat16)
    rest = u - first.astype(F32)
    second = rest.astype(jnp.bfloat16)
    third = (rest - second.astype(F32)).astype(jnp.bfloat16)
    packed = jnp.concatenate([first, second, third, first, second, first], axis=0)
    products = jnp.dot(packed_ref[...], packed, preferred_element_type=F32)
    for half in range(2):
        marks = jnp.broadcast_to(class_ref[pl.ds(slab + half, 1), :], (8, 128))
        columns = slice(128 * half, 128 * half + 128)
        chosen = [products[8 * g : 8 * g + 8, columns] for g in range(8)]
        for k in range(1, CLASSES):
            hit = marks == k
            for g in range(8):
                row = 64 * k + 8 * g
                chosen[g] = jnp.where(hit, products[row : row + 8, columns], chosen[g])
        faces = coupling(planes[half], planes[half + 1], planes[half + 2], weights_ref)
        for g in range(8):
            write(slab + half, g, chosen[g] - faces[g])


def restrict(source_ref, inverse_ref, sums_ref, weights_ref, total_ref, all_ref, out_ref):
    sub = iota((8, 128), 0)
    _, _, yi = lane_places((8, 128))
    wx, wy, wz = weights_ref[0], weights_ref[1], weights_ref[2]

    def collect(s, carry):
        r, inv, cols = source_ref[s], inverse_ref[s], sums_ref[s]
        x = inv * r
        d = groups(r - cols * x)
        xs = groups(x)
        even = (xs[0] + xs[2]) + (xs[4] + xs[6])
        odd = (xs[1] + xs[3]) + (xs[5] + xs[7])
        local = ((d[0] + d[1]) + (d[2] + d[3])) + ((d[4] + d[5]) + (d[6] + d[7]))
        local = local + wx * (roll(xs[0] + xs[1], -2, 1) + roll(xs[6] + xs[7], 2, 1))
        local = local + jnp.where(sub < 4, wy, 0.0) * next_y(even, yi)
        local = local + jnp.where(sub >= 4, wy, 0.0) * previous_y(odd, yi)
        total_ref[s] = local
        all_ref[s] = even + odd
        return carry

    lax.fori_loop(3, 13, collect, 0)
    bottom = jnp.where((sub & 3) == 0, wz, 0.0)
    top = jnp.where((sub & 3) == 3, wz, 0.0)
    for z in range(8):
        s = z + 4
        value = total_ref[s] + bottom * all_ref[s + 1] + top * all_ref[s - 1]
        out_ref[z : z + 1, :] = jnp.sum(value, axis=0, keepdims=True)


def payload(cells, place_ref, scale):
    shape = (128, 128)
    source, target = iota(shape, 0), iota(shape, 1)
    hit = (source >= 56) & (source < 64) & (((source - 56) >> 2) == (target >> 6))
    hit = hit & ((target & 15) == place_ref[1])
    spread = dot(cells, jnp.where(hit, scale, 0.0))
    z, lane = iota((8, 128), 0), iota((8, 128), 1)
    return jnp.sum(jnp.where((z >> 1) == ((lane >> 4) & 3), spread, 0.0), axis=0, keepdims=True)


def compact(ref, out_ref):
    for pair in range(4):
        both = jnp.concatenate([ref[4 + 2 * pair], ref[5 + 2 * pair]], axis=0)
        out_ref[:, 128 * pair : 128 * pair + 128] = both.T[56:64]


def own_right(own_ref):
    return jnp.concatenate([own_ref[:, 0:256], own_ref[:, 384:640]], axis=1)


def split(values):
    first = values.astype(jnp.bfloat16).astype(F32)
    rest = values - first
    second = rest.astype(jnp.bfloat16).astype(F32)
    return first, second, rest - second


def own_kernel(right_ref, marks_ref, out_ref):
    out_ref[:, 256:384] = jnp.zeros((8, 128), F32)
    for x in range(4):
        rows = slice(2 * x, 2 * x + 2)
        values = right_ref[x]
        out_ref[rows, 0:256] = values[:, 0:256]
        out_ref[rows, 384:640] = values[:, 256:512]
        out_ref[rows, 256:264] = marks_ref[x].astype(F32)


def pack_kernel(blocks_ref, packed_ref, table_ref):
    diagonal = jnp.where(iota((64, 64), 0) == iota((64, 64), 1), 1.0, 0.0)
    low = iota((64, 128), 1) < 64
    rows = []
    for k in range(CLASSES):
        block = blocks_ref[k]
        first, second, third = split(jnp.concatenate([block, block], axis=1))
        at = slice(64 * k, 64 * k + 64)
        packed_ref[at, 0:128] = first.astype(jnp.bfloat16)
        packed_ref[at, 128:256] = jnp.where(low, first, second).astype(jnp.bfloat16)
        packed_ref[at, 256:384] = jnp.where(low, second, third).astype(jnp.bfloat16)
        diag = jnp.sum(block * diagonal, axis=0, keepdims=True)
        rows.append(jnp.concatenate([diag, jnp.sum(block, axis=0, keepdims=True)], axis=1))
    parts = split(jnp.concatenate(rows, axis=0))
    table = jnp.concatenate(list(parts) + [jnp.zeros((80, 128), F32)], axis=0).T
    table_ref[...] = table[:, 0:48].astype(jnp.bfloat16)


def start_kernel(
    place_ref, weights_ref, class_shift_ref, middle_ref, low_ref, high_ref, table_ref,
    field_ref, class_ref, inverse_ref, sums_ref, payload_ref,
    total_ref, all_ref, cells_ref,
):
    rows = jnp.zeros((8, 128), F32)

    def turned(ref, block):
        return jnp.concatenate([ref[:, 128 * block : 128 * block + 128], rows], axis=0).T

    blocks = [turned(low_ref, 1), turned(low_ref, 2), turned(middle_ref, 0), turned(middle_ref, 1)]
    blocks += [turned(middle_ref, 3), turned(middle_ref, 4), turned(high_ref, 0), turned(high_ref, 1)]
    for pair, block in enumerate(blocks):
        field_ref[2 * pair] = block[:64]
        field_ref[2 * pair + 1] = block[64:]
    marks = jnp.concatenate(
        [turned(low_ref, 0)[0:8], turned(middle_ref, 2)[0:8], turned(high_ref, 2)[0:8]], axis=0
    )
    class_ref[...] = jnp.concatenate([marks[4:16], marks[16:20]], axis=0).astype(jnp.int32)

    gx0, gy0, gz0 = place_ref[0], place_ref[1], place_ref[2]
    x, yd, _ = lane_places((1, 128))
    gx, gy = gx0 - 1 + (x >> 2), gy0 - 2 + yd
    inside = (gx >= 0) & (gx < 8) & (gy >= 0) & (gy < 16) & (yd < 5)
    relax = jnp.where(inside, RELAX, 0.0)

    for pair in range(SLABS // 2):
        slabs = (2 * pair, 2 * pair + 1)
        halves = []
        for s in slabs:
            row = jnp.broadcast_to(class_ref[s : s + 1, :], (CLASSES, 128))
            halves.append(jnp.where(row == iota((CLASSES, 128), 0), 1.0, 0.0))
        onehot = jnp.concatenate(halves, axis=1)
        onehot = jnp.concatenate([onehot] * 3, axis=0).astype(jnp.bfloat16)
        both = jnp.dot(table_ref[...], onehot, preferred_element_type=F32)
        for half, s in enumerate(slabs):
            gz = gz0 - 1 + ((s + 4) >> 3)
            valid = jnp.where((gz >= 0) & (gz < 8), 1.0, 0.0)
            columns = slice(128 * half, 128 * half + 128)
            inverse_ref[s] = (relax * valid) / both[:64, columns]
            sums_ref[s] = both[64:, columns]

    restrict(field_ref, inverse_ref, sums_ref, weights_ref, total_ref, all_ref, cells_ref)
    own_marks = class_ref[4:12, :]
    shifts = jnp.zeros((8, 128), F32)
    for k in range(CLASSES):
        shifts = jnp.where(own_marks == k, class_shift_ref[k], shifts)
    payload_ref[:, 0:128] = payload(cells_ref[...], place_ref, 1.0 / NODES)
    payload_ref[:, 128:256] = payload(shifts, place_ref, 0.125)


def first_kernel(
    place_ref, weights_ref, gathered_ref, field_ref, class_ref, inverse_ref, sums_ref, packed_ref, right_ref,
    image_ref, own_direction_ref, own_image_ref, payload_ref,
    iterate_ref, smooth_ref, pad_ref, rows_ref, shift_ref, total_ref, all_ref, cells_ref,
):
    coarse = coarse_cycle(
        [gathered_ref[g, :, 0:128] for g in range(8)], [gathered_ref[g, :, 128:256] for g in range(8)]
    )
    place_correction(coarse, place_ref, pad_ref, rows_ref, shift_ref)

    def correct(s, carry):
        iterate_ref[s] = inverse_ref[s] * field_ref[s] + shift_ref[pl.ds(s, 1), :]
        return carry

    lax.fori_loop(0, SLABS, correct, 0)

    def smooth(s, g, value):
        at = (s, pl.ds(8 * g, 8))
        smooth_ref[at] = iterate_ref[at] + inverse_ref[at] * (field_ref[at] - value)

    def smooth_pair(i, carry):
        apply_pair(iterate_ref, 2 * i + 1, packed_ref, class_ref, weights_ref, smooth)
        return carry

    for i in range(7):
        smooth_pair(i, 0)

    def store(s, g, value):
        image_ref[s, pl.ds(8 * g, 8)] = value

    def image_pair(i, carry):
        apply_pair(smooth_ref, 2 * i + 2, packed_ref, class_ref, weights_ref, store)
        return carry

    for i in range(6):
        image_pair(i, 0)
    for s in (0, 1, 14, 15):
        image_ref[s] = jnp.zeros((64, 128), F32)
    restrict(image_ref, inverse_ref, sums_ref, weights_ref, total_ref, all_ref, cells_ref)
    payload_ref[:, 0:128] = payload(cells_ref[...], place_ref, 1.0 / NODES)
    compact(smooth_ref, own_direction_ref)
    compact(image_ref, own_image_ref)
    direction = own_direction_ref[...]
    gamma = jnp.sum(jnp.sum(own_right(right_ref) * direction, axis=0, keepdims=True), axis=1, keepdims=True)
    delta = jnp.sum(jnp.sum(direction * own_image_ref[...], axis=0, keepdims=True), axis=1, keepdims=True)
    lane = iota((1, 128), 1)
    payload_ref[:, 128:256] = jnp.where(lane == 0, gamma, jnp.where(lane == 1, delta, 0.0))


def second_kernel(
    place_ref, weights_ref, gathered_ref, shifts_ref, image_ref, class_ref, inverse_ref, packed_ref, right_ref,
    own_direction_ref, own_image_ref,
    residual_ref, smoothed_ref, applied_ref, known_ref, payload_ref,
    iterate_ref, smooth_ref, second_ref, pad_ref, rows_ref, shift_ref, turned_ref,
):
    coarse = coarse_cycle(
        [gathered_ref[g, :, 0:128] for g in range(8)], [shifts_ref[g, :, 128:256] for g in range(8)]
    )
    place_correction(coarse, place_ref, pad_ref, rows_ref, shift_ref)

    def correct(s, carry):
        iterate_ref[s] = inverse_ref[s] * image_ref[s] + shift_ref[pl.ds(s, 1), :]
        return carry

    lax.fori_loop(2, 14, correct, 0)

    def smooth(s, g, value):
        at = (s, pl.ds(8 * g, 8))
        smooth_ref[at] = iterate_ref[at] + inverse_ref[at] * (image_ref[at] - value)

    def smooth_pair(i, carry):
        apply_pair(iterate_ref, 2 * i + 3, packed_ref, class_ref, weights_ref, smooth)
        return carry

    for i in range(5):
        smooth_pair(i, 0)

    def store(s, g, value):
        second_ref[s, pl.ds(8 * g, 8)] = value

    def second_pair(i, carry):
        apply_pair(smooth_ref, 2 * i + 4, packed_ref, class_ref, weights_ref, store)
        return carry

    for i in range(4):
        second_pair(i, 0)

    sums = gathered_ref[0, :, 128:256]
    for g in range(1, 8):
        sums = sums + gathered_ref[g, :, 128:256]
    sums = jnp.sum(sums, axis=0, keepdims=True)
    known_ref[...] = sums
    step = sums[:, 0:1] / sums[:, 1:2]
    compact(smooth_ref, turned_ref)
    smoothed = own_direction_ref[...] - step * turned_ref[...]
    smoothed_ref[...] = smoothed
    compact(second_ref, turned_ref)
    applied = own_image_ref[...] - step * turned_ref[...]
    applied_ref[...] = applied
    residual = own_right(right_ref) - step * own_image_ref[...]
    residual_ref[...] = residual

    def total(values):
        return jnp.sum(jnp.sum(values, axis=0, keepdims=True), axis=1, keepdims=True)

    lane = iota((1, 128), 1)
    cross = own_direction_ref[...] * applied + own_image_ref[...] * smoothed
    row = jnp.where(lane == 0, total(residual * smoothed), 0.0)
    row = jnp.where(lane == 1, total(smoothed * applied), row)
    payload_ref[...] = jnp.where(lane == 2, total(cross), row)


def last_kernel(
    parts_ref, known_ref, direction_ref, own_image_ref, smoothed_ref, applied_ref, residual_ref, field_ref, out_ref
):
    totals = parts_ref[0]
    for gx in range(1, 8):
        totals = totals + parts_ref[gx]
    gamma, delta = known_ref[:, 0:1], known_ref[:, 1:2]
    beta = totals[:, 0:1] / gamma
    step = totals[:, 0:1] / (totals[:, 1:2] + beta * (totals[:, 2:3] + beta * delta))
    direction = direction_ref[...]
    field = (gamma / delta) * direction + step * (smoothed_ref[...] + beta * direction)
    residual = residual_ref[...] - step * (applied_ref[...] + beta * own_image_ref[...])
    for x in range(4):
        field_ref[x] = field[2 * x : 2 * x + 2]
        out_ref[x] = residual[2 * x : 2 * x + 2]


VMEM = pl.BlockSpec(memory_space=pltpu.VMEM)
SMEM = pl.BlockSpec(memory_space=pltpu.SMEM)


def call(body, scalars, out_shape, scratch, *args):
    specs = [SMEM] * scalars + [VMEM] * (len(args) - scalars)
    shapes = [jax.ShapeDtypeStruct(shape, dtype) for shape, dtype in out_shape]
    return pl.pallas_call(
        body,
        out_shape=shapes,
        in_specs=specs,
        out_specs=[VMEM] * len(shapes),
        scratch_shapes=[pltpu.VMEM(shape, F32) for shape in scratch],
        compiler_params=pltpu.CompilerParams(vmem_limit_bytes=16 * 1024 * 1024),
    )(*args)


FIELD = (SLABS, NODES, 128)
COARSE_SCRATCH = [(10, 24, 128), (16, 128), (16, 128)]
SUM_SCRATCH = [(SLABS, 8, 128), (SLABS, 8, 128), (8, 128)]
OWN = (8, 512)


def start_call(*args):
    shapes = [(FIELD, F32), ((SLABS, 128), jnp.int32), (FIELD, F32), (FIELD, F32), ((1, 256), F32)]
    return call(start_kernel, 3, shapes, SUM_SCRATCH, *args)


def first_call(*args):
    shapes = [(FIELD, F32), (OWN, F32), (OWN, F32), ((1, 256), F32)]
    return call(first_kernel, 2, shapes, [FIELD, FIELD] + COARSE_SCRATCH + SUM_SCRATCH, *args)


def second_call(*args):
    shapes = [(OWN, F32), (OWN, F32), (OWN, F32), ((1, 128), F32), ((1, 128), F32)]
    return call(second_kernel, 2, shapes, [FIELD, FIELD, FIELD] + COARSE_SCRATCH + [OWN], *args)


def shifted(x, axis, step):
    size = lax.axis_size(axis)
    pairs = [(i, i + step) for i in range(size) if 0 <= i + step < size]
    return lax.ppermute(x, axis, pairs)


def extend(own):
    wide = jnp.concatenate([shifted(own, "gx", 1), own, shifted(own, "gx", -1)], axis=0)
    middle = jnp.concatenate(
        [
            shifted(wide, "gy", 2), shifted(wide, "gy", 1), wide, shifted(wide, "gy", -1), shifted(wide, "gy", -2),
        ],
        axis=0,
    )
    low = shifted(middle[:, 256:640], "gz", 1)
    high = shifted(middle[:, 0:384], "gz", -1)
    return middle, low, high


def gather_cells(row):
    parts = lax.all_to_all(jnp.broadcast_to(row[None], (128, 1, 256)), ("gy", "gz"), 0, 0, tiled=True)
    plane = parts.reshape(16, 8, 256).sum(axis=0)
    return lax.all_to_all(jnp.broadcast_to(plane[None], (8, 8, 256)), "gx", 0, 0, tiled=True)


def gather_sum(row):
    parts = lax.all_to_all(jnp.broadcast_to(row[None], (128, 1, 128)), ("gy", "gz"), 0, 0, tiled=True)
    part = parts.reshape(128, 128).sum(axis=0)
    return lax.all_to_all(jnp.broadcast_to(part[None, None], (8, 1, 128)), "gx", 0, 0, tiled=True)


def per_device(right_side, element_class, class_blocks, class_shift, face_weights):
    place = jnp.stack([lax.axis_index(axis) for axis in AXES]).astype(jnp.int32)
    own = call(own_kernel, 0, [((8, 640), F32)], [], right_side, element_class)[0]
    middle, low, high = extend(own)
    packed, table = call(
        pack_kernel, 0, [((CLASSES * NODES, 384), jnp.bfloat16), ((128, 48), jnp.bfloat16)], [], class_blocks
    )
    field, classes, inverse, sums, row = start_call(place, face_weights, class_shift, middle, low, high, table)
    gathered = gather_cells(row)
    image, direction, own_image, row = first_call(
        place, face_weights, gathered, field, classes, inverse, sums, packed, own
    )
    again = gather_cells(row)
    residual, smoothed, applied, known, row = second_call(
        place, face_weights, again, gathered, image, classes, inverse, packed, own, direction, own_image
    )
    parts = gather_sum(row)
    shapes = [(right_side.shape, F32)] * 2
    return tuple(call(last_kernel, 0, shapes, [], parts, known, direction, own_image, smoothed, applied, residual))


def solution(mesh):
    in_specs = (P("gx", "gy", "gz"), P("gx", "gy", "gz"), P(), P(), P())
    out_specs = (P("gx", "gy", "gz"), P("gx", "gy", "gz"))
    return jax.shard_map(
        per_device, mesh=mesh, in_specs=in_specs, out_specs=out_specs, check_vma=False
    )
```

```python
import jax
import jax.numpy as jnp
from jax import lax
from jax.experimental import pallas as pl
from jax.experimental.pallas import tpu as pltpu
from jax.sharding import PartitionSpec as P

NODES = 64
CLASSES = 16
SLABS = 16
RELAX = 0.6
F32 = jnp.float32
HIGHEST = lax.Precision.HIGHEST
AXES = ("gx", "gy", "gz")


def dot(left, right):
    return jnp.dot(left, right, precision=HIGHEST, preferred_element_type=F32)


def iota(shape, dim):
    return lax.broadcasted_iota(jnp.int32, shape, dim)


def roll(values, shift, axis):
    return pltpu.roll(values, shift % values.shape[axis], axis)


def lane_places(shape):
    lane = iota(shape, len(shape) - 1)
    yd = (lane * 171) >> 12
    rest = lane - 24 * yd
    return rest >> 1, yd, rest & 1


def beside_1(v, lane, sub):
    a, b, gy = lane >> 6, (lane >> 4) & 3, lane & 15
    swapped = [roll(x, 64, 1) for x in v]
    result = []
    for gx in range(8):
        x = v[gx]
        total = swapped[gx] + jnp.where((gy & 1) == 0, roll(x, -1, 1), roll(x, 1, 1))
        if gx % 2 == 0:
            total = total + jnp.where(a == 1, swapped[gx + 1], 0.0)
        else:
            total = total + jnp.where(a == 0, swapped[gx - 1], 0.0)
        after = jnp.where((sub & 1) == 0, roll(roll(x, -1, 0), 48, 1), 0.0)
        before = jnp.where((sub & 1) == 1, roll(roll(x, 1, 0), -48, 1), 0.0)
        total = total + jnp.where(b < 3, roll(x, -16, 1), after)
        total = total + jnp.where(b > 0, roll(x, 16, 1), before)
        result.append(total)
    return result


def beside_2(v, lane, sub):
    b, gy = (lane >> 4) & 3, lane & 15
    result = []
    for gx in range(8):
        x = v[gx]
        total = jnp.where((gy & 2) == 0, roll(x, -2, 1), roll(x, 2, 1))
        if gx % 4 < 3:
            total = total + v[gx + 1]
        if gx % 4 > 0:
            total = total + v[gx - 1]
        after = jnp.where((sub & 3) < 3, roll(roll(x, -1, 0), 32, 1), 0.0)
        before = jnp.where((sub & 3) > 0, roll(roll(x, 1, 0), -32, 1), 0.0)
        total = total + jnp.where(b < 2, roll(x, -32, 1), after)
        total = total + jnp.where(b >= 2, roll(x, 32, 1), before)
        result.append(total)
    return result


def beside_3(v, lane, sub):
    gy = lane & 15
    result = []
    for gx in range(8):
        x = v[gx]
        total = jnp.where((gy & 4) == 0, roll(x, -4, 1), roll(x, 4, 1))
        if gx + 2 < 8:
            total = total + v[gx + 2]
        if gx - 2 >= 0:
            total = total + v[gx - 2]
        total = total + jnp.where(sub < 7, roll(x, -1, 0), 0.0)
        total = total + jnp.where(sub > 0, roll(x, 1, 0), 0.0)
        result.append(total)
    return result


def coarsen_1(v, lane):
    b, gy = (lane >> 4) & 3, lane & 15
    result = []
    for x in v:
        x = x + roll(x, 64, 1)
        x = x + jnp.where((b & 1) == 0, roll(x, -16, 1), roll(x, 16, 1))
        x = x + jnp.where((gy & 1) == 0, roll(x, -1, 1), roll(x, 1, 1))
        result.append(x)
    return result


def coarsen_2(v, lane):
    b, gy = (lane >> 4) & 3, lane & 15
    result = []
    for gx in range(8):
        x = v[gx] + v[gx ^ 1]
        x = x + jnp.where(b < 2, roll(x, -32, 1), roll(x, 32, 1))
        x = x + jnp.where((gy & 2) == 0, roll(x, -2, 1), roll(x, 2, 1))
        result.append(x)
    return result


def coarse_cycle(source, shift):
    lane, sub = iota((8, 128), 1), iota((8, 128), 0)
    eight = range(8)

    def remainder(beside, q, d, x):
        around = beside(x, lane, sub)
        return [q[i] - (d[i] * x[i] - around[i]) for i in eight]

    d1 = [6.0 + s for s in shift]
    shift2 = [0.125 * s for s in coarsen_1(shift, lane)]
    d2 = [6.0 + s for s in shift2]
    d3 = [6.0 + 0.125 * s for s in coarsen_2(shift2, lane)]
    w1 = [RELAX / d for d in d1]
    w2 = [RELAX / d for d in d2]
    w3 = [RELAX / d for d in d3]
    x1 = [w1[i] * source[i] for i in eight]
    q2 = [0.25 * t for t in coarsen_1(remainder(beside_1, source, d1, x1), lane)]
    x2 = [w2[i] * q2[i] for i in eight]
    q3 = [0.25 * t for t in coarsen_2(remainder(beside_2, q2, d2, x2), lane)]
    x3 = [w3[i] * q3[i] for i in eight]
    for _ in range(3):
        t3 = remainder(beside_3, q3, d3, x3)
        x3 = [x3[i] + w3[i] * t3[i] for i in eight]
    x2 = [x2[i] + x3[i] for i in eight]
    t2 = remainder(beside_2, q2, d2, x2)
    x2 = [x2[i] + w2[i] * t2[i] for i in eight]
    x1 = [x1[i] + x2[i] for i in eight]
    t1 = remainder(beside_1, source, d1, x1)
    return [x1[i] + w1[i] * t1[i] for i in eight]


def place_correction(coarse, place_ref, pad_ref, rows_ref, out_ref):
    gx0, gy0, gz0 = place_ref[0], place_ref[1], place_ref[2]
    pad_ref[...] = jnp.zeros_like(pad_ref)
    for gx in range(8):
        pad_ref[gx + 1, 8:16, :] = coarse[gx]
    rows_ref[...] = jnp.zeros_like(rows_ref)
    for e in range(3):
        for d in range(3):
            rows_ref[3 * e + d : 3 * e + d + 1, :] = pad_ref[gx0 + d, pl.ds(gz0 + 7 + e, 1), :]
    shape = (128, 512)
    source = iota(shape, 0)
    column = iota(shape, 1)
    target = column & 127
    yd = (target * 171) >> 12
    x = (target - 24 * yd) >> 1
    hit = ((source >> 4) & 3) == (column >> 7)
    hit = hit & ((source >> 6) == ((x >> 1) & 1))
    hit = hit & ((source & 15) == gy0 - 2 + yd) & (target < 120)
    spread = dot(rows_ref[...], jnp.where(hit, 1.0, 0.0))
    lane_x, _, _ = lane_places((1, 128))
    part = lane_x >> 2
    for t in range(8):
        e, b = (t + 2) // 4, (t + 2) % 4
        pieces = [spread[3 * e + d : 3 * e + d + 1, 128 * b : 128 * b + 128] for d in range(3)]
        row = jnp.where(part == 0, pieces[0], jnp.where(part == 1, pieces[1], pieces[2]))
        out_ref[2 * t : 2 * t + 1, :] = row
        out_ref[2 * t + 1 : 2 * t + 2, :] = row


def groups(values):
    return [values[8 * g : 8 * g + 8] for g in range(8)]


def packed_places(shape):
    lane = iota(shape, len(shape) - 1)
    rest = (lane & 63) + 4
    yd = 1 + ((rest * 171) >> 12)
    rest = rest - 24 * (yd - 1)
    return rest >> 1, yd, rest & 1, lane >> 6


def dense(values, marks, packed_ref):
    first = values.astype(jnp.bfloat16)
    rest = values - first.astype(F32)
    second = rest.astype(jnp.bfloat16)
    third = (rest - second.astype(F32)).astype(jnp.bfloat16)
    stack = jnp.concatenate([first, second, third, first, second, first], axis=0)
    products = jnp.dot(packed_ref[...], stack, preferred_element_type=F32)
    result = []
    for part, row in enumerate(marks):
        row = jnp.broadcast_to(row, (8, 128))
        columns = slice(128 * part, 128 * part + 128)
        chosen = [products[8 * g : 8 * g + 8, columns] for g in range(8)]
        for k in range(1, CLASSES):
            hit = row == k
            for g in range(8):
                at = 64 * k + 8 * g
                chosen[g] = jnp.where(hit, products[at : at + 8, columns], chosen[g])
        result.append(chosen)
    return result


class Full:
    def __init__(self, slab):
        self.parts = groups(slab)
        self.yi = lane_places((8, 128))[2]

    def here(self, g):
        return self.parts[g]

    def shift(self, g, step):
        return roll(self.parts[g], -step, 1)


class Pack:
    def __init__(self, low, high):
        self.low, self.high = groups(low), groups(high)
        self.yi = packed_places((8, 128))[2]

    def here(self, g):
        return self.shift(g, 0)

    def shift(self, g, step):
        lane = iota((8, 128), 1)
        return jnp.where(lane < 64, roll(self.low[g], -28 - step, 1), roll(self.high[g], 36 - step, 1))


class Block(Full):
    def __init__(self, block):
        self.parts = groups(block)
        self.yi = packed_places((8, 128))[2]


def upward_y(view, g):
    return jnp.where(view.yi == 0, view.shift(g, 1), view.shift(g, 23))


def downward_y(view, g):
    return jnp.where(view.yi == 1, view.shift(g, -1), view.shift(g, -23))


def face_weights_of(weights_ref):
    sub = iota((8, 128), 0)
    wx, wy, wz = weights_ref[0], weights_ref[1], weights_ref[2]
    top = jnp.where((sub & 3) == 3, wz, 0.0), jnp.where(sub >= 4, wy, 0.0)
    bottom = jnp.where((sub & 3) == 0, wz, 0.0), jnp.where(sub < 4, wy, 0.0)
    return wx, top, bottom


def coupling(before, view, after, weights_ref):
    wx, (wz_top, wy_top), (wz_bottom, wy_bottom) = face_weights_of(weights_ref)
    result = []
    for g in range(8):
        term = wz_top * roll(after[g], 3, 0) + wz_bottom * roll(before[g], -3, 0)
        if g % 2 == 1:
            term = term + wy_top * roll(upward_y(view, g - 1), 4, 0)
        else:
            term = term + wy_bottom * roll(downward_y(view, g + 1), 4, 0)
        if g >= 6:
            term = term + wx * view.shift(g - 6, 2)
        if g < 2:
            term = term + wx * view.shift(g + 6, -2)
        result.append(term)
    return result


def constant_coupling(before, here, after, yi, weights_ref):
    wx, (wz_top, wy_top), (wz_bottom, wy_bottom) = face_weights_of(weights_ref)

    def wide(row):
        return jnp.broadcast_to(row, (8, 128))

    here = wide(here)
    up = jnp.where(yi == 0, roll(here, -1, 1), roll(here, -23, 1))
    down = jnp.where(yi == 1, roll(here, 1, 1), roll(here, 23, 1))
    along = wz_top * wide(after) + wz_bottom * wide(before)
    even, odd = along + wy_bottom * down, along + wy_top * up
    result = [even if g % 2 == 0 else odd for g in range(8)]
    for g in (0, 1):
        result[g] = result[g] + wx * roll(here, 2, 1)
    for g in (6, 7):
        result[g] = result[g] + wx * roll(here, -2, 1)
    return result


def block_before(ref, j):
    return ref[j - 1] if j > 0 else roll(ref[5], 64, 1)


def block_after(ref, j):
    return ref[j + 1] if j < 5 else roll(ref[0], 64, 1)


def restrict(source_ref, inverse_ref, sums_ref, weights_ref, all_ref, out_ref):
    wx, (wz_top, wy_top), (wz_bottom, wy_bottom) = face_weights_of(weights_ref)
    _, _, yi, _ = packed_places((8, 128))
    totals = []
    for j in range(6):
        r = source_ref[j]
        x = inverse_ref[j] * r
        d = groups(r - sums_ref[j] * x)
        xs = groups(x)
        even = (xs[0] + xs[2]) + (xs[4] + xs[6])
        odd = (xs[1] + xs[3]) + (xs[5] + xs[7])
        local = ((d[0] + d[1]) + (d[2] + d[3])) + ((d[4] + d[5]) + (d[6] + d[7]))
        local = local + wx * (roll(xs[0] + xs[1], -2, 1) + roll(xs[6] + xs[7], 2, 1))
        local = local + wy_bottom * jnp.where(yi == 0, roll(even, -1, 1), roll(even, -23, 1))
        local = local + wy_top * jnp.where(yi == 1, roll(odd, 1, 1), roll(odd, 23, 1))
        totals.append(local)
        all_ref[j] = even + odd
    out_ref[...] = jnp.zeros_like(out_ref)
    for j in range(6):
        value = totals[j] + wz_bottom * block_after(all_ref, j) + wz_top * block_before(all_ref, j)
        out_ref[j : j + 1, :] = jnp.sum(value, axis=0, keepdims=True)


def payload(cells, place_ref, scale):
    shape = (128, 256)
    source, column = iota(shape, 0), iota(shape, 1)
    target, own = column & 127, (source & 63) - 28
    hit = (own >= 0) & (own < 8) & ((source >> 6) == (column >> 7))
    hit = hit & ((own >> 2) == (target >> 6)) & ((target & 15) == place_ref[1])
    spread = dot(cells, jnp.where(hit, scale, 0.0))
    block, column = iota((8, 256), 0), iota((8, 256), 1)
    z = block - 2 + 6 * (column >> 7)
    keep = (block < 6) & (z >= 0) & (z < 8) & ((z >> 1) == ((column >> 4) & 3))
    row = jnp.sum(jnp.where(keep, spread, 0.0), axis=0, keepdims=True)
    return row[:, 0:128] + row[:, 128:256]


def gather_own(planes):
    lane = iota((64, 128), 1)
    result = jnp.zeros((64, 128), F32)
    for z, (plane, first) in enumerate(planes):
        result = jnp.where((lane >> 3) == z, roll(plane, 8 * z - first, 1), result)
    return result


def own_of_packed(blocks):
    return gather_own([(blocks[z + 2], 28) if z < 4 else (blocks[z - 4], 92) for z in range(8)])


def own_rows(first, second, first_ref, second_ref):
    turned = jnp.concatenate([first, second], axis=0).T
    low = iota((8, 128), 1) < 64
    for pair in range(4):
        even = turned[16 * pair : 16 * pair + 8]
        odd = turned[16 * pair + 8 : 16 * pair + 16]
        columns = slice(128 * pair, 128 * pair + 128)
        first_ref[:, columns] = jnp.where(low, even, roll(odd, 64, 1))
        second_ref[:, columns] = jnp.where(low, roll(even, 64, 1), odd)


def coefficients(rows, table_ref):
    halves = []
    for row in rows:
        wide = jnp.broadcast_to(row, (CLASSES, 128))
        halves.append(jnp.where(wide == iota((CLASSES, 128), 0), 1.0, 0.0))
    onehot = jnp.concatenate(halves, axis=1)
    onehot = jnp.concatenate([onehot] * 3, axis=0).astype(jnp.bfloat16)
    return jnp.dot(table_ref[...], onehot, preferred_element_type=F32)


def relaxation(x, yd, slab, place_ref):
    gx, gy = place_ref[0] - 1 + (x >> 2), place_ref[1] - 2 + yd
    gz = place_ref[2] - 1 + ((slab + 4) >> 3)
    inside = (gx >= 0) & (gx < 8) & (gy >= 0) & (gy < 16) & (gz >= 0) & (gz < 8) & (yd < 5)
    return jnp.where(inside, RELAX, 0.0)


def total(values):
    return jnp.sum(jnp.sum(values, axis=0, keepdims=True), axis=1, keepdims=True)


def own_right(own_ref):
    return jnp.concatenate([own_ref[:, 0:256], own_ref[:, 384:640]], axis=1)


def split(values):
    first = values.astype(jnp.bfloat16).astype(F32)
    rest = values - first
    second = rest.astype(jnp.bfloat16).astype(F32)
    return first, second, rest - second


def own_kernel(right_ref, marks_ref, out_ref):
    out_ref[:, 256:384] = jnp.zeros((8, 128), F32)
    for x in range(4):
        rows = slice(2 * x, 2 * x + 2)
        values = right_ref[x]
        out_ref[rows, 0:256] = values[:, 0:256]
        out_ref[rows, 384:640] = values[:, 256:512]
        out_ref[rows, 256:264] = marks_ref[x].astype(F32)


def pack_kernel(blocks_ref, packed_ref, table_ref):
    diagonal = jnp.where(iota((64, 64), 0) == iota((64, 64), 1), 1.0, 0.0)
    low = iota((64, 128), 1) < 64
    rows = []
    for k in range(CLASSES):
        block = blocks_ref[k]
        first, second, third = split(jnp.concatenate([block, block], axis=1))
        at = slice(64 * k, 64 * k + 64)
        packed_ref[at, 0:128] = first.astype(jnp.bfloat16)
        packed_ref[at, 128:256] = jnp.where(low, first, second).astype(jnp.bfloat16)
        packed_ref[at, 256:384] = jnp.where(low, second, third).astype(jnp.bfloat16)
        diag = jnp.sum(block * diagonal, axis=0, keepdims=True)
        rows.append(jnp.concatenate([diag, jnp.sum(block, axis=0, keepdims=True)], axis=1))
    parts = split(jnp.concatenate(rows, axis=0))
    table = jnp.concatenate(list(parts) + [jnp.zeros((80, 128), F32)], axis=0).T
    table_ref[...] = table[:, 0:48].astype(jnp.bfloat16)


def start_kernel(
    place_ref, weights_ref, class_shift_ref, below_ref, here_ref, above_ref, table_ref,
    class_ref, inverse_ref, sums_ref, payload_ref,
    field_ref, all_ref, cells_ref,
):
    def window(block):
        columns = slice(128 * block, 128 * block + 128)
        return jnp.concatenate([below_ref[4:24, columns], here_ref[:, columns], above_ref[0:20, columns]], axis=0)

    for j in (0, 2, 4):
        both = jnp.concatenate([window(2 + j // 2), window(5 + j // 2)], axis=0).T
        field_ref[j] = both[:64]
        field_ref[j + 1] = both[64:]
    marks = window(0)
    marks = jnp.concatenate([marks, marks], axis=0).T[0:16].astype(jnp.int32)
    low = iota((1, 128), 1) < 64
    class_ref[...] = jnp.zeros((8, 128), jnp.int32)
    x, yd, _, half = packed_places((1, 128))
    for j in range(6):
        class_ref[j : j + 1, :] = jnp.where(low, marks[2 + j : 3 + j], marks[8 + j : 9 + j])
    for j in (0, 2, 4):
        both = coefficients([class_ref[j : j + 1, :], class_ref[j + 1 : j + 2, :]], table_ref)
        for part in range(2):
            columns = slice(128 * part, 128 * part + 128)
            relax = relaxation(x, yd, 2 + j + part + 6 * half, place_ref)
            inverse_ref[j + part] = relax / both[:64, columns]
            sums_ref[j + part] = both[64:, columns]
    restrict(field_ref, inverse_ref, sums_ref, weights_ref, all_ref, cells_ref)
    shifts = jnp.zeros((8, 128), F32)
    for k in range(CLASSES):
        shifts = jnp.where(class_ref[...] == k, class_shift_ref[k], shifts)
    payload_ref[:, 0:128] = payload(cells_ref[...], place_ref, 1.0 / NODES)
    payload_ref[:, 128:256] = payload(shifts, place_ref, 0.125)


def local_kernel(
    place_ref, weights_ref, far_below_ref, below_ref, here_ref, above_ref, far_above_ref, table_ref, packed_ref,
    smooth_ref, inverse_ref, keep_ref,
    field_ref, iterate_ref, class_ref,
):
    def turned(block):
        columns = slice(128 * block, 128 * block + 128)
        middle = [ref[:, columns] for ref in (below_ref, here_ref, above_ref)]
        nothing = jnp.zeros((24, 128), F32)
        first = far_below_ref[:, columns] if block < 8 else nothing
        last = far_above_ref[:, columns] if block < 8 else nothing
        return jnp.concatenate([first] + middle + [last, jnp.zeros((8, 128), F32)], axis=0).T

    class_ref[...] = turned(0)[0:16].astype(jnp.int32)
    x, yd, _ = lane_places((1, 128))
    for pair in range(SLABS // 2):
        block = turned(pair + 1)
        both = coefficients([class_ref[2 * pair + i : 2 * pair + i + 1, :] for i in (0, 1)], table_ref)
        for part in range(2):
            s = 2 * pair + part
            columns = slice(128 * part, 128 * part + 128)
            values = block[64 * part : 64 * part + 64]
            inverse = relaxation(x, yd, s, place_ref) / both[:64, columns]
            field_ref[s] = values
            inverse_ref[s] = inverse
            keep_ref[s] = 1.0 - inverse * both[64:, columns]
            iterate_ref[s] = inverse * values
    for s in (0, 15):
        smooth_ref[s] = jnp.zeros((64, 128), F32)
    for s in range(1, 14, 2):
        planes = [iterate_ref[s + i] for i in (-1, 0, 1, 2)]
        marks = [class_ref[s + i : s + i + 1, :] for i in (0, 1)]
        chosen = dense(jnp.concatenate(planes[1:3], axis=1), marks, packed_ref)
        for part in range(2):
            faces = coupling(groups(planes[part]), Full(planes[part + 1]), groups(planes[part + 2]), weights_ref)
            for g in range(8):
                at = (s + part, slice(8 * g, 8 * g + 8))
                value = chosen[part][g] - faces[g]
                smooth_ref[at] = iterate_ref[at] + inverse_ref[at] * (field_ref[at] - value)


def first_kernel(
    place_ref, weights_ref, gathered_ref, local_ref, inverse_ref, keep_ref, class_ref, near_inverse_ref, sums_ref,
    packed_ref, right_ref,
    image_ref, own_direction_ref, own_image_ref, payload_ref,
    smooth_ref, pad_ref, rows_ref, shift_ref, all_ref, cells_ref,
):
    coarse = coarse_cycle(
        [gathered_ref[g, :, 0:128] for g in range(8)], [gathered_ref[g, :, 128:256] for g in range(8)]
    )
    place_correction(coarse, place_ref, pad_ref, rows_ref, shift_ref)
    _, _, yi = lane_places((8, 128))
    for s in range(1, 15):
        here = shift_ref[s : s + 1, :]
        faces = constant_coupling(shift_ref[s - 1 : s, :], here, shift_ref[s + 1 : s + 2, :], yi, weights_ref)
        here = jnp.broadcast_to(here, (8, 128))
        for g in range(8):
            at = (s, slice(8 * g, 8 * g + 8))
            smooth_ref[at] = local_ref[at] + (keep_ref[at] * here + inverse_ref[at] * faces[g])

    lane = iota((64, 128), 1)

    def block(j):
        return jnp.where(lane < 64, roll(smooth_ref[2 + j], -28, 1), roll(smooth_ref[8 + j], 36, 1))

    blocks = [block(j) for j in range(-1, 7)]
    for j in (0, 2, 4):
        marks = [class_ref[j + i : j + i + 1, :] for i in (0, 1)]
        chosen = dense(jnp.concatenate([blocks[j + 1], blocks[j + 2]], axis=1), marks, packed_ref)
        for part in range(2):
            at = j + part
            view = Pack(smooth_ref[2 + at], smooth_ref[8 + at])
            faces = coupling(groups(blocks[at]), view, groups(blocks[at + 2]), weights_ref)
            for g in range(8):
                image_ref[at, 8 * g : 8 * g + 8] = chosen[part][g] - faces[g]
    restrict(image_ref, near_inverse_ref, sums_ref, weights_ref, all_ref, cells_ref)
    payload_ref[:, 0:128] = payload(cells_ref[...], place_ref, 1.0 / NODES)
    own_z = gather_own([(smooth_ref[z + 4], 56) for z in range(8)])
    own_rows(own_z, own_of_packed(image_ref), own_direction_ref, own_image_ref)
    direction = own_direction_ref[...]
    lane = iota((1, 128), 1)
    gamma, delta = total(own_right(right_ref) * direction), total(direction * own_image_ref[...])
    payload_ref[:, 128:256] = jnp.where(lane == 0, gamma, jnp.where(lane == 1, delta, 0.0))


def near_kernel(
    weights_ref, image_ref, class_ref, inverse_ref, packed_ref,
    smooth_ref,
    iterate_ref,
):
    for j in range(6):
        iterate_ref[j] = inverse_ref[j] * image_ref[j]
    for j in (0, 2, 4):
        marks = [class_ref[j + i : j + i + 1, :] for i in (0, 1)]
        chosen = dense(jnp.concatenate([iterate_ref[j], iterate_ref[j + 1]], axis=1), marks, packed_ref)
        for part in range(2):
            at = j + part
            before, after = groups(block_before(iterate_ref, at)), groups(block_after(iterate_ref, at))
            faces = coupling(before, Block(iterate_ref[at]), after, weights_ref)
            for g in range(8):
                place = (at, slice(8 * g, 8 * g + 8))
                value = chosen[part][g] - faces[g]
                smooth_ref[place] = iterate_ref[place] + inverse_ref[place] * (image_ref[place] - value)


def second_kernel(
    place_ref, weights_ref, gathered_ref, shifts_ref, local_ref, class_ref, inverse_ref, sums_ref, packed_ref,
    right_ref, own_direction_ref, own_image_ref,
    residual_ref, smoothed_ref, applied_ref, known_ref, payload_ref,
    smooth_ref, pad_ref, rows_ref, shift_ref, turned_ref, image_ref, near_ref,
):
    coarse = coarse_cycle(
        [gathered_ref[g, :, 0:128] for g in range(8)], [shifts_ref[g, :, 128:256] for g in range(8)]
    )
    place_correction(coarse, place_ref, pad_ref, rows_ref, shift_ref)
    lane = iota((8, 128), 1)
    near_ref[...] = jnp.where(lane < 64, roll(shift_ref[2:10, :], -28, 1), roll(shift_ref[8:16, :], 36, 1))
    _, _, yi, _ = packed_places((8, 128))

    def row(j):
        return near_ref[j : j + 1, :]

    for j in range(6):
        before = row(j - 1) if j > 0 else roll(row(5), 64, 1)
        after = row(j + 1) if j < 5 else roll(row(0), 64, 1)
        faces = constant_coupling(before, row(j), after, yi, weights_ref)
        here = jnp.broadcast_to(row(j), (8, 128))
        for g in range(8):
            at = (j, slice(8 * g, 8 * g + 8))
            inverse = inverse_ref[at]
            smooth_ref[at] = local_ref[at] + (here + inverse * (faces[g] - sums_ref[at] * here))

    own_y = own_of_packed(smooth_ref)
    own_marks = gather_own(
        [(jnp.broadcast_to(class_ref[j : j + 1, :].astype(F32), (64, 128)), first)
         for j, first in [(2, 28), (3, 28), (4, 28), (5, 28), (0, 92), (1, 92), (2, 92), (3, 92)]]
    )
    chosen = dense(own_y, [own_marks[0:1].astype(jnp.int32)], packed_ref)[0]
    for j in range(6):
        before, after = groups(block_before(smooth_ref, j)), groups(block_after(smooth_ref, j))
        faces = coupling(before, Block(smooth_ref[j]), after, weights_ref)
        for g in range(8):
            image_ref[j, 8 * g : 8 * g + 8] = faces[g]
    own_v = jnp.concatenate(chosen, axis=0) - own_of_packed(image_ref)

    sums = gathered_ref[0, :, 128:256]
    for g in range(1, 8):
        sums = sums + gathered_ref[g, :, 128:256]
    sums = jnp.sum(sums, axis=0, keepdims=True)
    known_ref[...] = sums
    step = sums[:, 0:1] / sums[:, 1:2]
    own_rows(own_y, own_v, smoothed_ref, turned_ref)
    smoothed = own_direction_ref[...] - step * smoothed_ref[...]
    smoothed_ref[...] = smoothed
    applied = own_image_ref[...] - step * turned_ref[...]
    applied_ref[...] = applied
    residual = own_right(right_ref) - step * own_image_ref[...]
    residual_ref[...] = residual
    lane = iota((1, 128), 1)
    cross = own_direction_ref[...] * applied + own_image_ref[...] * smoothed
    values = jnp.where(lane == 0, total(residual * smoothed), 0.0)
    values = jnp.where(lane == 1, total(smoothed * applied), values)
    payload_ref[...] = jnp.where(lane == 2, total(cross), values)


def last_kernel(
    parts_ref, known_ref, direction_ref, own_image_ref, smoothed_ref, applied_ref, residual_ref, field_ref, out_ref
):
    totals = parts_ref[0]
    for gx in range(1, 8):
        totals = totals + parts_ref[gx]
    gamma, delta = known_ref[:, 0:1], known_ref[:, 1:2]
    beta = totals[:, 0:1] / gamma
    step = totals[:, 0:1] / (totals[:, 1:2] + beta * (totals[:, 2:3] + beta * delta))
    direction = direction_ref[...]
    field = (gamma / delta) * direction + step * (smoothed_ref[...] + beta * direction)
    residual = residual_ref[...] - step * (applied_ref[...] + beta * own_image_ref[...])
    for x in range(4):
        field_ref[x] = field[2 * x : 2 * x + 2]
        out_ref[x] = residual[2 * x : 2 * x + 2]


VMEM = pl.BlockSpec(memory_space=pltpu.VMEM)
SMEM = pl.BlockSpec(memory_space=pltpu.SMEM)


def call(body, scalars, out_shape, scratch, *args, flops=10**7):
    specs = [SMEM] * scalars + [VMEM] * (len(args) - scalars)
    shapes = [jax.ShapeDtypeStruct(shape, dtype) for shape, dtype in out_shape]
    return pl.pallas_call(
        body,
        out_shape=shapes,
        in_specs=specs,
        out_specs=[VMEM] * len(shapes),
        scratch_shapes=[pltpu.VMEM(shape, dtype) for shape, dtype in scratch],
        cost_estimate=pl.CostEstimate(flops=flops, bytes_accessed=10**6, transcendentals=0),
        compiler_params=pltpu.CompilerParams(vmem_limit_bytes=16 * 1024 * 1024),
    )(*args)


FIELD = ((SLABS, NODES, 128), F32)
BLOCKS = ((6, NODES, 128), F32)
MARKS = ((8, 128), jnp.int32)
OWN = ((8, 512), F32)
CELLS = ((8, 128), F32)
ROW, WIDE = ((1, 128), F32), ((1, 256), F32)
COARSE_SCRATCH = [((10, 24, 128), F32), ((16, 128), F32), ((16, 128), F32)]
SUM_SCRATCH = [((6, 8, 128), F32), CELLS]
PAIR_FLOPS = 2 * 1024 * 384 * 256


def start_call(*args):
    return call(start_kernel, 3, [MARKS, BLOCKS, BLOCKS, WIDE], [BLOCKS] + SUM_SCRATCH, *args)


def local_call(*args):
    scratch = [FIELD, FIELD, ((SLABS, 128), jnp.int32)]
    return call(local_kernel, 2, [FIELD, FIELD, FIELD], scratch, *args, flops=7 * PAIR_FLOPS)


def first_call(*args):
    scratch = [FIELD] + COARSE_SCRATCH + SUM_SCRATCH
    return call(first_kernel, 2, [BLOCKS, OWN, OWN, WIDE], scratch, *args, flops=3 * PAIR_FLOPS)


def near_call(*args):
    return call(near_kernel, 1, [BLOCKS], [BLOCKS], *args, flops=3 * PAIR_FLOPS)[0]


def second_call(*args):
    scratch = [BLOCKS] + COARSE_SCRATCH + [OWN, BLOCKS, CELLS]
    return call(second_kernel, 2, [OWN, OWN, OWN, ROW, ROW], scratch, *args, flops=PAIR_FLOPS)


def shifted(x, axis, step):
    size = lax.axis_size(axis)
    pairs = [(i, i + step) for i in range(size) if 0 <= i + step < size]
    return lax.ppermute(x, axis, pairs)


def extend_xz(own):
    wide = jnp.concatenate([shifted(own, "gx", 1), own, shifted(own, "gx", -1)], axis=0)
    low = shifted(wide[:, 256:640], "gz", 1)
    high = shifted(wide[:, 0:384], "gz", -1)
    nothing = jnp.zeros((24, 112), F32)
    pieces = [low[:, 4:8], wide[:, 256:264], high[:, 256:260], nothing]
    return jnp.concatenate(pieces + [low[:, 128:384], wide[:, 0:256], wide[:, 384:640], high[:, 0:256]], axis=1)


def gather_cells(row):
    parts = lax.all_to_all(jnp.broadcast_to(row[None], (128, 1, 256)), ("gy", "gz"), 0, 0, tiled=True)
    plane = parts.reshape(16, 8, 256).sum(axis=0)
    return lax.all_to_all(jnp.broadcast_to(plane[None], (8, 8, 256)), "gx", 0, 0, tiled=True)


def gather_sum(row):
    parts = lax.all_to_all(jnp.broadcast_to(row[None], (128, 1, 128)), ("gy", "gz"), 0, 0, tiled=True)
    part = parts.reshape(128, 128).sum(axis=0)
    return lax.all_to_all(jnp.broadcast_to(part[None, None], (8, 1, 128)), "gx", 0, 0, tiled=True)


def per_device(right_side, element_class, class_blocks, class_shift, face_weights):
    place = jnp.stack([lax.axis_index(axis) for axis in AXES]).astype(jnp.int32)
    own = call(own_kernel, 0, [((8, 640), F32)], [], right_side, element_class)[0]
    here = extend_xz(own)
    below, above = shifted(here, "gy", 1), shifted(here, "gy", -1)
    packed, table = call(
        pack_kernel, 0, [((CLASSES * NODES, 384), jnp.bfloat16), ((128, 48), jnp.bfloat16)], [], class_blocks
    )
    marks, near_inverse, sums, row = start_call(place, face_weights, class_shift, below, here, above, table)
    gathered = gather_cells(row)
    far_below, far_above = shifted(here[:, 0:1024], "gy", 2), shifted(here[:, 0:1024], "gy", -2)
    local, inverse, keep = local_call(
        place, face_weights, far_below, below, here, above, far_above, table, packed
    )
    image, direction, own_image, row = first_call(
        place, face_weights, gathered, local, inverse, keep, marks, near_inverse, sums, packed, own
    )
    again = gather_cells(row)
    near = near_call(face_weights, image, marks, near_inverse, packed)
    residual, smoothed, applied, known, row = second_call(
        place, face_weights, again, gathered, near, marks, near_inverse, sums, packed, own, direction, own_image
    )
    parts = gather_sum(row)
    shapes = [(right_side.shape, F32)] * 2
    return tuple(call(last_kernel, 0, shapes, [], parts, known, direction, own_image, smoothed, applied, residual))


def solution(mesh):
    in_specs = (P("gx", "gy", "gz"), P("gx", "gy", "gz"), P(), P(), P())
    out_specs = (P("gx", "gy", "gz"), P("gx", "gy", "gz"))
    return jax.shard_map(
        per_device, mesh=mesh, in_specs=in_specs, out_specs=out_specs, check_vma=False
    )
```

```python
import jax
import jax.numpy as jnp
from jax import lax
from jax.experimental import pallas as pl
from jax.experimental.pallas import tpu as pltpu
from jax.sharding import PartitionSpec as P

NODES = 64
CLASSES = 16
SLABS = 16
RELAX = 0.6
F32 = jnp.float32
HIGHEST = lax.Precision.HIGHEST
AXES = ("gx", "gy", "gz")


def dot(left, right):
    return jnp.dot(left, right, precision=HIGHEST, preferred_element_type=F32)


def iota(shape, dim):
    return lax.broadcasted_iota(jnp.int32, shape, dim)


def roll(values, shift, axis):
    return pltpu.roll(values, shift % values.shape[axis], axis)


def lane_places(shape):
    lane = iota(shape, len(shape) - 1)
    yd = (lane * 171) >> 12
    rest = lane - 24 * yd
    return rest >> 1, yd, rest & 1


def beside_1(v, lane, sub):
    a, b, gy = lane >> 6, (lane >> 4) & 3, lane & 15
    swapped = [roll(x, 64, 1) for x in v]
    result = []
    for gx in range(8):
        x = v[gx]
        total = swapped[gx] + jnp.where((gy & 1) == 0, roll(x, -1, 1), roll(x, 1, 1))
        if gx % 2 == 0:
            total = total + jnp.where(a == 1, swapped[gx + 1], 0.0)
        else:
            total = total + jnp.where(a == 0, swapped[gx - 1], 0.0)
        after = jnp.where((sub & 1) == 0, roll(roll(x, -1, 0), 48, 1), 0.0)
        before = jnp.where((sub & 1) == 1, roll(roll(x, 1, 0), -48, 1), 0.0)
        total = total + jnp.where(b < 3, roll(x, -16, 1), after)
        total = total + jnp.where(b > 0, roll(x, 16, 1), before)
        result.append(total)
    return result


def beside_2(v, lane, sub):
    b, gy = (lane >> 4) & 3, lane & 15
    result = []
    for gx in range(8):
        x = v[gx]
        total = jnp.where((gy & 2) == 0, roll(x, -2, 1), roll(x, 2, 1))
        if gx % 4 < 3:
            total = total + v[gx + 1]
        if gx % 4 > 0:
            total = total + v[gx - 1]
        after = jnp.where((sub & 3) < 3, roll(roll(x, -1, 0), 32, 1), 0.0)
        before = jnp.where((sub & 3) > 0, roll(roll(x, 1, 0), -32, 1), 0.0)
        total = total + jnp.where(b < 2, roll(x, -32, 1), after)
        total = total + jnp.where(b >= 2, roll(x, 32, 1), before)
        result.append(total)
    return result


def beside_3(v, lane, sub):
    gy = lane & 15
    result = []
    for gx in range(8):
        x = v[gx]
        total = jnp.where((gy & 4) == 0, roll(x, -4, 1), roll(x, 4, 1))
        if gx + 2 < 8:
            total = total + v[gx + 2]
        if gx - 2 >= 0:
            total = total + v[gx - 2]
        total = total + jnp.where(sub < 7, roll(x, -1, 0), 0.0)
        total = total + jnp.where(sub > 0, roll(x, 1, 0), 0.0)
        result.append(total)
    return result


def coarsen_1(v, lane):
    b, gy = (lane >> 4) & 3, lane & 15
    result = []
    for x in v:
        x = x + roll(x, 64, 1)
        x = x + jnp.where((b & 1) == 0, roll(x, -16, 1), roll(x, 16, 1))
        x = x + jnp.where((gy & 1) == 0, roll(x, -1, 1), roll(x, 1, 1))
        result.append(x)
    return result


def coarsen_2(v, lane):
    b, gy = (lane >> 4) & 3, lane & 15
    result = []
    for gx in range(8):
        x = v[gx] + v[gx ^ 1]
        x = x + jnp.where(b < 2, roll(x, -32, 1), roll(x, 32, 1))
        x = x + jnp.where((gy & 2) == 0, roll(x, -2, 1), roll(x, 2, 1))
        result.append(x)
    return result


def coarse_cycle(source, shift):
    lane, sub = iota((8, 128), 1), iota((8, 128), 0)
    eight = range(8)

    def remainder(beside, q, d, x):
        around = beside(x, lane, sub)
        return [q[i] - (d[i] * x[i] - around[i]) for i in eight]

    d1 = [6.0 + s for s in shift]
    shift2 = [0.125 * s for s in coarsen_1(shift, lane)]
    d2 = [6.0 + s for s in shift2]
    d3 = [6.0 + 0.125 * s for s in coarsen_2(shift2, lane)]
    w1 = [RELAX / d for d in d1]
    w2 = [RELAX / d for d in d2]
    w3 = [RELAX / d for d in d3]
    x1 = [w1[i] * source[i] for i in eight]
    q2 = [0.25 * t for t in coarsen_1(remainder(beside_1, source, d1, x1), lane)]
    x2 = [w2[i] * q2[i] for i in eight]
    q3 = [0.25 * t for t in coarsen_2(remainder(beside_2, q2, d2, x2), lane)]
    x3 = [w3[i] * q3[i] for i in eight]
    for _ in range(3):
        t3 = remainder(beside_3, q3, d3, x3)
        x3 = [x3[i] + w3[i] * t3[i] for i in eight]
    x2 = [x2[i] + x3[i] for i in eight]
    t2 = remainder(beside_2, q2, d2, x2)
    x2 = [x2[i] + w2[i] * t2[i] for i in eight]
    x1 = [x1[i] + x2[i] for i in eight]
    t1 = remainder(beside_1, source, d1, x1)
    return [x1[i] + w1[i] * t1[i] for i in eight]


def place_correction(coarse, place_ref, pad_ref, rows_ref, out_ref):
    gx0, gy0, gz0 = place_ref[0], place_ref[1], place_ref[2]
    pad_ref[...] = jnp.zeros_like(pad_ref)
    for gx in range(8):
        pad_ref[gx + 1, 8:16, :] = coarse[gx]
    rows_ref[...] = jnp.zeros_like(rows_ref)
    for e in range(3):
        for d in range(3):
            rows_ref[3 * e + d : 3 * e + d + 1, :] = pad_ref[gx0 + d, pl.ds(gz0 + 7 + e, 1), :]
    shape = (128, 512)
    source = iota(shape, 0)
    column = iota(shape, 1)
    target = column & 127
    yd = (target * 171) >> 12
    x = (target - 24 * yd) >> 1
    hit = ((source >> 4) & 3) == (column >> 7)
    hit = hit & ((source >> 6) == ((x >> 1) & 1))
    hit = hit & ((source & 15) == gy0 - 2 + yd) & (target < 120)
    spread = dot(rows_ref[...], jnp.where(hit, 1.0, 0.0))
    lane_x, _, _ = lane_places((1, 128))
    part = lane_x >> 2
    for t in range(8):
        e, b = (t + 2) // 4, (t + 2) % 4
        pieces = [spread[3 * e + d : 3 * e + d + 1, 128 * b : 128 * b + 128] for d in range(3)]
        row = jnp.where(part == 0, pieces[0], jnp.where(part == 1, pieces[1], pieces[2]))
        out_ref[2 * t : 2 * t + 1, :] = row
        out_ref[2 * t + 1 : 2 * t + 2, :] = row


def groups(values):
    return [values[8 * g : 8 * g + 8] for g in range(8)]


def packed_places(shape):
    lane = iota(shape, len(shape) - 1)
    rest = (lane & 63) + 4
    yd = 1 + ((rest * 171) >> 12)
    rest = rest - 24 * (yd - 1)
    return rest >> 1, yd, rest & 1, lane >> 6


def dense(values, marks, packed_ref):
    first = values.astype(jnp.bfloat16)
    rest = values - first.astype(F32)
    second = rest.astype(jnp.bfloat16)
    third = (rest - second.astype(F32)).astype(jnp.bfloat16)
    stack = jnp.concatenate([first, second, third, first, second, first], axis=0)
    products = jnp.dot(packed_ref[...], stack, preferred_element_type=F32)
    result = []
    for part, row in enumerate(marks):
        row = jnp.broadcast_to(row, (8, 128))
        columns = slice(128 * part, 128 * part + 128)
        chosen = [products[8 * g : 8 * g + 8, columns] for g in range(8)]
        for k in range(1, CLASSES):
            hit = row == k
            for g in range(8):
                at = 64 * k + 8 * g
                chosen[g] = jnp.where(hit, products[at : at + 8, columns], chosen[g])
        result.append(chosen)
    return result


class Full:
    def __init__(self, slab):
        self.parts = groups(slab)
        self.yi = lane_places((8, 128))[2]

    def here(self, g):
        return self.parts[g]

    def shift(self, g, step):
        return roll(self.parts[g], -step, 1)


class Pack:
    def __init__(self, low, high):
        self.low, self.high = groups(low), groups(high)
        self.yi = packed_places((8, 128))[2]

    def here(self, g):
        return self.shift(g, 0)

    def shift(self, g, step):
        lane = iota((8, 128), 1)
        return jnp.where(lane < 64, roll(self.low[g], -28 - step, 1), roll(self.high[g], 36 - step, 1))


class Block(Full):
    def __init__(self, block):
        self.parts = groups(block)
        self.yi = packed_places((8, 128))[2]


def upward_y(view, g):
    return jnp.where(view.yi == 0, view.shift(g, 1), view.shift(g, 23))


def downward_y(view, g):
    return jnp.where(view.yi == 1, view.shift(g, -1), view.shift(g, -23))


def face_weights_of(weights_ref):
    sub = iota((8, 128), 0)
    wx, wy, wz = weights_ref[0], weights_ref[1], weights_ref[2]
    top = jnp.where((sub & 3) == 3, wz, 0.0), jnp.where(sub >= 4, wy, 0.0)
    bottom = jnp.where((sub & 3) == 0, wz, 0.0), jnp.where(sub < 4, wy, 0.0)
    return wx, top, bottom


def coupling(before, view, after, weights_ref):
    wx, (wz_top, wy_top), (wz_bottom, wy_bottom) = face_weights_of(weights_ref)
    result = []
    for g in range(8):
        term = wz_top * roll(after[g], 3, 0) + wz_bottom * roll(before[g], -3, 0)
        if g % 2 == 1:
            term = term + wy_top * roll(upward_y(view, g - 1), 4, 0)
        else:
            term = term + wy_bottom * roll(downward_y(view, g + 1), 4, 0)
        if g >= 6:
            term = term + wx * view.shift(g - 6, 2)
        if g < 2:
            term = term + wx * view.shift(g + 6, -2)
        result.append(term)
    return result


def constant_coupling(before, here, after, yi, weights_ref):
    wx, (wz_top, wy_top), (wz_bottom, wy_bottom) = face_weights_of(weights_ref)

    def wide(row):
        return jnp.broadcast_to(row, (8, 128))

    here = wide(here)
    up = jnp.where(yi == 0, roll(here, -1, 1), roll(here, -23, 1))
    down = jnp.where(yi == 1, roll(here, 1, 1), roll(here, 23, 1))
    along = wz_top * wide(after) + wz_bottom * wide(before)
    even, odd = along + wy_bottom * down, along + wy_top * up
    result = [even if g % 2 == 0 else odd for g in range(8)]
    for g in (0, 1):
        result[g] = result[g] + wx * roll(here, 2, 1)
    for g in (6, 7):
        result[g] = result[g] + wx * roll(here, -2, 1)
    return result


def block_before(ref, j):
    return ref[j - 1] if j > 0 else roll(ref[5], 64, 1)


def block_after(ref, j):
    return ref[j + 1] if j < 5 else roll(ref[0], 64, 1)


def restrict(source_ref, inverse_ref, sums_ref, weights_ref, all_ref, out_ref):
    wx, (wz_top, wy_top), (wz_bottom, wy_bottom) = face_weights_of(weights_ref)
    _, _, yi, _ = packed_places((8, 128))
    totals = []
    for j in range(6):
        r = source_ref[j]
        x = inverse_ref[j] * r
        d = groups(r - sums_ref[j] * x)
        xs = groups(x)
        even = (xs[0] + xs[2]) + (xs[4] + xs[6])
        odd = (xs[1] + xs[3]) + (xs[5] + xs[7])
        local = ((d[0] + d[1]) + (d[2] + d[3])) + ((d[4] + d[5]) + (d[6] + d[7]))
        local = local + wx * (roll(xs[0] + xs[1], -2, 1) + roll(xs[6] + xs[7], 2, 1))
        local = local + wy_bottom * jnp.where(yi == 0, roll(even, -1, 1), roll(even, -23, 1))
        local = local + wy_top * jnp.where(yi == 1, roll(odd, 1, 1), roll(odd, 23, 1))
        totals.append(local)
        all_ref[j] = even + odd
    out_ref[...] = jnp.zeros_like(out_ref)
    for j in range(6):
        value = totals[j] + wz_bottom * block_after(all_ref, j) + wz_top * block_before(all_ref, j)
        out_ref[j : j + 1, :] = jnp.sum(value, axis=0, keepdims=True)


def payload(cells, place_ref, scale):
    shape = (128, 256)
    source, column = iota(shape, 0), iota(shape, 1)
    target, own = column & 127, (source & 63) - 28
    hit = (own >= 0) & (own < 8) & ((source >> 6) == (column >> 7))
    hit = hit & ((own >> 2) == (target >> 6)) & ((target & 15) == place_ref[1])
    spread = dot(cells, jnp.where(hit, scale, 0.0))
    block, column = iota((8, 256), 0), iota((8, 256), 1)
    z = block - 2 + 6 * (column >> 7)
    keep = (block < 6) & (z >= 0) & (z < 8) & ((z >> 1) == ((column >> 4) & 3))
    row = jnp.sum(jnp.where(keep, spread, 0.0), axis=0, keepdims=True)
    return row[:, 0:128] + row[:, 128:256]


def gather_own(planes):
    lane = iota((64, 128), 1)
    result = jnp.zeros((64, 128), F32)
    for z, (plane, first) in enumerate(planes):
        result = jnp.where((lane >> 3) == z, roll(plane, 8 * z - first, 1), result)
    return result


def own_of_packed(blocks):
    return gather_own([(blocks[z + 2], 28) if z < 4 else (blocks[z - 4], 92) for z in range(8)])


def own_rows(first, second, first_ref, second_ref):
    turned = jnp.concatenate([first, second], axis=0).T
    low = iota((8, 128), 1) < 64
    for pair in range(4):
        even = turned[16 * pair : 16 * pair + 8]
        odd = turned[16 * pair + 8 : 16 * pair + 16]
        columns = slice(128 * pair, 128 * pair + 128)
        first_ref[:, columns] = jnp.where(low, even, roll(odd, 64, 1))
        second_ref[:, columns] = jnp.where(low, roll(even, 64, 1), odd)


def coefficients(rows, table_ref):
    halves = []
    for row in rows:
        wide = jnp.broadcast_to(row, (CLASSES, 128))
        halves.append(jnp.where(wide == iota((CLASSES, 128), 0), 1.0, 0.0))
    onehot = jnp.concatenate(halves, axis=1)
    onehot = jnp.concatenate([onehot] * 3, axis=0).astype(jnp.bfloat16)
    return jnp.dot(table_ref[...], onehot, preferred_element_type=F32)


def relaxation(x, yd, slab, place_ref):
    gx, gy = place_ref[0] - 1 + (x >> 2), place_ref[1] - 2 + yd
    gz = place_ref[2] - 1 + ((slab + 4) >> 3)
    inside = (gx >= 0) & (gx < 8) & (gy >= 0) & (gy < 16) & (gz >= 0) & (gz < 8) & (yd < 5)
    return jnp.where(inside, RELAX, 0.0)


def total(values):
    return jnp.sum(jnp.sum(values, axis=0, keepdims=True), axis=1, keepdims=True)


def own_right(own_ref):
    return jnp.concatenate([own_ref[:, 0:256], own_ref[:, 384:640]], axis=1)


def split(values):
    first = values.astype(jnp.bfloat16).astype(F32)
    rest = values - first
    second = rest.astype(jnp.bfloat16).astype(F32)
    return first, second, rest - second


def cell_parts(own_ref, table, weights_ref, shift_ref):
    pieces = []
    for pair in range(4):
        start = 128 * pair if pair < 2 else 128 * pair + 128
        values = own_ref[:, start : start + 128]
        pieces += [values, roll(values, 64, 1)]
    b = jnp.concatenate(pieces + [jnp.zeros((64, 128), F32)], axis=0).T[0:64]
    turned = jnp.concatenate([own_ref[:, 256:384], jnp.zeros((120, 128), F32)], axis=0).T
    lane = iota((1, 128), 1)
    marks = jnp.zeros((1, 128), F32)
    for z in range(8):
        marks = jnp.where((lane >> 3) == z, roll(turned[z : z + 1], 8 * z, 1), marks)
    marks = marks.astype(jnp.int32)
    both = coefficients([marks], table)
    x0 = (RELAX / both[:64]) * b
    d, xs = groups(b - both[64:] * x0), groups(x0)
    wx, wy, wz = weights_ref[0], weights_ref[1], weights_ref[2]
    sub = iota((8, 128), 0)
    even = (xs[0] + xs[2]) + (xs[4] + xs[6])
    odd = (xs[1] + xs[3]) + (xs[5] + xs[7])
    every = even + odd

    def along(values):
        return jnp.sum(values, axis=0, keepdims=True)

    local = along(((d[0] + d[1]) + (d[2] + d[3])) + ((d[4] + d[5]) + (d[6] + d[7])))
    x_low, x_high = wx * along(xs[0] + xs[1]), wx * along(xs[6] + xs[7])
    y_low, y_high = wy * along(jnp.where(sub < 4, even, 0.0)), wy * along(jnp.where(sub >= 4, odd, 0.0))
    z_low = wz * along(jnp.where((sub & 3) == 0, every, 0.0))
    z_high = wz * along(jnp.where((sub & 3) == 3, every, 0.0))
    x, yi, z = (lane >> 1) & 3, lane & 1, lane >> 3
    local = local + jnp.where(x > 0, roll(x_high, 2, 1), 0.0) + jnp.where(x < 3, roll(x_low, -2, 1), 0.0)
    local = local + jnp.where(yi == 1, roll(y_high, 1, 1), roll(y_low, -1, 1))
    local = local + jnp.where(z > 0, roll(z_high, 8, 1), 0.0) + jnp.where(z < 7, roll(z_low, -8, 1), 0.0)
    shifts = jnp.zeros((1, 128), F32)
    for k in range(CLASSES):
        shifts = jnp.where(marks == k, shift_ref[k], shifts)
    scale = 1.0 / NODES
    return jnp.concatenate(
        [
            scale * local,
            scale * jnp.where(yi == 1, y_high, 0.0),
            scale * jnp.where(yi == 0, y_low, 0.0),
            0.125 * shifts,
            scale * jnp.where(x == 3, x_high, jnp.where(x == 0, x_low, 0.0)),
            scale * jnp.where(z == 7, z_high, jnp.where(z == 0, z_low, 0.0)),
            jnp.zeros((2, 128), F32),
        ],
        axis=0,
    )


def front_kernel(
    place_ref, weights_in, shift_in, right_in, marks_in, blocks_in,
    own_ref, table_ref, payload_ref,
    weights_ref, shift_ref, right_ref, marks_ref, blocks_ref, sems,
):
    moves = [(blocks_in, blocks_ref), (right_in, right_ref), (marks_in, marks_ref)]
    moves += [(weights_in, weights_ref), (shift_in, shift_ref)]
    copies = [pltpu.make_async_copy(source, target, sems.at[i]) for i, (source, target) in enumerate(moves)]
    for copy in copies:
        copy.start()
    for copy in copies:
        copy.wait()
    own_ref[:, 256:384] = jnp.zeros((8, 128), F32)
    for x in range(4):
        rows = slice(2 * x, 2 * x + 2)
        values = right_ref[x]
        own_ref[rows, 0:256] = values[:, 0:256]
        own_ref[rows, 384:640] = values[:, 256:512]
        own_ref[rows, 256:264] = marks_ref[x].astype(F32)
    diagonal = jnp.where(iota((64, 64), 0) == iota((64, 64), 1), 1.0, 0.0)
    rows = []
    for k in range(CLASSES):
        block = blocks_ref[k]
        diag = jnp.sum(block * diagonal, axis=0, keepdims=True)
        rows.append(jnp.concatenate([diag, jnp.sum(block, axis=0, keepdims=True)], axis=1))
    parts = split(jnp.concatenate(rows, axis=0))
    table = jnp.concatenate(list(parts) + [jnp.zeros((80, 128), F32)], axis=0).T
    table_ref[...] = table[:, 0:48].astype(jnp.bfloat16)

    parts = cell_parts(own_ref, table_ref, weights_ref, shift_ref)
    shape = (128, 128)
    source, target = iota(shape, 0), iota(shape, 1)
    hit = (source < 64) & (((source >> 2) & 1) == (target >> 6)) & ((source >> 4) == ((target >> 4) & 3))
    cells = dot(parts, jnp.where(hit, 1.0, 0.0))
    lane = iota((1, 128), 1)
    b, gy, gy0 = (lane >> 4) & 3, lane & 15, place_ref[1]
    own = gy == gy0
    row = jnp.where(own, cells[0:1], jnp.where(gy == gy0 + 1, cells[1:2], 0.0))
    payload_ref[:, 0:128] = row + jnp.where(gy == gy0 - 1, cells[2:3], 0.0)
    payload_ref[:, 128:256] = jnp.where(own, cells[3:4], 0.0)
    payload_ref[:, 256:384] = jnp.where(own, roll(cells[4:5], 64, 1), 0.0)
    high = jnp.where(own & (b == 3), roll(cells[5:6], 48, 1), 0.0)
    payload_ref[:, 384:512] = jnp.where(own & (b == 0), roll(cells[5:6], -48, 1), high)


def join_parts(gathered_ref):
    lane, sub = iota((8, 128), 1), iota((8, 128), 0)
    a, b = lane >> 6, (lane >> 4) & 3
    result = []
    for gx in range(8):
        value = gathered_ref[gx, :, 0:128]
        if gx > 0:
            value = value + jnp.where(a == 0, gathered_ref[gx - 1, :, 256:384], 0.0)
        if gx < 7:
            value = value + jnp.where(a == 1, gathered_ref[gx + 1, :, 256:384], 0.0)
        z = gathered_ref[gx, :, 384:512]
        value = value + jnp.where((b == 0) & (sub > 0), roll(z, 1, 0), 0.0)
        value = value + jnp.where((b == 3) & (sub < 7), roll(z, -1, 0), 0.0)
        result.append(value)
    return result


def pack_kernel(blocks_ref, packed_ref):
    low = iota((64, 128), 1) < 64
    for k in range(CLASSES):
        block = blocks_ref[k]
        first, second, third = split(jnp.concatenate([block, block], axis=1))
        at = slice(64 * k, 64 * k + 64)
        packed_ref[at, 0:128] = first.astype(jnp.bfloat16)
        packed_ref[at, 128:256] = jnp.where(low, first, second).astype(jnp.bfloat16)
        packed_ref[at, 256:384] = jnp.where(low, second, third).astype(jnp.bfloat16)


def coefficient_kernel(place_ref, below_ref, here_ref, above_ref, table_ref, class_ref, inverse_ref, sums_ref):
    marks = jnp.concatenate([below_ref[4:24, 0:128], here_ref[:, 0:128], above_ref[0:20, 0:128]], axis=0)
    marks = jnp.concatenate([marks, marks], axis=0).T[0:16].astype(jnp.int32)
    low = iota((1, 128), 1) < 64
    class_ref[...] = jnp.zeros((8, 128), jnp.int32)
    x, yd, _, half = packed_places((1, 128))
    for j in range(6):
        class_ref[j : j + 1, :] = jnp.where(low, marks[2 + j : 3 + j], marks[8 + j : 9 + j])
    for j in (0, 2, 4):
        both = coefficients([class_ref[j : j + 1, :], class_ref[j + 1 : j + 2, :]], table_ref)
        for part in range(2):
            columns = slice(128 * part, 128 * part + 128)
            relax = relaxation(x, yd, 2 + j + part + 6 * half, place_ref)
            inverse_ref[j + part] = relax / both[:64, columns]
            sums_ref[j + part] = both[64:, columns]


def local_kernel(
    place_ref, weights_ref, far_below_ref, below_ref, here_ref, above_ref, far_above_ref, table_ref, packed_ref,
    smooth_ref, inverse_ref, keep_ref,
    field_ref, iterate_ref, class_ref,
):
    def turned(block):
        columns = slice(128 * block, 128 * block + 128)
        middle = [ref[:, columns] for ref in (below_ref, here_ref, above_ref)]
        first, last = far_below_ref[:, columns], far_above_ref[:, columns]
        return jnp.concatenate([first] + middle + [last, jnp.zeros((8, 128), F32)], axis=0).T

    class_ref[...] = turned(0)[0:16].astype(jnp.int32)
    x, yd, _ = lane_places((1, 128))
    for pair in range(SLABS // 2):
        block = turned(pair + 1)
        both = coefficients([class_ref[2 * pair + i : 2 * pair + i + 1, :] for i in (0, 1)], table_ref)
        for part in range(2):
            s = 2 * pair + part
            columns = slice(128 * part, 128 * part + 128)
            values = block[64 * part : 64 * part + 64]
            inverse = relaxation(x, yd, s, place_ref) / both[:64, columns]
            field_ref[s] = values
            inverse_ref[s] = inverse
            keep_ref[s] = 1.0 - inverse * both[64:, columns]
            iterate_ref[s] = inverse * values
    for s in (0, 15):
        smooth_ref[s] = jnp.zeros((64, 128), F32)
    for s in range(1, 14, 2):
        planes = [iterate_ref[s + i] for i in (-1, 0, 1, 2)]
        marks = [class_ref[s + i : s + i + 1, :] for i in (0, 1)]
        chosen = dense(jnp.concatenate(planes[1:3], axis=1), marks, packed_ref)
        for part in range(2):
            faces = coupling(groups(planes[part]), Full(planes[part + 1]), groups(planes[part + 2]), weights_ref)
            for g in range(8):
                at = (s + part, slice(8 * g, 8 * g + 8))
                value = chosen[part][g] - faces[g]
                smooth_ref[at] = iterate_ref[at] + inverse_ref[at] * (field_ref[at] - value)


def first_kernel(
    place_ref, weights_ref, gathered_ref, local_ref, inverse_ref, keep_ref, class_ref, near_inverse_ref, sums_ref,
    packed_ref, right_ref,
    image_ref, own_direction_ref, own_image_ref, payload_ref,
    smooth_ref, pad_ref, rows_ref, shift_ref, all_ref, cells_ref,
):
    coarse = coarse_cycle(join_parts(gathered_ref), [gathered_ref[g, :, 128:256] for g in range(8)])
    place_correction(coarse, place_ref, pad_ref, rows_ref, shift_ref)
    _, _, yi = lane_places((8, 128))
    for s in range(1, 15):
        here = shift_ref[s : s + 1, :]
        faces = constant_coupling(shift_ref[s - 1 : s, :], here, shift_ref[s + 1 : s + 2, :], yi, weights_ref)
        here = jnp.broadcast_to(here, (8, 128))
        for g in range(8):
            at = (s, slice(8 * g, 8 * g + 8))
            smooth_ref[at] = local_ref[at] + (keep_ref[at] * here + inverse_ref[at] * faces[g])

    lane = iota((64, 128), 1)

    def block(j):
        return jnp.where(lane < 64, roll(smooth_ref[2 + j], -28, 1), roll(smooth_ref[8 + j], 36, 1))

    blocks = [block(j) for j in range(-1, 7)]
    for j in (0, 2, 4):
        marks = [class_ref[j + i : j + i + 1, :] for i in (0, 1)]
        chosen = dense(jnp.concatenate([blocks[j + 1], blocks[j + 2]], axis=1), marks, packed_ref)
        for part in range(2):
            at = j + part
            view = Pack(smooth_ref[2 + at], smooth_ref[8 + at])
            faces = coupling(groups(blocks[at]), view, groups(blocks[at + 2]), weights_ref)
            for g in range(8):
                image_ref[at, 8 * g : 8 * g + 8] = chosen[part][g] - faces[g]
    restrict(image_ref, near_inverse_ref, sums_ref, weights_ref, all_ref, cells_ref)
    payload_ref[:, 0:128] = payload(cells_ref[...], place_ref, 1.0 / NODES)
    own_z = gather_own([(smooth_ref[z + 4], 56) for z in range(8)])
    own_rows(own_z, own_of_packed(image_ref), own_direction_ref, own_image_ref)
    direction = own_direction_ref[...]
    lane = iota((1, 128), 1)
    gamma, delta = total(own_right(right_ref) * direction), total(direction * own_image_ref[...])
    payload_ref[:, 128:256] = jnp.where(lane == 0, gamma, jnp.where(lane == 1, delta, 0.0))


def near_kernel(
    weights_ref, image_ref, class_ref, inverse_ref, packed_ref,
    smooth_ref,
    iterate_ref,
):
    for j in range(6):
        iterate_ref[j] = inverse_ref[j] * image_ref[j]
    for j in (0, 2, 4):
        marks = [class_ref[j + i : j + i + 1, :] for i in (0, 1)]
        chosen = dense(jnp.concatenate([iterate_ref[j], iterate_ref[j + 1]], axis=1), marks, packed_ref)
        for part in range(2):
            at = j + part
            before, after = groups(block_before(iterate_ref, at)), groups(block_after(iterate_ref, at))
            faces = coupling(before, Block(iterate_ref[at]), after, weights_ref)
            for g in range(8):
                place = (at, slice(8 * g, 8 * g + 8))
                value = chosen[part][g] - faces[g]
                smooth_ref[place] = iterate_ref[place] + inverse_ref[place] * (image_ref[place] - value)


def second_kernel(
    place_ref, weights_ref, gathered_ref, shifts_ref, local_ref, class_ref, inverse_ref, sums_ref, packed_ref,
    right_ref, own_direction_ref, own_image_ref,
    residual_ref, smoothed_ref, applied_ref, known_ref, payload_ref,
    smooth_ref, pad_ref, rows_ref, shift_ref, turned_ref, image_ref, near_ref,
):
    coarse = coarse_cycle(
        [gathered_ref[g, :, 0:128] for g in range(8)], [shifts_ref[g, :, 128:256] for g in range(8)]
    )
    place_correction(coarse, place_ref, pad_ref, rows_ref, shift_ref)
    lane = iota((8, 128), 1)
    near_ref[...] = jnp.where(lane < 64, roll(shift_ref[2:10, :], -28, 1), roll(shift_ref[8:16, :], 36, 1))
    _, _, yi, _ = packed_places((8, 128))

    def row(j):
        return near_ref[j : j + 1, :]

    for j in range(6):
        before = row(j - 1) if j > 0 else roll(row(5), 64, 1)
        after = row(j + 1) if j < 5 else roll(row(0), 64, 1)
        faces = constant_coupling(before, row(j), after, yi, weights_ref)
        here = jnp.broadcast_to(row(j), (8, 128))
        for g in range(8):
            at = (j, slice(8 * g, 8 * g + 8))
            inverse = inverse_ref[at]
            smooth_ref[at] = local_ref[at] + (here + inverse * (faces[g] - sums_ref[at] * here))

    own_y = own_of_packed(smooth_ref)
    own_marks = gather_own(
        [(jnp.broadcast_to(class_ref[j : j + 1, :].astype(F32), (64, 128)), first)
         for j, first in [(2, 28), (3, 28), (4, 28), (5, 28), (0, 92), (1, 92), (2, 92), (3, 92)]]
    )
    chosen = dense(own_y, [own_marks[0:1].astype(jnp.int32)], packed_ref)[0]
    for j in range(6):
        before, after = groups(block_before(smooth_ref, j)), groups(block_after(smooth_ref, j))
        faces = coupling(before, Block(smooth_ref[j]), after, weights_ref)
        for g in range(8):
            image_ref[j, 8 * g : 8 * g + 8] = faces[g]
    own_v = jnp.concatenate(chosen, axis=0) - own_of_packed(image_ref)

    sums = gathered_ref[0, :, 128:256]
    for g in range(1, 8):
        sums = sums + gathered_ref[g, :, 128:256]
    sums = jnp.sum(sums, axis=0, keepdims=True)
    known_ref[...] = sums
    step = sums[:, 0:1] / sums[:, 1:2]
    own_rows(own_y, own_v, smoothed_ref, turned_ref)
    smoothed = own_direction_ref[...] - step * smoothed_ref[...]
    smoothed_ref[...] = smoothed
    applied = own_image_ref[...] - step * turned_ref[...]
    applied_ref[...] = applied
    residual = own_right(right_ref) - step * own_image_ref[...]
    residual_ref[...] = residual
    lane = iota((1, 128), 1)
    cross = own_direction_ref[...] * applied + own_image_ref[...] * smoothed
    values = jnp.where(lane == 0, total(residual * smoothed), 0.0)
    values = jnp.where(lane == 1, total(smoothed * applied), values)
    payload_ref[...] = jnp.where(lane == 2, total(cross), values)


def last_kernel(
    parts_ref, known_ref, direction_ref, own_image_ref, smoothed_ref, applied_ref, residual_ref, field_ref, out_ref
):
    totals = parts_ref[0]
    for gx in range(1, 8):
        totals = totals + parts_ref[gx]
    gamma, delta = known_ref[:, 0:1], known_ref[:, 1:2]
    beta = totals[:, 0:1] / gamma
    step = totals[:, 0:1] / (totals[:, 1:2] + beta * (totals[:, 2:3] + beta * delta))
    direction = direction_ref[...]
    field = (gamma / delta) * direction + step * (smoothed_ref[...] + beta * direction)
    residual = residual_ref[...] - step * (applied_ref[...] + beta * own_image_ref[...])
    for x in range(4):
        field_ref[x] = field[2 * x : 2 * x + 2]
        out_ref[x] = residual[2 * x : 2 * x + 2]


VMEM = pl.BlockSpec(memory_space=pltpu.VMEM)
SMEM = pl.BlockSpec(memory_space=pltpu.SMEM)


def call(body, scalars, out_shape, scratch, *args, flops=10**7, space=VMEM):
    specs = [SMEM] * scalars + [space] * (len(args) - scalars)
    shapes = [jax.ShapeDtypeStruct(shape, dtype) for shape, dtype in out_shape]
    return pl.pallas_call(
        body,
        out_shape=shapes,
        in_specs=specs,
        out_specs=[VMEM] * len(shapes),
        scratch_shapes=[entry if not isinstance(entry, tuple) else pltpu.VMEM(*entry) for entry in scratch],
        cost_estimate=pl.CostEstimate(flops=flops, bytes_accessed=10**6, transcendentals=0),
        compiler_params=pltpu.CompilerParams(vmem_limit_bytes=16 * 1024 * 1024),
    )(*args)


FIELD = ((SLABS, NODES, 128), F32)
BLOCKS = ((6, NODES, 128), F32)
MARKS = ((8, 128), jnp.int32)
OWN = ((8, 512), F32)
CELLS = ((8, 128), F32)
ROW, WIDE = ((1, 128), F32), ((1, 256), F32)
COARSE_SCRATCH = [((10, 24, 128), F32), ((16, 128), F32), ((16, 128), F32)]
SUM_SCRATCH = [((6, 8, 128), F32), CELLS]
PAIR_FLOPS = 2 * 1024 * 384 * 256


def front_call(*args):
    scratch = [pltpu.SMEM((3,), F32), pltpu.SMEM((CLASSES,), F32), ((4, 2, 512), F32), ((4, 2, 8), jnp.int32)]
    scratch += [((CLASSES, NODES, NODES), F32), pltpu.SemaphoreType.DMA((5,))]
    shapes = [((8, 640), F32), ((128, 48), jnp.bfloat16), ((1, 512), F32)]
    return call(front_kernel, 1, shapes, scratch, *args, space=pl.BlockSpec(memory_space=pltpu.HBM))


def pack_call(blocks):
    return call(pack_kernel, 0, [((CLASSES * NODES, 384), jnp.bfloat16)], [], blocks)[0]


def coefficient_call(*args):
    return call(coefficient_kernel, 1, [MARKS, BLOCKS, BLOCKS], [], *args)


def local_call(*args):
    scratch = [FIELD, FIELD, ((SLABS, 128), jnp.int32)]
    return call(local_kernel, 2, [FIELD, FIELD, FIELD], scratch, *args, flops=7 * PAIR_FLOPS)


def first_call(*args):
    scratch = [FIELD] + COARSE_SCRATCH + SUM_SCRATCH
    return call(first_kernel, 2, [BLOCKS, OWN, OWN, WIDE], scratch, *args, flops=3 * PAIR_FLOPS)


def near_call(*args):
    return call(near_kernel, 1, [BLOCKS], [BLOCKS], *args, flops=3 * PAIR_FLOPS)[0]


def second_call(*args):
    scratch = [BLOCKS] + COARSE_SCRATCH + [OWN, BLOCKS, CELLS]
    return call(second_kernel, 2, [OWN, OWN, OWN, ROW, ROW], scratch, *args, flops=PAIR_FLOPS)


def shifted(x, axis, step):
    size = lax.axis_size(axis)
    pairs = [(i, i + step) for i in range(size) if 0 <= i + step < size]
    return lax.ppermute(x, axis, pairs)


def extend_xz(own):
    wide = jnp.concatenate([shifted(own, "gx", 1), own, shifted(own, "gx", -1)], axis=0)
    low = shifted(wide[:, 256:640], "gz", 1)
    high = shifted(wide[:, 0:384], "gz", -1)
    nothing = jnp.zeros((24, 112), F32)
    pieces = [low[:, 4:8], wide[:, 256:264], high[:, 256:260], nothing]
    return jnp.concatenate(pieces + [low[:, 128:384], wide[:, 0:256], wide[:, 384:640], high[:, 0:256]], axis=1)


def gather_cells(row):
    width = row.shape[1]
    parts = lax.all_to_all(jnp.broadcast_to(row[None], (128, 1, width)), ("gy", "gz"), 0, 0, tiled=True)
    plane = parts.reshape(16, 8, width).sum(axis=0)
    return lax.all_to_all(jnp.broadcast_to(plane[None], (8, 8, width)), "gx", 0, 0, tiled=True)


def gather_sum(row):
    parts = lax.all_to_all(jnp.broadcast_to(row[None], (128, 1, 128)), ("gy", "gz"), 0, 0, tiled=True)
    part = parts.reshape(128, 128).sum(axis=0)
    return lax.all_to_all(jnp.broadcast_to(part[None, None], (8, 1, 128)), "gx", 0, 0, tiled=True)


def per_device(right_side, element_class, class_blocks, class_shift, face_weights):
    place = jnp.stack([lax.axis_index(axis) for axis in AXES]).astype(jnp.int32)
    own, table, row = front_call(place, face_weights, class_shift, right_side, element_class, class_blocks)
    gathered = gather_cells(row)
    packed = pack_call(class_blocks)
    here = extend_xz(own)
    below, above = shifted(here, "gy", 1), shifted(here, "gy", -1)
    far_below, far_above = shifted(here, "gy", 2), shifted(here, "gy", -2)
    marks, near_inverse, sums = coefficient_call(place, below, here, above, table)
    local, inverse, keep = local_call(
        place, face_weights, far_below, below, here, above, far_above, table, packed
    )
    image, direction, own_image, row = first_call(
        place, face_weights, gathered, local, inverse, keep, marks, near_inverse, sums, packed, own
    )
    again = gather_cells(row)
    near = near_call(face_weights, image, marks, near_inverse, packed)
    residual, smoothed, applied, known, row = second_call(
        place, face_weights, again, gathered, near, marks, near_inverse, sums, packed, own, direction, own_image
    )
    parts = gather_sum(row)
    shapes = [(right_side.shape, F32)] * 2
    return tuple(call(last_kernel, 0, shapes, [], parts, known, direction, own_image, smoothed, applied, residual))


def solution(mesh):
    in_specs = (P("gx", "gy", "gz"), P("gx", "gy", "gz"), P(), P(), P())
    out_specs = (P("gx", "gy", "gz"), P("gx", "gy", "gz"))
    return jax.shard_map(
        per_device, mesh=mesh, in_specs=in_specs, out_specs=out_specs, check_vma=False
    )
```

```python
import jax
import jax.numpy as jnp
from jax import lax
from jax.experimental import pallas as pl
from jax.experimental.pallas import tpu as pltpu
from jax.sharding import PartitionSpec as P

NODES = 64
CLASSES = 16
SLABS = 16
RELAX = 0.6
F32 = jnp.float32
HIGHEST = lax.Precision.HIGHEST
AXES = ("gx", "gy", "gz")


def dot(left, right):
    return jnp.dot(left, right, precision=HIGHEST, preferred_element_type=F32)


def iota(shape, dim):
    return lax.broadcasted_iota(jnp.int32, shape, dim)


def roll(values, shift, axis):
    return pltpu.roll(values, shift % values.shape[axis], axis)


def lane_places(shape):
    lane = iota(shape, len(shape) - 1)
    yd = (lane * 171) >> 12
    rest = lane - 24 * yd
    return rest >> 1, yd, rest & 1


def beside_1(v, lane, sub):
    a, b, gy = lane >> 6, (lane >> 4) & 3, lane & 15
    swapped = [roll(x, 64, 1) for x in v]
    result = []
    for gx in range(8):
        x = v[gx]
        total = swapped[gx] + jnp.where((gy & 1) == 0, roll(x, -1, 1), roll(x, 1, 1))
        if gx % 2 == 0:
            total = total + jnp.where(a == 1, swapped[gx + 1], 0.0)
        else:
            total = total + jnp.where(a == 0, swapped[gx - 1], 0.0)
        after = jnp.where((sub & 1) == 0, roll(roll(x, -1, 0), 48, 1), 0.0)
        before = jnp.where((sub & 1) == 1, roll(roll(x, 1, 0), -48, 1), 0.0)
        total = total + jnp.where(b < 3, roll(x, -16, 1), after)
        total = total + jnp.where(b > 0, roll(x, 16, 1), before)
        result.append(total)
    return result


def beside_2(v, lane, sub):
    b, gy = (lane >> 4) & 3, lane & 15
    result = []
    for gx in range(8):
        x = v[gx]
        total = jnp.where((gy & 2) == 0, roll(x, -2, 1), roll(x, 2, 1))
        if gx % 4 < 3:
            total = total + v[gx + 1]
        if gx % 4 > 0:
            total = total + v[gx - 1]
        after = jnp.where((sub & 3) < 3, roll(roll(x, -1, 0), 32, 1), 0.0)
        before = jnp.where((sub & 3) > 0, roll(roll(x, 1, 0), -32, 1), 0.0)
        total = total + jnp.where(b < 2, roll(x, -32, 1), after)
        total = total + jnp.where(b >= 2, roll(x, 32, 1), before)
        result.append(total)
    return result


def beside_3(v, lane, sub):
    gy = lane & 15
    result = []
    for gx in range(8):
        x = v[gx]
        total = jnp.where((gy & 4) == 0, roll(x, -4, 1), roll(x, 4, 1))
        if gx + 2 < 8:
            total = total + v[gx + 2]
        if gx - 2 >= 0:
            total = total + v[gx - 2]
        total = total + jnp.where(sub < 7, roll(x, -1, 0), 0.0)
        total = total + jnp.where(sub > 0, roll(x, 1, 0), 0.0)
        result.append(total)
    return result


def coarsen_1(v, lane):
    b, gy = (lane >> 4) & 3, lane & 15
    result = []
    for x in v:
        x = x + roll(x, 64, 1)
        x = x + jnp.where((b & 1) == 0, roll(x, -16, 1), roll(x, 16, 1))
        x = x + jnp.where((gy & 1) == 0, roll(x, -1, 1), roll(x, 1, 1))
        result.append(x)
    return result


def coarsen_2(v, lane):
    b, gy = (lane >> 4) & 3, lane & 15
    result = []
    for gx in range(8):
        x = v[gx] + v[gx ^ 1]
        x = x + jnp.where(b < 2, roll(x, -32, 1), roll(x, 32, 1))
        x = x + jnp.where((gy & 2) == 0, roll(x, -2, 1), roll(x, 2, 1))
        result.append(x)
    return result


def coarse_cycle(source, shift):
    lane, sub = iota((8, 128), 1), iota((8, 128), 0)
    eight = range(8)

    def remainder(beside, q, d, x):
        around = beside(x, lane, sub)
        return [q[i] - (d[i] * x[i] - around[i]) for i in eight]

    d1 = [6.0 + s for s in shift]
    shift2 = [0.125 * s for s in coarsen_1(shift, lane)]
    d2 = [6.0 + s for s in shift2]
    d3 = [6.0 + 0.125 * s for s in coarsen_2(shift2, lane)]
    w1 = [RELAX / d for d in d1]
    w2 = [RELAX / d for d in d2]
    w3 = [RELAX / d for d in d3]
    x1 = [w1[i] * source[i] for i in eight]
    q2 = [0.25 * t for t in coarsen_1(remainder(beside_1, source, d1, x1), lane)]
    x2 = [w2[i] * q2[i] for i in eight]
    q3 = [0.25 * t for t in coarsen_2(remainder(beside_2, q2, d2, x2), lane)]
    x3 = [w3[i] * q3[i] for i in eight]
    for _ in range(3):
        t3 = remainder(beside_3, q3, d3, x3)
        x3 = [x3[i] + w3[i] * t3[i] for i in eight]
    x2 = [x2[i] + x3[i] for i in eight]
    t2 = remainder(beside_2, q2, d2, x2)
    x2 = [x2[i] + w2[i] * t2[i] for i in eight]
    x1 = [x1[i] + x2[i] for i in eight]
    t1 = remainder(beside_1, source, d1, x1)
    return [x1[i] + w1[i] * t1[i] for i in eight]


def place_correction(coarse, place_ref, pad_ref, rows_ref, out_ref):
    gx0, gy0, gz0 = place_ref[0], place_ref[1], place_ref[2]
    pad_ref[...] = jnp.zeros_like(pad_ref)
    for gx in range(8):
        pad_ref[gx + 1, 8:16, :] = coarse[gx]
    rows_ref[...] = jnp.zeros_like(rows_ref)
    for e in range(3):
        for d in range(3):
            rows_ref[3 * e + d : 3 * e + d + 1, :] = pad_ref[gx0 + d, pl.ds(gz0 + 7 + e, 1), :]
    shape = (128, 512)
    source = iota(shape, 0)
    column = iota(shape, 1)
    target = column & 127
    yd = (target * 171) >> 12
    x = (target - 24 * yd) >> 1
    hit = ((source >> 4) & 3) == (column >> 7)
    hit = hit & ((source >> 6) == ((x >> 1) & 1))
    hit = hit & ((source & 15) == gy0 - 2 + yd) & (target < 120)
    spread = dot(rows_ref[...], jnp.where(hit, 1.0, 0.0))
    lane_x, _, _ = lane_places((1, 128))
    part = lane_x >> 2
    for t in range(8):
        e, b = (t + 2) // 4, (t + 2) % 4
        pieces = [spread[3 * e + d : 3 * e + d + 1, 128 * b : 128 * b + 128] for d in range(3)]
        row = jnp.where(part == 0, pieces[0], jnp.where(part == 1, pieces[1], pieces[2]))
        out_ref[2 * t : 2 * t + 1, :] = row
        out_ref[2 * t + 1 : 2 * t + 2, :] = row


def groups(values):
    return [values[8 * g : 8 * g + 8] for g in range(8)]


def packed_places(shape):
    lane = iota(shape, len(shape) - 1)
    rest = (lane & 63) + 4
    yd = 1 + ((rest * 171) >> 12)
    rest = rest - 24 * (yd - 1)
    return rest >> 1, yd, rest & 1, lane >> 6


def dense(values, marks, packed_ref):
    first = values.astype(jnp.bfloat16)
    rest = values - first.astype(F32)
    second = rest.astype(jnp.bfloat16)
    third = (rest - second.astype(F32)).astype(jnp.bfloat16)
    stack = jnp.concatenate([first, second, third, first, second, first], axis=0)
    products = jnp.dot(packed_ref[...], stack, preferred_element_type=F32)
    result = []
    for part, row in enumerate(marks):
        row = jnp.broadcast_to(row, (8, 128))
        columns = slice(128 * part, 128 * part + 128)
        chosen = [products[8 * g : 8 * g + 8, columns] for g in range(8)]
        for k in range(1, CLASSES):
            hit = row == k
            for g in range(8):
                at = 64 * k + 8 * g
                chosen[g] = jnp.where(hit, products[at : at + 8, columns], chosen[g])
        result.append(chosen)
    return result


class Full:
    def __init__(self, slab):
        self.parts = groups(slab)
        self.yi = lane_places((8, 128))[2]

    def here(self, g):
        return self.parts[g]

    def shift(self, g, step):
        return roll(self.parts[g], -step, 1)


class Pack:
    def __init__(self, low, high):
        self.low, self.high = groups(low), groups(high)
        self.yi = packed_places((8, 128))[2]

    def here(self, g):
        return self.shift(g, 0)

    def shift(self, g, step):
        lane = iota((8, 128), 1)
        return jnp.where(lane < 64, roll(self.low[g], -28 - step, 1), roll(self.high[g], 36 - step, 1))


class Block(Full):
    def __init__(self, block):
        self.parts = groups(block)
        self.yi = packed_places((8, 128))[2]


def upward_y(view, g):
    return jnp.where(view.yi == 0, view.shift(g, 1), view.shift(g, 23))


def downward_y(view, g):
    return jnp.where(view.yi == 1, view.shift(g, -1), view.shift(g, -23))


def face_weights_of(weights_ref):
    sub = iota((8, 128), 0)
    wx, wy, wz = weights_ref[0], weights_ref[1], weights_ref[2]
    top = jnp.where((sub & 3) == 3, wz, 0.0), jnp.where(sub >= 4, wy, 0.0)
    bottom = jnp.where((sub & 3) == 0, wz, 0.0), jnp.where(sub < 4, wy, 0.0)
    return wx, top, bottom


def coupling(before, view, after, weights_ref):
    wx, (wz_top, wy_top), (wz_bottom, wy_bottom) = face_weights_of(weights_ref)
    result = []
    for g in range(8):
        term = wz_top * roll(after[g], 3, 0) + wz_bottom * roll(before[g], -3, 0)
        if g % 2 == 1:
            term = term + wy_top * roll(upward_y(view, g - 1), 4, 0)
        else:
            term = term + wy_bottom * roll(downward_y(view, g + 1), 4, 0)
        if g >= 6:
            term = term + wx * view.shift(g - 6, 2)
        if g < 2:
            term = term + wx * view.shift(g + 6, -2)
        result.append(term)
    return result


def constant_coupling(before, here, after, yi, weights_ref):
    wx, (wz_top, wy_top), (wz_bottom, wy_bottom) = face_weights_of(weights_ref)

    def wide(row):
        return jnp.broadcast_to(row, (8, 128))

    here = wide(here)
    up = jnp.where(yi == 0, roll(here, -1, 1), roll(here, -23, 1))
    down = jnp.where(yi == 1, roll(here, 1, 1), roll(here, 23, 1))
    along = wz_top * wide(after) + wz_bottom * wide(before)
    even, odd = along + wy_bottom * down, along + wy_top * up
    result = [even if g % 2 == 0 else odd for g in range(8)]
    for g in (0, 1):
        result[g] = result[g] + wx * roll(here, 2, 1)
    for g in (6, 7):
        result[g] = result[g] + wx * roll(here, -2, 1)
    return result


def block_before(ref, j):
    return ref[j - 1] if j > 0 else roll(ref[5], 64, 1)


def block_after(ref, j):
    return ref[j + 1] if j < 5 else roll(ref[0], 64, 1)


def restrict(source_ref, inverse_ref, sums_ref, weights_ref, all_ref, out_ref):
    wx, (wz_top, wy_top), (wz_bottom, wy_bottom) = face_weights_of(weights_ref)
    _, _, yi, _ = packed_places((8, 128))
    totals = []
    out_ref[...] = jnp.zeros_like(out_ref)
    for j in range(6):
        r = source_ref[j]
        x = inverse_ref[j] * r
        d = groups(r - sums_ref[j] * x)
        xs = groups(x)
        even = (xs[0] + xs[2]) + (xs[4] + xs[6])
        odd = (xs[1] + xs[3]) + (xs[5] + xs[7])
        local = ((d[0] + d[1]) + (d[2] + d[3])) + ((d[4] + d[5]) + (d[6] + d[7]))
        local = local + wx * (roll(xs[0] + xs[1], -2, 1) + roll(xs[6] + xs[7], 2, 1))
        upper, lower = wy_top * odd, wy_bottom * even
        totals.append(local + jnp.where(yi == 0, roll(lower, -1, 1), roll(upper, 1, 1)))
        all_ref[j] = even + odd
        out_ref[8 + j : 9 + j, :] = jnp.sum(jnp.where(yi == 1, upper, 0.0), axis=0, keepdims=True)
        out_ref[16 + j : 17 + j, :] = jnp.sum(jnp.where(yi == 0, lower, 0.0), axis=0, keepdims=True)
    for j in range(6):
        value = totals[j] + wz_bottom * block_after(all_ref, j) + wz_top * block_before(all_ref, j)
        out_ref[j : j + 1, :] = jnp.sum(value, axis=0, keepdims=True)


def payload(cells, place_ref, scale):
    shape = (128, 256)
    source, column = iota(shape, 0), iota(shape, 1)
    own = (source & 63) - 28
    hit = (own >= 0) & (own < 8) & ((source >> 6) == (column >> 7)) & ((own >> 2) == ((column & 127) >> 6))
    spread = dot(cells, jnp.where(hit, scale, 0.0))
    block, column = iota((8, 256), 0), iota((8, 256), 1)
    z = block - 2 + 6 * (column >> 7)
    keep = (block < 6) & (z >= 0) & (z < 8) & ((z >> 1) == ((column >> 4) & 3))
    gy, gy0 = column & 15, place_ref[1]
    value = jnp.where(gy == gy0, spread[0:8], jnp.where(gy == gy0 + 1, spread[8:16], 0.0))
    value = value + jnp.where(gy == gy0 - 1, spread[16:24], 0.0)
    row = jnp.sum(jnp.where(keep, value, 0.0), axis=0, keepdims=True)
    return row[:, 0:128] + row[:, 128:256]


def gather_own(planes):
    lane = iota((64, 128), 1)
    result = jnp.zeros((64, 128), F32)
    for z, (plane, first) in enumerate(planes):
        result = jnp.where((lane >> 3) == z, roll(plane, 8 * z - first, 1), result)
    return result


def own_of_packed(blocks):
    return gather_own([(blocks[z + 2], 28) if z < 4 else (blocks[z - 4], 92) for z in range(8)])


def own_rows(first, second, first_ref, second_ref):
    turned = jnp.concatenate([first, second], axis=0).T
    low = iota((8, 128), 1) < 64
    for pair in range(4):
        even = turned[16 * pair : 16 * pair + 8]
        odd = turned[16 * pair + 8 : 16 * pair + 16]
        columns = slice(128 * pair, 128 * pair + 128)
        first_ref[:, columns] = jnp.where(low, even, roll(odd, 64, 1))
        second_ref[:, columns] = jnp.where(low, roll(even, 64, 1), odd)


def coefficients(rows, table_ref):
    halves = []
    for row in rows:
        wide = jnp.broadcast_to(row, (CLASSES, 128))
        halves.append(jnp.where(wide == iota((CLASSES, 128), 0), 1.0, 0.0))
    onehot = jnp.concatenate(halves, axis=1)
    onehot = jnp.concatenate([onehot] * 3, axis=0).astype(jnp.bfloat16)
    return jnp.dot(table_ref[...], onehot, preferred_element_type=F32)


def relaxation(x, yd, slab, place_ref):
    gx, gy = place_ref[0] - 1 + (x >> 2), place_ref[1] - 2 + yd
    gz = place_ref[2] - 1 + ((slab + 4) >> 3)
    inside = (gx >= 0) & (gx < 8) & (gy >= 0) & (gy < 16) & (gz >= 0) & (gz < 8) & (yd < 5)
    return jnp.where(inside, RELAX, 0.0)


def total(values):
    return jnp.sum(jnp.sum(values, axis=0, keepdims=True), axis=1, keepdims=True)


def own_right(own_ref):
    return jnp.concatenate([own_ref[:, 0:256], own_ref[:, 384:640]], axis=1)


def split(values):
    first = values.astype(jnp.bfloat16).astype(F32)
    rest = values - first
    second = rest.astype(jnp.bfloat16).astype(F32)
    return first, second, rest - second


def cell_parts(own_ref, table, weights_ref, shift_ref):
    pieces = []
    for pair in range(4):
        start = 128 * pair if pair < 2 else 128 * pair + 128
        values = own_ref[:, start : start + 128]
        pieces += [values, roll(values, 64, 1)]
    b = jnp.concatenate(pieces + [jnp.zeros((64, 128), F32)], axis=0).T[0:64]
    turned = jnp.concatenate([own_ref[:, 256:384], jnp.zeros((120, 128), F32)], axis=0).T
    lane = iota((1, 128), 1)
    marks = jnp.zeros((1, 128), F32)
    for z in range(8):
        marks = jnp.where((lane >> 3) == z, roll(turned[z : z + 1], 8 * z, 1), marks)
    marks = marks.astype(jnp.int32)
    both = coefficients([marks], table)
    x0 = (RELAX / both[:64]) * b
    d, xs = groups(b - both[64:] * x0), groups(x0)
    wx, wy, wz = weights_ref[0], weights_ref[1], weights_ref[2]
    sub = iota((8, 128), 0)
    even = (xs[0] + xs[2]) + (xs[4] + xs[6])
    odd = (xs[1] + xs[3]) + (xs[5] + xs[7])
    every = even + odd

    def along(values):
        return jnp.sum(values, axis=0, keepdims=True)

    local = along(((d[0] + d[1]) + (d[2] + d[3])) + ((d[4] + d[5]) + (d[6] + d[7])))
    x_low, x_high = wx * along(xs[0] + xs[1]), wx * along(xs[6] + xs[7])
    y_low, y_high = wy * along(jnp.where(sub < 4, even, 0.0)), wy * along(jnp.where(sub >= 4, odd, 0.0))
    z_low = wz * along(jnp.where((sub & 3) == 0, every, 0.0))
    z_high = wz * along(jnp.where((sub & 3) == 3, every, 0.0))
    x, yi, z = (lane >> 1) & 3, lane & 1, lane >> 3
    local = local + jnp.where(x > 0, roll(x_high, 2, 1), 0.0) + jnp.where(x < 3, roll(x_low, -2, 1), 0.0)
    local = local + jnp.where(yi == 1, roll(y_high, 1, 1), roll(y_low, -1, 1))
    local = local + jnp.where(z > 0, roll(z_high, 8, 1), 0.0) + jnp.where(z < 7, roll(z_low, -8, 1), 0.0)
    shifts = jnp.zeros((1, 128), F32)
    for k in range(CLASSES):
        shifts = jnp.where(marks == k, shift_ref[k], shifts)
    scale = 1.0 / NODES
    return jnp.concatenate(
        [
            scale * local,
            scale * jnp.where(yi == 1, y_high, 0.0),
            scale * jnp.where(yi == 0, y_low, 0.0),
            0.125 * shifts,
            scale * jnp.where(x == 3, x_high, jnp.where(x == 0, x_low, 0.0)),
            scale * jnp.where(z == 7, z_high, jnp.where(z == 0, z_low, 0.0)),
            jnp.zeros((2, 128), F32),
        ],
        axis=0,
    )


def front_kernel(
    place_ref, weights_ref, shift_ref, right_ref, marks_ref, blocks_ref,
    own_ref, table_ref, payload_ref,
):
    own_ref[:, 256:384] = jnp.zeros((8, 128), F32)
    for x in range(4):
        rows = slice(2 * x, 2 * x + 2)
        values = right_ref[x]
        own_ref[rows, 0:256] = values[:, 0:256]
        own_ref[rows, 384:640] = values[:, 256:512]
        own_ref[rows, 256:264] = marks_ref[x].astype(F32)
    diagonal = jnp.where(iota((64, 64), 0) == iota((64, 64), 1), 1.0, 0.0)
    rows = []
    for k in range(CLASSES):
        block = blocks_ref[k]
        diag = jnp.sum(block * diagonal, axis=0, keepdims=True)
        rows.append(jnp.concatenate([diag, jnp.sum(block, axis=0, keepdims=True)], axis=1))
    parts = split(jnp.concatenate(rows, axis=0))
    table = jnp.concatenate(list(parts) + [jnp.zeros((80, 128), F32)], axis=0).T
    table_ref[...] = table[:, 0:48].astype(jnp.bfloat16)

    parts = cell_parts(own_ref, table_ref, weights_ref, shift_ref)
    shape = (128, 128)
    source, target = iota(shape, 0), iota(shape, 1)
    hit = (source < 64) & (((source >> 2) & 1) == (target >> 6)) & ((source >> 4) == ((target >> 4) & 3))
    cells = dot(parts, jnp.where(hit, 1.0, 0.0))
    lane = iota((1, 128), 1)
    b, gy, gy0 = (lane >> 4) & 3, lane & 15, place_ref[1]
    own = gy == gy0
    row = jnp.where(own, cells[0:1], jnp.where(gy == gy0 + 1, cells[1:2], 0.0))
    payload_ref[:, 0:128] = row + jnp.where(gy == gy0 - 1, cells[2:3], 0.0)
    payload_ref[:, 128:256] = jnp.where(own, cells[3:4], 0.0)
    payload_ref[:, 256:384] = jnp.where(own, roll(cells[4:5], 64, 1), 0.0)
    high = jnp.where(own & (b == 3), roll(cells[5:6], 48, 1), 0.0)
    payload_ref[:, 384:512] = jnp.where(own & (b == 0), roll(cells[5:6], -48, 1), high)


def join_parts(gathered_ref):
    lane, sub = iota((8, 128), 1), iota((8, 128), 0)
    a, b = lane >> 6, (lane >> 4) & 3
    result = []
    for gx in range(8):
        value = gathered_ref[gx, :, 0:128]
        if gx > 0:
            value = value + jnp.where(a == 0, gathered_ref[gx - 1, :, 256:384], 0.0)
        if gx < 7:
            value = value + jnp.where(a == 1, gathered_ref[gx + 1, :, 256:384], 0.0)
        z = gathered_ref[gx, :, 384:512]
        value = value + jnp.where((b == 0) & (sub > 0), roll(z, 1, 0), 0.0)
        value = value + jnp.where((b == 3) & (sub < 7), roll(z, -1, 0), 0.0)
        result.append(value)
    return result


def pack_kernel(blocks_ref, packed_ref):
    low = iota((64, 128), 1) < 64
    for k in range(CLASSES):
        block = blocks_ref[k]
        first, second, third = split(jnp.concatenate([block, block], axis=1))
        at = slice(64 * k, 64 * k + 64)
        packed_ref[at, 0:128] = first.astype(jnp.bfloat16)
        packed_ref[at, 128:256] = jnp.where(low, first, second).astype(jnp.bfloat16)
        packed_ref[at, 256:384] = jnp.where(low, second, third).astype(jnp.bfloat16)


def coefficient_kernel(place_ref, below_ref, here_ref, above_ref, table_ref, class_ref, inverse_ref, sums_ref):
    marks = jnp.concatenate([below_ref[4:24, 0:128], here_ref[:, 0:128], above_ref[0:20, 0:128]], axis=0)
    marks = jnp.concatenate([marks, marks], axis=0).T[0:16].astype(jnp.int32)
    low = iota((1, 128), 1) < 64
    class_ref[...] = jnp.zeros((8, 128), jnp.int32)
    x, yd, _, half = packed_places((1, 128))
    for j in range(6):
        class_ref[j : j + 1, :] = jnp.where(low, marks[2 + j : 3 + j], marks[8 + j : 9 + j])
    for j in (0, 2, 4):
        both = coefficients([class_ref[j : j + 1, :], class_ref[j + 1 : j + 2, :]], table_ref)
        for part in range(2):
            columns = slice(128 * part, 128 * part + 128)
            relax = relaxation(x, yd, 2 + j + part + 6 * half, place_ref)
            inverse_ref[j + part] = relax / both[:64, columns]
            sums_ref[j + part] = both[64:, columns]


def local_kernel(
    place_ref, weights_ref, below_ref, here_ref, above_ref, table_ref, packed_ref,
    smooth_ref, inverse_ref, keep_ref,
    field_ref, iterate_ref, class_ref,
):
    def turned(block):
        columns = slice(128 * block, 128 * block + 128)
        middle = [ref[:, columns] for ref in (below_ref, here_ref, above_ref)]
        return jnp.concatenate([jnp.zeros((24, 128), F32)] + middle + [jnp.zeros((32, 128), F32)], axis=0).T

    class_ref[...] = turned(0)[0:16].astype(jnp.int32)
    x, yd, _ = lane_places((1, 128))
    for pair in range(SLABS // 2):
        block = turned(pair + 1)
        both = coefficients([class_ref[2 * pair + i : 2 * pair + i + 1, :] for i in (0, 1)], table_ref)
        for part in range(2):
            s = 2 * pair + part
            columns = slice(128 * part, 128 * part + 128)
            values = block[64 * part : 64 * part + 64]
            inverse = relaxation(x, yd, s, place_ref) / both[:64, columns]
            field_ref[s] = values
            inverse_ref[s] = inverse
            keep_ref[s] = 1.0 - inverse * both[64:, columns]
            iterate_ref[s] = inverse * values
    for s in (0, 15):
        smooth_ref[s] = jnp.zeros((64, 128), F32)
    for s in range(1, 14, 2):
        planes = [iterate_ref[s + i] for i in (-1, 0, 1, 2)]
        marks = [class_ref[s + i : s + i + 1, :] for i in (0, 1)]
        chosen = dense(jnp.concatenate(planes[1:3], axis=1), marks, packed_ref)
        for part in range(2):
            faces = coupling(groups(planes[part]), Full(planes[part + 1]), groups(planes[part + 2]), weights_ref)
            for g in range(8):
                at = (s + part, slice(8 * g, 8 * g + 8))
                value = chosen[part][g] - faces[g]
                smooth_ref[at] = iterate_ref[at] + inverse_ref[at] * (field_ref[at] - value)


def first_kernel(
    place_ref, weights_ref, gathered_ref, local_ref, inverse_ref, keep_ref, class_ref, near_inverse_ref, sums_ref,
    packed_ref, right_ref,
    image_ref, edge_ref, own_direction_ref, own_image_ref, payload_ref,
    smooth_ref, pad_ref, rows_ref, shift_ref, all_ref, cells_ref,
):
    coarse = coarse_cycle(join_parts(gathered_ref), [gathered_ref[g, :, 128:256] for g in range(8)])
    place_correction(coarse, place_ref, pad_ref, rows_ref, shift_ref)
    _, _, yi = lane_places((8, 128))
    for s in range(1, 15):
        here = shift_ref[s : s + 1, :]
        faces = constant_coupling(shift_ref[s - 1 : s, :], here, shift_ref[s + 1 : s + 2, :], yi, weights_ref)
        here = jnp.broadcast_to(here, (8, 128))
        for g in range(8):
            at = (s, slice(8 * g, 8 * g + 8))
            smooth_ref[at] = local_ref[at] + (keep_ref[at] * here + inverse_ref[at] * faces[g])

    lane = iota((64, 128), 1)

    def block(j):
        return jnp.where(lane < 64, roll(smooth_ref[2 + j], -28, 1), roll(smooth_ref[8 + j], 36, 1))

    blocks = [block(j) for j in range(-1, 7)]
    for j in (0, 2, 4):
        marks = [class_ref[j + i : j + i + 1, :] for i in (0, 1)]
        chosen = dense(jnp.concatenate([blocks[j + 1], blocks[j + 2]], axis=1), marks, packed_ref)
        for part in range(2):
            at = j + part
            view = Pack(smooth_ref[2 + at], smooth_ref[8 + at])
            faces = coupling(groups(blocks[at]), view, groups(blocks[at + 2]), weights_ref)
            for g in range(8):
                image_ref[at, 8 * g : 8 * g + 8] = chosen[part][g] - faces[g]
    own = (lane & 63) >= 20
    own = own & ((lane & 63) < 44)
    for j in range(3):
        edge_ref[j] = jnp.where(own, image_ref[j], roll(image_ref[j + 3], 32, 1))
    restrict(image_ref, near_inverse_ref, sums_ref, weights_ref, all_ref, cells_ref)
    payload_ref[:, 0:128] = payload(cells_ref[...], place_ref, 1.0 / NODES)
    own_z = gather_own([(smooth_ref[z + 4], 56) for z in range(8)])
    own_rows(own_z, own_of_packed(image_ref), own_direction_ref, own_image_ref)
    direction = own_direction_ref[...]
    lane = iota((1, 128), 1)
    gamma, delta = total(own_right(right_ref) * direction), total(direction * own_image_ref[...])
    payload_ref[:, 128:256] = jnp.where(lane == 0, gamma, jnp.where(lane == 1, delta, 0.0))


def near_kernel(
    weights_ref, own_ref, below_ref, above_ref, class_ref, inverse_ref, packed_ref,
    smooth_ref,
    iterate_ref, image_ref,
):
    lane = iota((64, 128), 1) & 63
    for j in range(6):
        below = roll(below_ref[j % 3], -24 if j < 3 else -56, 1)
        above = roll(above_ref[j % 3], 24 if j < 3 else -8, 1)
        image_ref[j] = jnp.where(lane < 20, below, jnp.where(lane < 44, own_ref[j], above))
        iterate_ref[j] = inverse_ref[j] * image_ref[j]
    for j in (0, 2, 4):
        marks = [class_ref[j + i : j + i + 1, :] for i in (0, 1)]
        chosen = dense(jnp.concatenate([iterate_ref[j], iterate_ref[j + 1]], axis=1), marks, packed_ref)
        for part in range(2):
            at = j + part
            before, after = groups(block_before(iterate_ref, at)), groups(block_after(iterate_ref, at))
            faces = coupling(before, Block(iterate_ref[at]), after, weights_ref)
            for g in range(8):
                place = (at, slice(8 * g, 8 * g + 8))
                value = chosen[part][g] - faces[g]
                smooth_ref[place] = iterate_ref[place] + inverse_ref[place] * (image_ref[place] - value)


def second_kernel(
    place_ref, weights_ref, gathered_ref, shifts_ref, local_ref, class_ref, inverse_ref, sums_ref, packed_ref,
    right_ref, own_direction_ref, own_image_ref,
    residual_ref, smoothed_ref, applied_ref, known_ref, payload_ref,
    smooth_ref, pad_ref, rows_ref, shift_ref, turned_ref, image_ref, near_ref,
):
    coarse = coarse_cycle(
        [gathered_ref[g, :, 0:128] for g in range(8)], [shifts_ref[g, :, 128:256] for g in range(8)]
    )
    place_correction(coarse, place_ref, pad_ref, rows_ref, shift_ref)
    lane = iota((8, 128), 1)
    near_ref[...] = jnp.where(lane < 64, roll(shift_ref[2:10, :], -28, 1), roll(shift_ref[8:16, :], 36, 1))
    _, _, yi, _ = packed_places((8, 128))

    def row(j):
        return near_ref[j : j + 1, :]

    for j in range(6):
        before = row(j - 1) if j > 0 else roll(row(5), 64, 1)
        after = row(j + 1) if j < 5 else roll(row(0), 64, 1)
        faces = constant_coupling(before, row(j), after, yi, weights_ref)
        here = jnp.broadcast_to(row(j), (8, 128))
        for g in range(8):
            at = (j, slice(8 * g, 8 * g + 8))
            inverse = inverse_ref[at]
            smooth_ref[at] = local_ref[at] + (here + inverse * (faces[g] - sums_ref[at] * here))

    own_y = own_of_packed(smooth_ref)
    own_marks = gather_own(
        [(jnp.broadcast_to(class_ref[j : j + 1, :].astype(F32), (64, 128)), first)
         for j, first in [(2, 28), (3, 28), (4, 28), (5, 28), (0, 92), (1, 92), (2, 92), (3, 92)]]
    )
    chosen = dense(own_y, [own_marks[0:1].astype(jnp.int32)], packed_ref)[0]
    for j in range(6):
        before, after = groups(block_before(smooth_ref, j)), groups(block_after(smooth_ref, j))
        faces = coupling(before, Block(smooth_ref[j]), after, weights_ref)
        for g in range(8):
            image_ref[j, 8 * g : 8 * g + 8] = faces[g]
    own_v = jnp.concatenate(chosen, axis=0) - own_of_packed(image_ref)

    sums = gathered_ref[0, :, 128:256]
    for g in range(1, 8):
        sums = sums + gathered_ref[g, :, 128:256]
    sums = jnp.sum(sums, axis=0, keepdims=True)
    known_ref[...] = sums
    step = sums[:, 0:1] / sums[:, 1:2]
    own_rows(own_y, own_v, smoothed_ref, turned_ref)
    smoothed = own_direction_ref[...] - step * smoothed_ref[...]
    smoothed_ref[...] = smoothed
    applied = own_image_ref[...] - step * turned_ref[...]
    applied_ref[...] = applied
    residual = own_right(right_ref) - step * own_image_ref[...]
    residual_ref[...] = residual
    lane = iota((1, 128), 1)
    cross = own_direction_ref[...] * applied + own_image_ref[...] * smoothed
    values = jnp.where(lane == 0, total(residual * smoothed), 0.0)
    values = jnp.where(lane == 1, total(smoothed * applied), values)
    payload_ref[...] = jnp.where(lane == 2, total(cross), values)


def last_kernel(
    parts_ref, known_ref, direction_ref, own_image_ref, smoothed_ref, applied_ref, residual_ref, field_ref, out_ref
):
    totals = parts_ref[0]
    for gx in range(1, 8):
        totals = totals + parts_ref[gx]
    gamma, delta = known_ref[:, 0:1], known_ref[:, 1:2]
    beta = totals[:, 0:1] / gamma
    step = totals[:, 0:1] / (totals[:, 1:2] + beta * (totals[:, 2:3] + beta * delta))
    direction = direction_ref[...]
    field = (gamma / delta) * direction + step * (smoothed_ref[...] + beta * direction)
    residual = residual_ref[...] - step * (applied_ref[...] + beta * own_image_ref[...])
    for x in range(4):
        field_ref[x] = field[2 * x : 2 * x + 2]
        out_ref[x] = residual[2 * x : 2 * x + 2]


VMEM = pl.BlockSpec(memory_space=pltpu.VMEM)
SMEM = pl.BlockSpec(memory_space=pltpu.SMEM)


def call(body, scalars, out_shape, scratch, *args, flops=10**7):
    specs = [SMEM] * scalars + [VMEM] * (len(args) - scalars)
    shapes = [jax.ShapeDtypeStruct(shape, dtype) for shape, dtype in out_shape]
    return pl.pallas_call(
        body,
        out_shape=shapes,
        in_specs=specs,
        out_specs=[VMEM] * len(shapes),
        scratch_shapes=[pltpu.VMEM(shape, dtype) for shape, dtype in scratch],
        cost_estimate=pl.CostEstimate(flops=flops, bytes_accessed=10**6, transcendentals=0),
        compiler_params=pltpu.CompilerParams(vmem_limit_bytes=16 * 1024 * 1024),
    )(*args)


FIELD = ((SLABS, NODES, 128), F32)
BLOCKS = ((6, NODES, 128), F32)
MARKS = ((8, 128), jnp.int32)
OWN = ((8, 512), F32)
CELLS = ((8, 128), F32)
ROW, WIDE = ((1, 128), F32), ((1, 256), F32)
COARSE_SCRATCH = [((10, 24, 128), F32), ((16, 128), F32), ((16, 128), F32)]
SUM_SCRATCH = [((6, 8, 128), F32), ((24, 128), F32)]
EDGE = ((3, NODES, 128), F32)
PAIR_FLOPS = 2 * 1024 * 384 * 256


def front_call(*args):
    return call(front_kernel, 3, [((8, 640), F32), ((128, 48), jnp.bfloat16), ((1, 512), F32)], [], *args)


def pack_call(blocks):
    return call(pack_kernel, 0, [((CLASSES * NODES, 384), jnp.bfloat16)], [], blocks)[0]


def coefficient_call(*args):
    return call(coefficient_kernel, 1, [MARKS, BLOCKS, BLOCKS], [], *args)


def local_call(*args):
    scratch = [FIELD, FIELD, ((SLABS, 128), jnp.int32)]
    return call(local_kernel, 2, [FIELD, FIELD, FIELD], scratch, *args, flops=7 * PAIR_FLOPS)


def first_call(*args):
    scratch = [FIELD] + COARSE_SCRATCH + SUM_SCRATCH
    return call(first_kernel, 2, [BLOCKS, EDGE, OWN, OWN, WIDE], scratch, *args, flops=3 * PAIR_FLOPS)


def near_call(*args):
    return call(near_kernel, 1, [BLOCKS], [BLOCKS, BLOCKS], *args, flops=3 * PAIR_FLOPS)[0]


def second_call(*args):
    scratch = [BLOCKS] + COARSE_SCRATCH + [OWN, BLOCKS, CELLS]
    return call(second_kernel, 2, [OWN, OWN, OWN, ROW, ROW], scratch, *args, flops=PAIR_FLOPS)


def shifted(x, axis, step):
    size = lax.axis_size(axis)
    pairs = [(i, i + step) for i in range(size) if 0 <= i + step < size]
    return lax.ppermute(x, axis, pairs)


def extend_xz(own):
    wide = jnp.concatenate([shifted(own, "gx", 1), own, shifted(own, "gx", -1)], axis=0)
    low = shifted(wide[:, 256:640], "gz", 1)
    high = shifted(wide[:, 0:384], "gz", -1)
    nothing = jnp.zeros((24, 112), F32)
    pieces = [low[:, 4:8], wide[:, 256:264], high[:, 256:260], nothing]
    return jnp.concatenate(pieces + [low[:, 128:384], wide[:, 0:256], wide[:, 384:640], high[:, 0:256]], axis=1)


def gather_cells(row):
    width = row.shape[1]
    parts = lax.all_to_all(jnp.broadcast_to(row[None], (128, 1, width)), ("gy", "gz"), 0, 0, tiled=True)
    plane = parts.reshape(16, 8, width).sum(axis=0)
    return lax.all_to_all(jnp.broadcast_to(plane[None], (8, 8, width)), "gx", 0, 0, tiled=True)


def gather_sum(row):
    parts = lax.all_to_all(jnp.broadcast_to(row[None], (128, 1, 128)), ("gy", "gz"), 0, 0, tiled=True)
    part = parts.reshape(128, 128).sum(axis=0)
    return lax.all_to_all(jnp.broadcast_to(part[None, None], (8, 1, 128)), "gx", 0, 0, tiled=True)


def per_device(right_side, element_class, class_blocks, class_shift, face_weights):
    place = jnp.stack([lax.axis_index(axis) for axis in AXES]).astype(jnp.int32)
    own, table, row = front_call(place, face_weights, class_shift, right_side, element_class, class_blocks)
    gathered = gather_cells(row)
    packed = pack_call(class_blocks)
    here = extend_xz(own)
    below, above = shifted(here, "gy", 1), shifted(here, "gy", -1)
    marks, near_inverse, sums = coefficient_call(place, below, here, above, table)
    local, inverse, keep = local_call(place, face_weights, below, here, above, table, packed)
    image, edge, direction, own_image, row = first_call(
        place, face_weights, gathered, local, inverse, keep, marks, near_inverse, sums, packed, own
    )
    again = gather_cells(row)
    from_below, from_above = shifted(edge, "gy", 1), shifted(edge, "gy", -1)
    near = near_call(face_weights, image, from_below, from_above, marks, near_inverse, packed)
    residual, smoothed, applied, known, row = second_call(
        place, face_weights, again, gathered, near, marks, near_inverse, sums, packed, own, direction, own_image
    )
    parts = gather_sum(row)
    shapes = [(right_side.shape, F32)] * 2
    return tuple(call(last_kernel, 0, shapes, [], parts, known, direction, own_image, smoothed, applied, residual))


def solution(mesh):
    in_specs = (P("gx", "gy", "gz"), P("gx", "gy", "gz"), P(), P(), P())
    out_specs = (P("gx", "gy", "gz"), P("gx", "gy", "gz"))
    return jax.shard_map(
        per_device, mesh=mesh, in_specs=in_specs, out_specs=out_specs, check_vma=False
    )
```

```python
import jax
import jax.numpy as jnp
from jax import lax
from jax.experimental import pallas as pl
from jax.experimental.pallas import tpu as pltpu
from jax.sharding import PartitionSpec as P

NODES = 64
CLASSES = 16
SLABS = 16
RELAX = 0.6
F32 = jnp.float32
HIGHEST = lax.Precision.HIGHEST
AXES = ("gx", "gy", "gz")


def dot(left, right):
    return jnp.dot(left, right, precision=HIGHEST, preferred_element_type=F32)


def iota(shape, dim):
    return lax.broadcasted_iota(jnp.int32, shape, dim)


def roll(values, shift, axis):
    return pltpu.roll(values, shift % values.shape[axis], axis)


def lane_places(shape):
    lane = iota(shape, len(shape) - 1)
    yd = (lane * 171) >> 12
    rest = lane - 24 * yd
    return rest >> 1, yd, rest & 1


def beside_1(v, lane, sub):
    a, b, gy = lane >> 6, (lane >> 4) & 3, lane & 15
    swapped = [roll(x, 64, 1) for x in v]
    result = []
    for gx in range(8):
        x = v[gx]
        total = swapped[gx] + jnp.where((gy & 1) == 0, roll(x, -1, 1), roll(x, 1, 1))
        if gx % 2 == 0:
            total = total + jnp.where(a == 1, swapped[gx + 1], 0.0)
        else:
            total = total + jnp.where(a == 0, swapped[gx - 1], 0.0)
        after = jnp.where((sub & 1) == 0, roll(roll(x, -1, 0), 48, 1), 0.0)
        before = jnp.where((sub & 1) == 1, roll(roll(x, 1, 0), -48, 1), 0.0)
        total = total + jnp.where(b < 3, roll(x, -16, 1), after)
        total = total + jnp.where(b > 0, roll(x, 16, 1), before)
        result.append(total)
    return result


def beside_2(v, lane, sub):
    b, gy = (lane >> 4) & 3, lane & 15
    result = []
    for gx in range(8):
        x = v[gx]
        total = jnp.where((gy & 2) == 0, roll(x, -2, 1), roll(x, 2, 1))
        if gx % 4 < 3:
            total = total + v[gx + 1]
        if gx % 4 > 0:
            total = total + v[gx - 1]
        after = jnp.where((sub & 3) < 3, roll(roll(x, -1, 0), 32, 1), 0.0)
        before = jnp.where((sub & 3) > 0, roll(roll(x, 1, 0), -32, 1), 0.0)
        total = total + jnp.where(b < 2, roll(x, -32, 1), after)
        total = total + jnp.where(b >= 2, roll(x, 32, 1), before)
        result.append(total)
    return result


def beside_3(v, lane, sub):
    gy = lane & 15
    result = []
    for gx in range(8):
        x = v[gx]
        total = jnp.where((gy & 4) == 0, roll(x, -4, 1), roll(x, 4, 1))
        if gx + 2 < 8:
            total = total + v[gx + 2]
        if gx - 2 >= 0:
            total = total + v[gx - 2]
        total = total + jnp.where(sub < 7, roll(x, -1, 0), 0.0)
        total = total + jnp.where(sub > 0, roll(x, 1, 0), 0.0)
        result.append(total)
    return result


def coarsen_1(v, lane):
    b, gy = (lane >> 4) & 3, lane & 15
    result = []
    for x in v:
        x = x + roll(x, 64, 1)
        x = x + jnp.where((b & 1) == 0, roll(x, -16, 1), roll(x, 16, 1))
        x = x + jnp.where((gy & 1) == 0, roll(x, -1, 1), roll(x, 1, 1))
        result.append(x)
    return result


def coarsen_2(v, lane):
    b, gy = (lane >> 4) & 3, lane & 15
    result = []
    for gx in range(8):
        x = v[gx] + v[gx ^ 1]
        x = x + jnp.where(b < 2, roll(x, -32, 1), roll(x, 32, 1))
        x = x + jnp.where((gy & 2) == 0, roll(x, -2, 1), roll(x, 2, 1))
        result.append(x)
    return result


def coarse_cycle(source, shift):
    lane, sub = iota((8, 128), 1), iota((8, 128), 0)
    eight = range(8)

    def remainder(beside, q, d, x):
        around = beside(x, lane, sub)
        return [q[i] - (d[i] * x[i] - around[i]) for i in eight]

    d1 = [6.0 + s for s in shift]
    shift2 = [0.125 * s for s in coarsen_1(shift, lane)]
    d2 = [6.0 + s for s in shift2]
    d3 = [6.0 + 0.125 * s for s in coarsen_2(shift2, lane)]
    w1 = [RELAX / d for d in d1]
    w2 = [RELAX / d for d in d2]
    w3 = [RELAX / d for d in d3]
    x1 = [w1[i] * source[i] for i in eight]
    q2 = [0.25 * t for t in coarsen_1(remainder(beside_1, source, d1, x1), lane)]
    x2 = [w2[i] * q2[i] for i in eight]
    q3 = [0.25 * t for t in coarsen_2(remainder(beside_2, q2, d2, x2), lane)]
    x3 = [w3[i] * q3[i] for i in eight]
    for _ in range(3):
        t3 = remainder(beside_3, q3, d3, x3)
        x3 = [x3[i] + w3[i] * t3[i] for i in eight]
    x2 = [x2[i] + x3[i] for i in eight]
    t2 = remainder(beside_2, q2, d2, x2)
    x2 = [x2[i] + w2[i] * t2[i] for i in eight]
    x1 = [x1[i] + x2[i] for i in eight]
    t1 = remainder(beside_1, source, d1, x1)
    return [x1[i] + w1[i] * t1[i] for i in eight]


def place_correction(coarse, place_ref, pad_ref, rows_ref, out_ref):
    gx0, gy0, gz0 = place_ref[0], place_ref[1], place_ref[2]
    pad_ref[...] = jnp.zeros_like(pad_ref)
    for gx in range(8):
        pad_ref[gx + 1, 8:16, :] = coarse[gx]
    rows_ref[...] = jnp.zeros_like(rows_ref)
    for e in range(3):
        for d in range(3):
            rows_ref[3 * e + d : 3 * e + d + 1, :] = pad_ref[gx0 + d, pl.ds(gz0 + 7 + e, 1), :]
    shape = (128, 512)
    source = iota(shape, 0)
    column = iota(shape, 1)
    target = column & 127
    yd = (target * 171) >> 12
    x = (target - 24 * yd) >> 1
    hit = ((source >> 4) & 3) == (column >> 7)
    hit = hit & ((source >> 6) == ((x >> 1) & 1))
    hit = hit & ((source & 15) == gy0 - 2 + yd) & (target < 120)
    spread = dot(rows_ref[...], jnp.where(hit, 1.0, 0.0))
    lane_x, _, _ = lane_places((1, 128))
    part = lane_x >> 2
    for t in range(8):
        e, b = (t + 2) // 4, (t + 2) % 4
        pieces = [spread[3 * e + d : 3 * e + d + 1, 128 * b : 128 * b + 128] for d in range(3)]
        row = jnp.where(part == 0, pieces[0], jnp.where(part == 1, pieces[1], pieces[2]))
        out_ref[2 * t : 2 * t + 1, :] = row
        out_ref[2 * t + 1 : 2 * t + 2, :] = row


def groups(values):
    return [values[8 * g : 8 * g + 8] for g in range(8)]


def packed_places(shape):
    lane = iota(shape, len(shape) - 1)
    rest = (lane & 63) + 4
    yd = 1 + ((rest * 171) >> 12)
    rest = rest - 24 * (yd - 1)
    return rest >> 1, yd, rest & 1, lane >> 6


def dense(values, marks, packed_ref):
    first = values.astype(jnp.bfloat16)
    rest = values - first.astype(F32)
    second = rest.astype(jnp.bfloat16)
    third = (rest - second.astype(F32)).astype(jnp.bfloat16)
    stack = jnp.concatenate([first, second, third, first, second, first], axis=0)
    products = jnp.dot(packed_ref[...], stack, preferred_element_type=F32)
    result = []
    for part, row in enumerate(marks):
        row = jnp.broadcast_to(row, (8, 128))
        columns = slice(128 * part, 128 * part + 128)
        chosen = [products[8 * g : 8 * g + 8, columns] for g in range(8)]
        for k in range(1, CLASSES):
            hit = row == k
            for g in range(8):
                at = 64 * k + 8 * g
                chosen[g] = jnp.where(hit, products[at : at + 8, columns], chosen[g])
        result.append(chosen)
    return result


class Full:
    def __init__(self, slab):
        self.parts = groups(slab)
        self.yi = lane_places((8, 128))[2]

    def here(self, g):
        return self.parts[g]

    def shift(self, g, step):
        return roll(self.parts[g], -step, 1)


class Pack:
    def __init__(self, low, high):
        self.low, self.high = groups(low), groups(high)
        self.yi = packed_places((8, 128))[2]

    def here(self, g):
        return self.shift(g, 0)

    def shift(self, g, step):
        lane = iota((8, 128), 1)
        return jnp.where(lane < 64, roll(self.low[g], -28 - step, 1), roll(self.high[g], 36 - step, 1))


class Block(Full):
    def __init__(self, block):
        self.parts = groups(block)
        self.yi = packed_places((8, 128))[2]


def upward_y(view, g):
    return jnp.where(view.yi == 0, view.shift(g, 1), view.shift(g, 23))


def downward_y(view, g):
    return jnp.where(view.yi == 1, view.shift(g, -1), view.shift(g, -23))


def face_weights_of(weights_ref):
    sub = iota((8, 128), 0)
    wx, wy, wz = weights_ref[0], weights_ref[1], weights_ref[2]
    top = jnp.where((sub & 3) == 3, wz, 0.0), jnp.where(sub >= 4, wy, 0.0)
    bottom = jnp.where((sub & 3) == 0, wz, 0.0), jnp.where(sub < 4, wy, 0.0)
    return wx, top, bottom


def coupling(before, view, after, weights_ref):
    wx, (wz_top, wy_top), (wz_bottom, wy_bottom) = face_weights_of(weights_ref)
    result = []
    for g in range(8):
        term = wz_top * roll(after[g], 3, 0) + wz_bottom * roll(before[g], -3, 0)
        if g % 2 == 1:
            term = term + wy_top * roll(upward_y(view, g - 1), 4, 0)
        else:
            term = term + wy_bottom * roll(downward_y(view, g + 1), 4, 0)
        if g >= 6:
            term = term + wx * view.shift(g - 6, 2)
        if g < 2:
            term = term + wx * view.shift(g + 6, -2)
        result.append(term)
    return result


def constant_coupling(before, here, after, yi, weights_ref):
    wx, (wz_top, wy_top), (wz_bottom, wy_bottom) = face_weights_of(weights_ref)

    def wide(row):
        return jnp.broadcast_to(row, (8, 128))

    here = wide(here)
    up = jnp.where(yi == 0, roll(here, -1, 1), roll(here, -23, 1))
    down = jnp.where(yi == 1, roll(here, 1, 1), roll(here, 23, 1))
    along = wz_top * wide(after) + wz_bottom * wide(before)
    even, odd = along + wy_bottom * down, along + wy_top * up
    result = [even if g % 2 == 0 else odd for g in range(8)]
    for g in (0, 1):
        result[g] = result[g] + wx * roll(here, 2, 1)
    for g in (6, 7):
        result[g] = result[g] + wx * roll(here, -2, 1)
    return result


def block_before(ref, j):
    return ref[j - 1] if j > 0 else roll(ref[5], 64, 1)


def block_after(ref, j):
    return ref[j + 1] if j < 5 else roll(ref[0], 64, 1)


def restrict(source_ref, inverse_ref, sums_ref, weights_ref, all_ref, out_ref):
    wx, (wz_top, wy_top), (wz_bottom, wy_bottom) = face_weights_of(weights_ref)
    _, _, yi, _ = packed_places((8, 128))
    totals = []
    out_ref[...] = jnp.zeros_like(out_ref)
    for j in range(6):
        r = source_ref[j]
        x = inverse_ref[j] * r
        d = groups(r - sums_ref[j] * x)
        xs = groups(x)
        even = (xs[0] + xs[2]) + (xs[4] + xs[6])
        odd = (xs[1] + xs[3]) + (xs[5] + xs[7])
        local = ((d[0] + d[1]) + (d[2] + d[3])) + ((d[4] + d[5]) + (d[6] + d[7]))
        local = local + wx * (roll(xs[0] + xs[1], -2, 1) + roll(xs[6] + xs[7], 2, 1))
        upper, lower = wy_top * odd, wy_bottom * even
        totals.append(local + jnp.where(yi == 0, roll(lower, -1, 1), roll(upper, 1, 1)))
        all_ref[j] = even + odd
        out_ref[8 + j : 9 + j, :] = jnp.sum(jnp.where(yi == 1, upper, 0.0), axis=0, keepdims=True)
        out_ref[16 + j : 17 + j, :] = jnp.sum(jnp.where(yi == 0, lower, 0.0), axis=0, keepdims=True)
    for j in range(6):
        value = totals[j] + wz_bottom * block_after(all_ref, j) + wz_top * block_before(all_ref, j)
        out_ref[j : j + 1, :] = jnp.sum(value, axis=0, keepdims=True)


def payload(cells, place_ref, scale):
    shape = (128, 256)
    source, column = iota(shape, 0), iota(shape, 1)
    own = (source & 63) - 28
    hit = (own >= 0) & (own < 8) & ((source >> 6) == (column >> 7)) & ((own >> 2) == ((column & 127) >> 6))
    spread = dot(cells, jnp.where(hit, scale, 0.0))
    block, column = iota((8, 256), 0), iota((8, 256), 1)
    z = block - 2 + 6 * (column >> 7)
    keep = (block < 6) & (z >= 0) & (z < 8) & ((z >> 1) == ((column >> 4) & 3))
    gy, gy0 = column & 15, place_ref[1]
    value = jnp.where(gy == gy0, spread[0:8], jnp.where(gy == gy0 + 1, spread[8:16], 0.0))
    value = value + jnp.where(gy == gy0 - 1, spread[16:24], 0.0)
    row = jnp.sum(jnp.where(keep, value, 0.0), axis=0, keepdims=True)
    return row[:, 0:128] + row[:, 128:256]


def gather_own(planes):
    lane = iota((64, 128), 1)
    result = jnp.zeros((64, 128), F32)
    for z, (plane, first) in enumerate(planes):
        result = jnp.where((lane >> 3) == z, roll(plane, 8 * z - first, 1), result)
    return result


def own_of_packed(blocks):
    return gather_own([(blocks[z + 2], 28) if z < 4 else (blocks[z - 4], 92) for z in range(8)])


def own_rows(first, second, first_ref, second_ref):
    turned = jnp.concatenate([first, second], axis=0).T
    low = iota((8, 128), 1) < 64
    for pair in range(4):
        even = turned[16 * pair : 16 * pair + 8]
        odd = turned[16 * pair + 8 : 16 * pair + 16]
        columns = slice(128 * pair, 128 * pair + 128)
        first_ref[:, columns] = jnp.where(low, even, roll(odd, 64, 1))
        second_ref[:, columns] = jnp.where(low, roll(even, 64, 1), odd)


def coefficients(rows, table_ref):
    halves = []
    for row in rows:
        wide = jnp.broadcast_to(row, (CLASSES, 128))
        halves.append(jnp.where(wide == iota((CLASSES, 128), 0), 1.0, 0.0))
    onehot = jnp.concatenate(halves, axis=1)
    onehot = jnp.concatenate([onehot] * 3, axis=0).astype(jnp.bfloat16)
    return jnp.dot(table_ref[...], onehot, preferred_element_type=F32)


def relaxation(x, yd, slab, place_ref):
    gx, gy = place_ref[0] - 1 + (x >> 2), place_ref[1] - 2 + yd
    gz = place_ref[2] - 1 + ((slab + 4) >> 3)
    inside = (gx >= 0) & (gx < 8) & (gy >= 0) & (gy < 16) & (gz >= 0) & (gz < 8) & (yd < 5)
    return jnp.where(inside, RELAX, 0.0)


def total(values):
    return jnp.sum(jnp.sum(values, axis=0, keepdims=True), axis=1, keepdims=True)


def own_right(own_ref):
    return jnp.concatenate([own_ref[:, 0:256], own_ref[:, 384:640]], axis=1)


def split(values):
    first = values.astype(jnp.bfloat16).astype(F32)
    rest = values - first
    second = rest.astype(jnp.bfloat16).astype(F32)
    return first, second, rest - second


def cell_parts(wide_ref, table, weights_ref, shift_ref):
    def own(columns):
        return wide_ref[8:16, columns]

    def beside(columns):
        return jnp.concatenate([wide_ref[6:8, columns], jnp.zeros((4, 128), F32), wide_ref[16:18, columns]], axis=0)

    pieces = []
    for rows in (own, beside):
        for pair in range(4):
            start = 128 * pair if pair < 2 else 128 * pair + 128
            values = rows(slice(start, start + 128))
            pieces += [values, roll(values, 64, 1)]
    b = jnp.concatenate(pieces, axis=0).T[0:64]
    middle = slice(256, 384)
    turned = jnp.concatenate([own(middle), beside(middle), jnp.zeros((112, 128), F32)], axis=0).T
    lane = iota((1, 128), 1)
    marks = jnp.zeros((1, 128), F32)
    for z in range(8):
        marks = jnp.where((lane >> 3) == z, roll(turned[z : z + 1], 8 * z, 1), marks)
        marks = jnp.where((lane >> 3) == 8 + z, roll(turned[z : z + 1], 8 * z + 56, 1), marks)
    marks = marks.astype(jnp.int32)
    both = coefficients([marks], table)
    x0 = (RELAX / both[:64]) * b
    d, xs = groups(b - both[64:] * x0), groups(x0)
    wx, wy, wz = weights_ref[0], weights_ref[1], weights_ref[2]
    sub = iota((8, 128), 0)
    even = (xs[0] + xs[2]) + (xs[4] + xs[6])
    odd = (xs[1] + xs[3]) + (xs[5] + xs[7])
    every = even + odd

    def along(values):
        return jnp.sum(values, axis=0, keepdims=True)

    local = along(((d[0] + d[1]) + (d[2] + d[3])) + ((d[4] + d[5]) + (d[6] + d[7])))
    x_low, x_high = wx * along(xs[0] + xs[1]), wx * along(xs[6] + xs[7])
    y_low, y_high = wy * along(jnp.where(sub < 4, even, 0.0)), wy * along(jnp.where(sub >= 4, odd, 0.0))
    z_low = wz * along(jnp.where((sub & 3) == 0, every, 0.0))
    z_high = wz * along(jnp.where((sub & 3) == 3, every, 0.0))
    x, yi, z = (lane >> 1) & 3, lane & 1, lane >> 3
    local = local + jnp.where(x > 0, roll(x_high, 2, 1), roll(x_high, -64, 1))
    local = local + jnp.where(x < 3, roll(x_low, -2, 1), roll(x_low, -64, 1))
    local = local + jnp.where(yi == 1, roll(y_high, 1, 1), roll(y_low, -1, 1))
    local = local + jnp.where(z > 0, roll(z_high, 8, 1), 0.0) + jnp.where(z < 7, roll(z_low, -8, 1), 0.0)
    shifts = jnp.zeros((1, 128), F32)
    for k in range(CLASSES):
        shifts = jnp.where(marks == k, shift_ref[k], shifts)
    scale = 1.0 / NODES
    return jnp.concatenate(
        [
            scale * local,
            scale * jnp.where(yi == 1, y_high, 0.0),
            scale * jnp.where(yi == 0, y_low, 0.0),
            0.125 * shifts,
            scale * jnp.where(z == 7, z_high, jnp.where(z == 0, z_low, 0.0)),
            jnp.zeros((3, 128), F32),
        ],
        axis=0,
    )


def own_kernel(right_ref, marks_ref, own_ref):
    own_ref[:, 256:384] = jnp.zeros((8, 128), F32)
    for x in range(4):
        rows = slice(2 * x, 2 * x + 2)
        values = right_ref[x]
        own_ref[rows, 0:256] = values[:, 0:256]
        own_ref[rows, 384:640] = values[:, 256:512]
        own_ref[rows, 256:264] = marks_ref[x].astype(F32)


def front_kernel(place_ref, weights_ref, shift_ref, wide_ref, table_ref, payload_ref):
    parts = cell_parts(wide_ref, table_ref, weights_ref, shift_ref)
    shape = (128, 128)
    source, target = iota(shape, 0), iota(shape, 1)
    hit = (source < 64) & (((source >> 2) & 1) == (target >> 6)) & ((source >> 4) == ((target >> 4) & 3))
    cells = dot(parts, jnp.where(hit, 1.0, 0.0))
    lane = iota((1, 128), 1)
    b, gy, gy0 = (lane >> 4) & 3, lane & 15, place_ref[1]
    own = gy == gy0
    row = jnp.where(own, cells[0:1], jnp.where(gy == gy0 + 1, cells[1:2], 0.0))
    payload_ref[:, 0:128] = row + jnp.where(gy == gy0 - 1, cells[2:3], 0.0)
    payload_ref[:, 128:256] = jnp.where(own, cells[3:4], 0.0)
    high = jnp.where(own & (b == 3), roll(cells[4:5], 48, 1), 0.0)
    payload_ref[:, 256:384] = jnp.where(own & (b == 0), roll(cells[4:5], -48, 1), high)


def join_parts(gathered_ref):
    lane, sub = iota((8, 128), 1), iota((8, 128), 0)
    b = (lane >> 4) & 3
    result = []
    for gx in range(8):
        value = gathered_ref[gx, :, 0:128]
        z = gathered_ref[gx, :, 256:384]
        value = value + jnp.where((b == 0) & (sub > 0), roll(z, 1, 0), 0.0)
        value = value + jnp.where((b == 3) & (sub < 7), roll(z, -1, 0), 0.0)
        result.append(value)
    return result


def pack_kernel(blocks_ref, packed_ref, table_ref):
    diagonal = jnp.where(iota((64, 64), 0) == iota((64, 64), 1), 1.0, 0.0)
    low = iota((64, 128), 1) < 64
    rows = []
    for k in range(CLASSES):
        block = blocks_ref[k]
        first, second, third = split(jnp.concatenate([block, block], axis=1))
        at = slice(64 * k, 64 * k + 64)
        packed_ref[at, 0:128] = first.astype(jnp.bfloat16)
        packed_ref[at, 128:256] = jnp.where(low, first, second).astype(jnp.bfloat16)
        packed_ref[at, 256:384] = jnp.where(low, second, third).astype(jnp.bfloat16)
        diag = jnp.sum(block * diagonal, axis=0, keepdims=True)
        rows.append(jnp.concatenate([diag, jnp.sum(block, axis=0, keepdims=True)], axis=1))
    parts = split(jnp.concatenate(rows, axis=0))
    table = jnp.concatenate(list(parts) + [jnp.zeros((80, 128), F32)], axis=0).T
    table_ref[...] = table[:, 0:48].astype(jnp.bfloat16)


def coefficient_kernel(place_ref, below_ref, here_ref, above_ref, table_ref, class_ref, inverse_ref, sums_ref):
    marks = jnp.concatenate([below_ref[4:24, 0:128], here_ref[:, 0:128], above_ref[0:20, 0:128]], axis=0)
    marks = jnp.concatenate([marks, marks], axis=0).T[0:16].astype(jnp.int32)
    low = iota((1, 128), 1) < 64
    class_ref[...] = jnp.zeros((8, 128), jnp.int32)
    x, yd, _, half = packed_places((1, 128))
    for j in range(6):
        class_ref[j : j + 1, :] = jnp.where(low, marks[2 + j : 3 + j], marks[8 + j : 9 + j])
    for j in (0, 2, 4):
        both = coefficients([class_ref[j : j + 1, :], class_ref[j + 1 : j + 2, :]], table_ref)
        for part in range(2):
            columns = slice(128 * part, 128 * part + 128)
            relax = relaxation(x, yd, 2 + j + part + 6 * half, place_ref)
            inverse_ref[j + part] = relax / both[:64, columns]
            sums_ref[j + part] = both[64:, columns]


def local_kernel(
    place_ref, weights_ref, below_ref, here_ref, above_ref, table_ref, packed_ref,
    smooth_ref, inverse_ref, keep_ref,
    field_ref, iterate_ref, class_ref,
):
    def turned(block):
        columns = slice(128 * block, 128 * block + 128)
        middle = [ref[:, columns] for ref in (below_ref, here_ref, above_ref)]
        return jnp.concatenate([jnp.zeros((24, 128), F32)] + middle + [jnp.zeros((32, 128), F32)], axis=0).T

    class_ref[...] = turned(0)[0:16].astype(jnp.int32)
    x, yd, _ = lane_places((1, 128))
    for pair in range(SLABS // 2):
        block = turned(pair + 1)
        both = coefficients([class_ref[2 * pair + i : 2 * pair + i + 1, :] for i in (0, 1)], table_ref)
        for part in range(2):
            s = 2 * pair + part
            columns = slice(128 * part, 128 * part + 128)
            values = block[64 * part : 64 * part + 64]
            inverse = relaxation(x, yd, s, place_ref) / both[:64, columns]
            field_ref[s] = values
            inverse_ref[s] = inverse
            keep_ref[s] = 1.0 - inverse * both[64:, columns]
            iterate_ref[s] = inverse * values
    for s in (0, 15):
        smooth_ref[s] = jnp.zeros((64, 128), F32)
    for s in range(1, 14, 2):
        planes = [iterate_ref[s + i] for i in (-1, 0, 1, 2)]
        marks = [class_ref[s + i : s + i + 1, :] for i in (0, 1)]
        chosen = dense(jnp.concatenate(planes[1:3], axis=1), marks, packed_ref)
        for part in range(2):
            faces = coupling(groups(planes[part]), Full(planes[part + 1]), groups(planes[part + 2]), weights_ref)
            for g in range(8):
                at = (s + part, slice(8 * g, 8 * g + 8))
                value = chosen[part][g] - faces[g]
                smooth_ref[at] = iterate_ref[at] + inverse_ref[at] * (field_ref[at] - value)


def first_kernel(
    place_ref, weights_ref, gathered_ref, local_ref, inverse_ref, keep_ref, class_ref, near_inverse_ref, sums_ref,
    packed_ref, right_ref,
    image_ref, edge_ref, own_direction_ref, own_image_ref, payload_ref,
    smooth_ref, pad_ref, rows_ref, shift_ref, all_ref, cells_ref,
):
    coarse = coarse_cycle(join_parts(gathered_ref), [gathered_ref[g, :, 128:256] for g in range(8)])
    place_correction(coarse, place_ref, pad_ref, rows_ref, shift_ref)
    _, _, yi = lane_places((8, 128))
    for s in range(1, 15):
        here = shift_ref[s : s + 1, :]
        faces = constant_coupling(shift_ref[s - 1 : s, :], here, shift_ref[s + 1 : s + 2, :], yi, weights_ref)
        here = jnp.broadcast_to(here, (8, 128))
        for g in range(8):
            at = (s, slice(8 * g, 8 * g + 8))
            smooth_ref[at] = local_ref[at] + (keep_ref[at] * here + inverse_ref[at] * faces[g])

    lane = iota((64, 128), 1)

    def block(j):
        return jnp.where(lane < 64, roll(smooth_ref[2 + j], -28, 1), roll(smooth_ref[8 + j], 36, 1))

    blocks = [block(j) for j in range(-1, 7)]
    own = (lane & 63) >= 20
    own = own & ((lane & 63) < 44)
    halves = [jnp.where(own, blocks[j + 1], roll(blocks[j + 4], 32, 1)) for j in range(3)]
    marks = class_ref[...]
    marks = jnp.where(own[0:8], marks, roll(jnp.concatenate([marks[3:8], marks[0:3]], axis=0), 32, 1))
    chosen = dense(jnp.concatenate(halves, axis=1), [marks[j : j + 1] for j in range(3)], packed_ref)
    for j in range(6):
        view = Pack(smooth_ref[2 + j], smooth_ref[8 + j])
        faces = coupling(groups(blocks[j]), view, groups(blocks[j + 2]), weights_ref)
        for g in range(8):
            value = chosen[j][g] if j < 3 else roll(chosen[j - 3][g], -32, 1)
            image_ref[j, 8 * g : 8 * g + 8] = value - faces[g]
    for j in range(3):
        edge_ref[j] = jnp.where(own, image_ref[j], roll(image_ref[j + 3], 32, 1))
    restrict(image_ref, near_inverse_ref, sums_ref, weights_ref, all_ref, cells_ref)
    payload_ref[:, 0:128] = payload(cells_ref[...], place_ref, 1.0 / NODES)
    own_z = gather_own([(smooth_ref[z + 4], 56) for z in range(8)])
    own_rows(own_z, own_of_packed(image_ref), own_direction_ref, own_image_ref)
    direction = own_direction_ref[...]
    lane = iota((1, 128), 1)
    gamma, delta = total(own_right(right_ref) * direction), total(direction * own_image_ref[...])
    payload_ref[:, 128:256] = jnp.where(lane == 0, gamma, jnp.where(lane == 1, delta, 0.0))


def near_kernel(
    weights_ref, own_ref, below_ref, above_ref, class_ref, inverse_ref, packed_ref,
    smooth_ref,
    iterate_ref, image_ref,
):
    lane = iota((64, 128), 1) & 63
    for j in range(6):
        below = roll(below_ref[j % 3], -24 if j < 3 else -56, 1)
        above = roll(above_ref[j % 3], 24 if j < 3 else -8, 1)
        image_ref[j] = jnp.where(lane < 20, below, jnp.where(lane < 44, own_ref[j], above))
        iterate_ref[j] = inverse_ref[j] * image_ref[j]
    for j in (0, 2, 4):
        marks = [class_ref[j + i : j + i + 1, :] for i in (0, 1)]
        chosen = dense(jnp.concatenate([iterate_ref[j], iterate_ref[j + 1]], axis=1), marks, packed_ref)
        for part in range(2):
            at = j + part
            before, after = groups(block_before(iterate_ref, at)), groups(block_after(iterate_ref, at))
            faces = coupling(before, Block(iterate_ref[at]), after, weights_ref)
            for g in range(8):
                place = (at, slice(8 * g, 8 * g + 8))
                value = chosen[part][g] - faces[g]
                smooth_ref[place] = iterate_ref[place] + inverse_ref[place] * (image_ref[place] - value)


def second_kernel(
    place_ref, weights_ref, gathered_ref, shifts_ref, local_ref, class_ref, inverse_ref, sums_ref, packed_ref,
    right_ref, own_direction_ref, own_image_ref,
    residual_ref, smoothed_ref, applied_ref, known_ref, payload_ref,
    smooth_ref, pad_ref, rows_ref, shift_ref, turned_ref, image_ref, near_ref,
):
    coarse = coarse_cycle(
        [gathered_ref[g, :, 0:128] for g in range(8)], [shifts_ref[g, :, 128:256] for g in range(8)]
    )
    place_correction(coarse, place_ref, pad_ref, rows_ref, shift_ref)
    lane = iota((8, 128), 1)
    near_ref[...] = jnp.where(lane < 64, roll(shift_ref[2:10, :], -28, 1), roll(shift_ref[8:16, :], 36, 1))
    _, _, yi, _ = packed_places((8, 128))

    def row(j):
        return near_ref[j : j + 1, :]

    for j in range(6):
        before = row(j - 1) if j > 0 else roll(row(5), 64, 1)
        after = row(j + 1) if j < 5 else roll(row(0), 64, 1)
        faces = constant_coupling(before, row(j), after, yi, weights_ref)
        here = jnp.broadcast_to(row(j), (8, 128))
        for g in range(8):
            at = (j, slice(8 * g, 8 * g + 8))
            inverse = inverse_ref[at]
            smooth_ref[at] = local_ref[at] + (here + inverse * (faces[g] - sums_ref[at] * here))

    own_y = own_of_packed(smooth_ref)
    own_marks = gather_own(
        [(jnp.broadcast_to(class_ref[j : j + 1, :].astype(F32), (64, 128)), first)
         for j, first in [(2, 28), (3, 28), (4, 28), (5, 28), (0, 92), (1, 92), (2, 92), (3, 92)]]
    )
    chosen = dense(own_y, [own_marks[0:1].astype(jnp.int32)], packed_ref)[0]
    for j in range(6):
        before, after = groups(block_before(smooth_ref, j)), groups(block_after(smooth_ref, j))
        faces = coupling(before, Block(smooth_ref[j]), after, weights_ref)
        for g in range(8):
            image_ref[j, 8 * g : 8 * g + 8] = faces[g]
    own_v = jnp.concatenate(chosen, axis=0) - own_of_packed(image_ref)

    sums = gathered_ref[0, :, 128:256]
    for g in range(1, 8):
        sums = sums + gathered_ref[g, :, 128:256]
    sums = jnp.sum(sums, axis=0, keepdims=True)
    known_ref[...] = sums
    step = sums[:, 0:1] / sums[:, 1:2]
    own_rows(own_y, own_v, smoothed_ref, turned_ref)
    smoothed = own_direction_ref[...] - step * smoothed_ref[...]
    smoothed_ref[...] = smoothed
    applied = own_image_ref[...] - step * turned_ref[...]
    applied_ref[...] = applied
    residual = own_right(right_ref) - step * own_image_ref[...]
    residual_ref[...] = residual
    lane = iota((1, 128), 1)
    cross = own_direction_ref[...] * applied + own_image_ref[...] * smoothed
    values = jnp.where(lane == 0, total(residual * smoothed), 0.0)
    values = jnp.where(lane == 1, total(smoothed * applied), values)
    payload_ref[...] = jnp.where(lane == 2, total(cross), values)


def last_kernel(
    parts_ref, known_ref, direction_ref, own_image_ref, smoothed_ref, applied_ref, residual_ref, field_ref, out_ref
):
    totals = parts_ref[0]
    for gx in range(1, 8):
        totals = totals + parts_ref[gx]
    gamma, delta = known_ref[:, 0:1], known_ref[:, 1:2]
    beta = totals[:, 0:1] / gamma
    step = totals[:, 0:1] / (totals[:, 1:2] + beta * (totals[:, 2:3] + beta * delta))
    direction = direction_ref[...]
    field = (gamma / delta) * direction + step * (smoothed_ref[...] + beta * direction)
    residual = residual_ref[...] - step * (applied_ref[...] + beta * own_image_ref[...])
    for x in range(4):
        field_ref[x] = field[2 * x : 2 * x + 2]
        out_ref[x] = residual[2 * x : 2 * x + 2]


VMEM = pl.BlockSpec(memory_space=pltpu.VMEM)
SMEM = pl.BlockSpec(memory_space=pltpu.SMEM)


def call(body, scalars, out_shape, scratch, *args, flops=10**7):
    specs = [SMEM] * scalars + [VMEM] * (len(args) - scalars)
    shapes = [jax.ShapeDtypeStruct(shape, dtype) for shape, dtype in out_shape]
    return pl.pallas_call(
        body,
        out_shape=shapes,
        in_specs=specs,
        out_specs=[VMEM] * len(shapes),
        scratch_shapes=[pltpu.VMEM(shape, dtype) for shape, dtype in scratch],
        cost_estimate=pl.CostEstimate(flops=flops, bytes_accessed=10**6, transcendentals=0),
        compiler_params=pltpu.CompilerParams(vmem_limit_bytes=16 * 1024 * 1024),
    )(*args)


FIELD = ((SLABS, NODES, 128), F32)
BLOCKS = ((6, NODES, 128), F32)
MARKS = ((8, 128), jnp.int32)
OWN = ((8, 512), F32)
CELLS = ((8, 128), F32)
ROW, WIDE = ((1, 128), F32), ((1, 256), F32)
COARSE_SCRATCH = [((10, 24, 128), F32), ((16, 128), F32), ((16, 128), F32)]
SUM_SCRATCH = [((6, 8, 128), F32), ((24, 128), F32)]
EDGE = ((3, NODES, 128), F32)
PAIR_FLOPS = 2 * 1024 * 384 * 256


def front_call(*args):
    return call(front_kernel, 3, [((1, 384), F32)], [], *args)[0]


def pack_call(blocks):
    return call(pack_kernel, 0, [((CLASSES * NODES, 384), jnp.bfloat16), ((128, 48), jnp.bfloat16)], [], blocks)


def coefficient_call(*args):
    return call(coefficient_kernel, 1, [MARKS, BLOCKS, BLOCKS], [], *args)


def local_call(*args):
    scratch = [FIELD, FIELD, ((SLABS, 128), jnp.int32)]
    return call(local_kernel, 2, [FIELD, FIELD, FIELD], scratch, *args, flops=7 * PAIR_FLOPS)


def first_call(*args):
    scratch = [FIELD] + COARSE_SCRATCH + SUM_SCRATCH
    return call(first_kernel, 2, [BLOCKS, EDGE, OWN, OWN, WIDE], scratch, *args, flops=3 * PAIR_FLOPS)


def near_call(*args):
    return call(near_kernel, 1, [BLOCKS], [BLOCKS, BLOCKS], *args, flops=3 * PAIR_FLOPS)[0]


def second_call(*args):
    scratch = [BLOCKS] + COARSE_SCRATCH + [OWN, BLOCKS, CELLS]
    return call(second_kernel, 2, [OWN, OWN, OWN, ROW, ROW], scratch, *args, flops=PAIR_FLOPS)


def shifted(x, axis, step):
    size = lax.axis_size(axis)
    pairs = [(i, i + step) for i in range(size) if 0 <= i + step < size]
    return lax.ppermute(x, axis, pairs)


def extend_z(wide):
    low = shifted(wide[:, 256:640], "gz", 1)
    high = shifted(wide[:, 0:384], "gz", -1)
    nothing = jnp.zeros((24, 112), F32)
    pieces = [low[:, 4:8], wide[:, 256:264], high[:, 256:260], nothing]
    return jnp.concatenate(pieces + [low[:, 128:384], wide[:, 0:256], wide[:, 384:640], high[:, 0:256]], axis=1)


def gather_cells(row):
    width = row.shape[1]
    parts = lax.all_to_all(jnp.broadcast_to(row[None], (128, 1, width)), ("gy", "gz"), 0, 0, tiled=True)
    plane = parts.reshape(16, 8, width).sum(axis=0)
    return lax.all_to_all(jnp.broadcast_to(plane[None], (8, 8, width)), "gx", 0, 0, tiled=True)


def gather_sum(row):
    parts = lax.all_to_all(jnp.broadcast_to(row[None], (128, 1, 128)), ("gy", "gz"), 0, 0, tiled=True)
    part = parts.reshape(128, 128).sum(axis=0)
    return lax.all_to_all(jnp.broadcast_to(part[None, None], (8, 1, 128)), "gx", 0, 0, tiled=True)


def per_device(right_side, element_class, class_blocks, class_shift, face_weights):
    place = jnp.stack([lax.axis_index(axis) for axis in AXES]).astype(jnp.int32)
    own = call(own_kernel, 0, [((8, 640), F32)], [], right_side, element_class)[0]
    wide = jnp.concatenate([shifted(own, "gx", 1), own, shifted(own, "gx", -1)], axis=0)
    packed, table = pack_call(class_blocks)
    row = front_call(place, face_weights, class_shift, wide, table)
    gathered = gather_cells(row)
    here = extend_z(wide)
    below, above = shifted(here, "gy", 1), shifted(here, "gy", -1)
    marks, near_inverse, sums = coefficient_call(place, below, here, above, table)
    local, inverse, keep = local_call(place, face_weights, below, here, above, table, packed)
    image, edge, direction, own_image, row = first_call(
        place, face_weights, gathered, local, inverse, keep, marks, near_inverse, sums, packed, own
    )
    again = gather_cells(row)
    from_below, from_above = shifted(edge, "gy", 1), shifted(edge, "gy", -1)
    near = near_call(face_weights, image, from_below, from_above, marks, near_inverse, packed)
    residual, smoothed, applied, known, row = second_call(
        place, face_weights, again, gathered, near, marks, near_inverse, sums, packed, own, direction, own_image
    )
    parts = gather_sum(row)
    shapes = [(right_side.shape, F32)] * 2
    return tuple(call(last_kernel, 0, shapes, [], parts, known, direction, own_image, smoothed, applied, residual))


def solution(mesh):
    in_specs = (P("gx", "gy", "gz"), P("gx", "gy", "gz"), P(), P(), P())
    out_specs = (P("gx", "gy", "gz"), P("gx", "gy", "gz"))
    return jax.shard_map(
        per_device, mesh=mesh, in_specs=in_specs, out_specs=out_specs, check_vma=False
    )
```

```python
import jax
import jax.numpy as jnp
from jax import lax
from jax.experimental import pallas as pl
from jax.experimental.pallas import tpu as pltpu
from jax.sharding import PartitionSpec as P

NODES = 64
CLASSES = 16
SLABS = 16
RELAX = 0.6
F32 = jnp.float32
HIGHEST = lax.Precision.HIGHEST
AXES = ("gx", "gy", "gz")


def dot(left, right):
    return jnp.dot(left, right, precision=HIGHEST, preferred_element_type=F32)


def iota(shape, dim):
    return lax.broadcasted_iota(jnp.int32, shape, dim)


def roll(values, shift, axis):
    return pltpu.roll(values, shift % values.shape[axis], axis)


def lane_places(shape):
    lane = iota(shape, len(shape) - 1)
    yd = (lane * 171) >> 12
    rest = lane - 24 * yd
    return rest >> 1, yd, rest & 1


def beside_1(v, lane, sub):
    a, b, gy = lane >> 6, (lane >> 4) & 3, lane & 15
    swapped = [roll(x, 64, 1) for x in v]
    result = []
    for gx in range(8):
        x = v[gx]
        total = swapped[gx] + jnp.where((gy & 1) == 0, roll(x, -1, 1), roll(x, 1, 1))
        if gx % 2 == 0:
            total = total + jnp.where(a == 1, swapped[gx + 1], 0.0)
        else:
            total = total + jnp.where(a == 0, swapped[gx - 1], 0.0)
        after = jnp.where((sub & 1) == 0, roll(roll(x, -1, 0), 48, 1), 0.0)
        before = jnp.where((sub & 1) == 1, roll(roll(x, 1, 0), -48, 1), 0.0)
        total = total + jnp.where(b < 3, roll(x, -16, 1), after)
        total = total + jnp.where(b > 0, roll(x, 16, 1), before)
        result.append(total)
    return result


def beside_2(v, lane, sub):
    b, gy = (lane >> 4) & 3, lane & 15
    result = []
    for gx in range(8):
        x = v[gx]
        total = jnp.where((gy & 2) == 0, roll(x, -2, 1), roll(x, 2, 1))
        if gx % 4 < 3:
            total = total + v[gx + 1]
        if gx % 4 > 0:
            total = total + v[gx - 1]
        after = jnp.where((sub & 3) < 3, roll(roll(x, -1, 0), 32, 1), 0.0)
        before = jnp.where((sub & 3) > 0, roll(roll(x, 1, 0), -32, 1), 0.0)
        total = total + jnp.where(b < 2, roll(x, -32, 1), after)
        total = total + jnp.where(b >= 2, roll(x, 32, 1), before)
        result.append(total)
    return result


def beside_3(v, lane, sub):
    gy = lane & 15
    result = []
    for gx in range(8):
        x = v[gx]
        total = jnp.where((gy & 4) == 0, roll(x, -4, 1), roll(x, 4, 1))
        if gx + 2 < 8:
            total = total + v[gx + 2]
        if gx - 2 >= 0:
            total = total + v[gx - 2]
        total = total + jnp.where(sub < 7, roll(x, -1, 0), 0.0)
        total = total + jnp.where(sub > 0, roll(x, 1, 0), 0.0)
        result.append(total)
    return result


def coarsen_1(v, lane):
    b, gy = (lane >> 4) & 3, lane & 15
    result = []
    for x in v:
        x = x + roll(x, 64, 1)
        x = x + jnp.where((b & 1) == 0, roll(x, -16, 1), roll(x, 16, 1))
        x = x + jnp.where((gy & 1) == 0, roll(x, -1, 1), roll(x, 1, 1))
        result.append(x)
    return result


def coarsen_2(v, lane):
    b, gy = (lane >> 4) & 3, lane & 15
    result = []
    for gx in range(8):
        x = v[gx] + v[gx ^ 1]
        x = x + jnp.where(b < 2, roll(x, -32, 1), roll(x, 32, 1))
        x = x + jnp.where((gy & 2) == 0, roll(x, -2, 1), roll(x, 2, 1))
        result.append(x)
    return result


def coarse_cycle(source, shift):
    lane, sub = iota((8, 128), 1), iota((8, 128), 0)
    eight = range(8)

    def remainder(beside, q, d, x):
        around = beside(x, lane, sub)
        return [q[i] - (d[i] * x[i] - around[i]) for i in eight]

    d1 = [6.0 + s for s in shift]
    shift2 = [0.125 * s for s in coarsen_1(shift, lane)]
    d2 = [6.0 + s for s in shift2]
    d3 = [6.0 + 0.125 * s for s in coarsen_2(shift2, lane)]
    w1 = [RELAX / d for d in d1]
    w2 = [RELAX / d for d in d2]
    w3 = [RELAX / d for d in d3]
    x1 = [w1[i] * source[i] for i in eight]
    q2 = [0.25 * t for t in coarsen_1(remainder(beside_1, source, d1, x1), lane)]
    x2 = [w2[i] * q2[i] for i in eight]
    q3 = [0.25 * t for t in coarsen_2(remainder(beside_2, q2, d2, x2), lane)]
    x3 = [w3[i] * q3[i] for i in eight]
    for _ in range(3):
        t3 = remainder(beside_3, q3, d3, x3)
        x3 = [x3[i] + w3[i] * t3[i] for i in eight]
    x2 = [x2[i] + x3[i] for i in eight]
    t2 = remainder(beside_2, q2, d2, x2)
    x2 = [x2[i] + w2[i] * t2[i] for i in eight]
    x1 = [x1[i] + x2[i] for i in eight]
    t1 = remainder(beside_1, source, d1, x1)
    return [x1[i] + w1[i] * t1[i] for i in eight]


def place_correction(coarse, place_ref, pad_ref, rows_ref, out_ref):
    gx0, gy0, gz0 = place_ref[0], place_ref[1], place_ref[2]
    pad_ref[...] = jnp.zeros_like(pad_ref)
    for gx in range(8):
        pad_ref[gx + 1, 8:16, :] = coarse[gx]
    rows_ref[...] = jnp.zeros_like(rows_ref)
    for e in range(3):
        for d in range(3):
            rows_ref[3 * e + d : 3 * e + d + 1, :] = pad_ref[gx0 + d, pl.ds(gz0 + 7 + e, 1), :]
    shape = (128, 512)
    source = iota(shape, 0)
    column = iota(shape, 1)
    target = column & 127
    yd = (target * 171) >> 12
    x = (target - 24 * yd) >> 1
    hit = ((source >> 4) & 3) == (column >> 7)
    hit = hit & ((source >> 6) == ((x >> 1) & 1))
    hit = hit & ((source & 15) == gy0 - 2 + yd) & (target < 120)
    spread = dot(rows_ref[...], jnp.where(hit, 1.0, 0.0))
    lane_x, _, _ = lane_places((1, 128))
    part = lane_x >> 2
    for t in range(8):
        e, b = (t + 2) // 4, (t + 2) % 4
        pieces = [spread[3 * e + d : 3 * e + d + 1, 128 * b : 128 * b + 128] for d in range(3)]
        row = jnp.where(part == 0, pieces[0], jnp.where(part == 1, pieces[1], pieces[2]))
        out_ref[2 * t : 2 * t + 1, :] = row
        out_ref[2 * t + 1 : 2 * t + 2, :] = row


def groups(values):
    return [values[8 * g : 8 * g + 8] for g in range(8)]


def packed_places(shape):
    lane = iota(shape, len(shape) - 1)
    rest = (lane & 63) + 4
    yd = 1 + ((rest * 171) >> 12)
    rest = rest - 24 * (yd - 1)
    return rest >> 1, yd, rest & 1, lane >> 6


def dense(values, marks, packed_ref):
    first = values.astype(jnp.bfloat16)
    rest = values - first.astype(F32)
    second = rest.astype(jnp.bfloat16)
    third = (rest - second.astype(F32)).astype(jnp.bfloat16)
    stack = jnp.concatenate([first, second, third, first, second, first], axis=0)
    products = jnp.dot(packed_ref[...], stack, preferred_element_type=F32)
    result = []
    for part, row in enumerate(marks):
        row = jnp.broadcast_to(row, (8, 128))
        columns = slice(128 * part, 128 * part + 128)
        chosen = [products[8 * g : 8 * g + 8, columns] for g in range(8)]
        for k in range(1, CLASSES):
            hit = row == k
            for g in range(8):
                at = 64 * k + 8 * g
                chosen[g] = jnp.where(hit, products[at : at + 8, columns], chosen[g])
        result.append(chosen)
    return result


class Full:
    def __init__(self, slab):
        self.parts = groups(slab)
        self.yi = lane_places((8, 128))[2]

    def here(self, g):
        return self.parts[g]

    def shift(self, g, step):
        return roll(self.parts[g], -step, 1)


class Pack:
    def __init__(self, low, high):
        self.low, self.high = groups(low), groups(high)
        self.yi = packed_places((8, 128))[2]

    def here(self, g):
        return self.shift(g, 0)

    def shift(self, g, step):
        lane = iota((8, 128), 1)
        return jnp.where(lane < 64, roll(self.low[g], -28 - step, 1), roll(self.high[g], 36 - step, 1))


class Block(Full):
    def __init__(self, block):
        self.parts = groups(block)
        self.yi = packed_places((8, 128))[2]


def upward_y(view, g):
    return jnp.where(view.yi == 0, view.shift(g, 1), view.shift(g, 23))


def downward_y(view, g):
    return jnp.where(view.yi == 1, view.shift(g, -1), view.shift(g, -23))


def face_weights_of(weights_ref):
    sub = iota((8, 128), 0)
    wx, wy, wz = weights_ref[0], weights_ref[1], weights_ref[2]
    top = jnp.where((sub & 3) == 3, wz, 0.0), jnp.where(sub >= 4, wy, 0.0)
    bottom = jnp.where((sub & 3) == 0, wz, 0.0), jnp.where(sub < 4, wy, 0.0)
    return wx, top, bottom


def coupling(before, view, after, weights_ref):
    wx, (wz_top, wy_top), (wz_bottom, wy_bottom) = face_weights_of(weights_ref)
    result = []
    for g in range(8):
        term = wz_top * roll(after[g], 3, 0) + wz_bottom * roll(before[g], -3, 0)
        if g % 2 == 1:
            term = term + wy_top * roll(upward_y(view, g - 1), 4, 0)
        else:
            term = term + wy_bottom * roll(downward_y(view, g + 1), 4, 0)
        if g >= 6:
            term = term + wx * view.shift(g - 6, 2)
        if g < 2:
            term = term + wx * view.shift(g + 6, -2)
        result.append(term)
    return result


def constant_coupling(before, here, after, yi, weights_ref):
    wx, (wz_top, wy_top), (wz_bottom, wy_bottom) = face_weights_of(weights_ref)

    def wide(row):
        return jnp.broadcast_to(row, (8, 128))

    here = wide(here)
    up = jnp.where(yi == 0, roll(here, -1, 1), roll(here, -23, 1))
    down = jnp.where(yi == 1, roll(here, 1, 1), roll(here, 23, 1))
    along = wz_top * wide(after) + wz_bottom * wide(before)
    even, odd = along + wy_bottom * down, along + wy_top * up
    result = [even if g % 2 == 0 else odd for g in range(8)]
    for g in (0, 1):
        result[g] = result[g] + wx * roll(here, 2, 1)
    for g in (6, 7):
        result[g] = result[g] + wx * roll(here, -2, 1)
    return result


def block_before(ref, j):
    return ref[j - 1] if j > 0 else roll(ref[5], 64, 1)


def block_after(ref, j):
    return ref[j + 1] if j < 5 else roll(ref[0], 64, 1)


def restrict(source_ref, inverse_ref, sums_ref, weights_ref, all_ref, out_ref):
    wx, (wz_top, wy_top), (wz_bottom, wy_bottom) = face_weights_of(weights_ref)
    _, _, yi, _ = packed_places((8, 128))
    totals = []
    out_ref[...] = jnp.zeros_like(out_ref)
    for j in range(6):
        r = source_ref[j]
        x = inverse_ref[j] * r
        d = groups(r - sums_ref[j] * x)
        xs = groups(x)
        even = (xs[0] + xs[2]) + (xs[4] + xs[6])
        odd = (xs[1] + xs[3]) + (xs[5] + xs[7])
        local = ((d[0] + d[1]) + (d[2] + d[3])) + ((d[4] + d[5]) + (d[6] + d[7]))
        local = local + wx * (roll(xs[0] + xs[1], -2, 1) + roll(xs[6] + xs[7], 2, 1))
        upper, lower = wy_top * odd, wy_bottom * even
        totals.append(local + jnp.where(yi == 0, roll(lower, -1, 1), roll(upper, 1, 1)))
        all_ref[j] = even + odd
        out_ref[8 + j : 9 + j, :] = jnp.sum(jnp.where(yi == 1, upper, 0.0), axis=0, keepdims=True)
        out_ref[16 + j : 17 + j, :] = jnp.sum(jnp.where(yi == 0, lower, 0.0), axis=0, keepdims=True)
    for j in range(6):
        value = totals[j] + wz_bottom * block_after(all_ref, j) + wz_top * block_before(all_ref, j)
        out_ref[j : j + 1, :] = jnp.sum(value, axis=0, keepdims=True)


def payload(cells, place_ref, scale):
    shape = (128, 256)
    source, column = iota(shape, 0), iota(shape, 1)
    own = (source & 63) - 28
    hit = (own >= 0) & (own < 8) & ((source >> 6) == (column >> 7)) & ((own >> 2) == ((column & 127) >> 6))
    spread = dot(cells, jnp.where(hit, scale, 0.0))
    block, column = iota((8, 256), 0), iota((8, 256), 1)
    z = block - 2 + 6 * (column >> 7)
    keep = (block < 6) & (z >= 0) & (z < 8) & ((z >> 1) == ((column >> 4) & 3))
    gy, gy0 = column & 15, place_ref[1]
    value = jnp.where(gy == gy0, spread[0:8], jnp.where(gy == gy0 + 1, spread[8:16], 0.0))
    value = value + jnp.where(gy == gy0 - 1, spread[16:24], 0.0)
    row = jnp.sum(jnp.where(keep, value, 0.0), axis=0, keepdims=True)
    return row[:, 0:128] + row[:, 128:256]


def gather_own(planes):
    lane = iota((64, 128), 1)
    result = jnp.zeros((64, 128), F32)
    for z, (plane, first) in enumerate(planes):
        result = jnp.where((lane >> 3) == z, roll(plane, 8 * z - first, 1), result)
    return result


def own_of_packed(blocks):
    return gather_own([(blocks[z + 2], 28) if z < 4 else (blocks[z - 4], 92) for z in range(8)])


def own_rows(first, second, first_ref, second_ref):
    turned = jnp.concatenate([first, second], axis=0).T
    low = iota((8, 128), 1) < 64
    for pair in range(4):
        even = turned[16 * pair : 16 * pair + 8]
        odd = turned[16 * pair + 8 : 16 * pair + 16]
        columns = slice(128 * pair, 128 * pair + 128)
        first_ref[:, columns] = jnp.where(low, even, roll(odd, 64, 1))
        second_ref[:, columns] = jnp.where(low, roll(even, 64, 1), odd)


def coefficients(rows, table_ref):
    halves = []
    for row in rows:
        wide = jnp.broadcast_to(row, (CLASSES, 128))
        halves.append(jnp.where(wide == iota((CLASSES, 128), 0), 1.0, 0.0))
    onehot = jnp.concatenate(halves, axis=1)
    onehot = jnp.concatenate([onehot] * 3, axis=0).astype(jnp.bfloat16)
    return jnp.dot(table_ref[...], onehot, preferred_element_type=F32)


def relaxation(x, yd, slab, place_ref):
    gx, gy = place_ref[0] - 1 + (x >> 2), place_ref[1] - 2 + yd
    gz = place_ref[2] - 1 + ((slab + 4) >> 3)
    inside = (gx >= 0) & (gx < 8) & (gy >= 0) & (gy < 16) & (gz >= 0) & (gz < 8) & (yd < 5)
    return jnp.where(inside, RELAX, 0.0)


def total(values):
    return jnp.sum(jnp.sum(values, axis=0, keepdims=True), axis=1, keepdims=True)


def own_right(own_ref):
    return jnp.concatenate([own_ref[:, 0:256], own_ref[:, 384:640]], axis=1)


def split(values):
    first = values.astype(jnp.bfloat16).astype(F32)
    rest = values - first
    second = rest.astype(jnp.bfloat16).astype(F32)
    return first, second, rest - second


def cell_parts(own_ref, table, weights_ref, shift_ref):
    pieces = []
    for pair in range(4):
        start = 128 * pair if pair < 2 else 128 * pair + 128
        values = own_ref[:, start : start + 128]
        pieces += [values, roll(values, 64, 1)]
    b = jnp.concatenate(pieces + [jnp.zeros((64, 128), F32)], axis=0).T[0:64]
    turned = jnp.concatenate([own_ref[:, 256:384], jnp.zeros((120, 128), F32)], axis=0).T
    lane = iota((1, 128), 1)
    marks = jnp.zeros((1, 128), F32)
    for z in range(8):
        marks = jnp.where((lane >> 3) == z, roll(turned[z : z + 1], 8 * z, 1), marks)
    marks = marks.astype(jnp.int32)
    both = coefficients([marks], table)
    x0 = (RELAX / both[:64]) * b
    d, xs = groups(b - both[64:] * x0), groups(x0)
    wx, wy, wz = weights_ref[0], weights_ref[1], weights_ref[2]
    sub = iota((8, 128), 0)
    even = (xs[0] + xs[2]) + (xs[4] + xs[6])
    odd = (xs[1] + xs[3]) + (xs[5] + xs[7])
    every = even + odd

    def along(values):
        return jnp.sum(values, axis=0, keepdims=True)

    local = along(((d[0] + d[1]) + (d[2] + d[3])) + ((d[4] + d[5]) + (d[6] + d[7])))
    x_low, x_high = wx * along(xs[0] + xs[1]), wx * along(xs[6] + xs[7])
    y_low, y_high = wy * along(jnp.where(sub < 4, even, 0.0)), wy * along(jnp.where(sub >= 4, odd, 0.0))
    z_low = wz * along(jnp.where((sub & 3) == 0, every, 0.0))
    z_high = wz * along(jnp.where((sub & 3) == 3, every, 0.0))
    x, yi, z = (lane >> 1) & 3, lane & 1, lane >> 3
    local = local + jnp.where(x > 0, roll(x_high, 2, 1), 0.0) + jnp.where(x < 3, roll(x_low, -2, 1), 0.0)
    local = local + jnp.where(yi == 1, roll(y_high, 1, 1), roll(y_low, -1, 1))
    local = local + jnp.where(z > 0, roll(z_high, 8, 1), 0.0) + jnp.where(z < 7, roll(z_low, -8, 1), 0.0)
    shifts = jnp.zeros((1, 128), F32)
    for k in range(CLASSES):
        shifts = jnp.where(marks == k, shift_ref[k], shifts)
    scale = 1.0 / NODES
    return jnp.concatenate(
        [
            scale * local,
            scale * jnp.where(yi == 1, y_high, 0.0),
            scale * jnp.where(yi == 0, y_low, 0.0),
            0.125 * shifts,
            scale * jnp.where(x == 3, x_high, jnp.where(x == 0, x_low, 0.0)),
            scale * jnp.where(z == 7, z_high, jnp.where(z == 0, z_low, 0.0)),
            jnp.zeros((2, 128), F32),
        ],
        axis=0,
    )


def front_kernel(
    place_ref, weights_ref, shift_ref, right_ref, marks_ref, blocks_ref,
    own_ref, table_ref, payload_ref,
):
    own_ref[:, 256:384] = jnp.zeros((8, 128), F32)
    for x in range(4):
        rows = slice(2 * x, 2 * x + 2)
        values = right_ref[x]
        own_ref[rows, 0:256] = values[:, 0:256]
        own_ref[rows, 384:640] = values[:, 256:512]
        own_ref[rows, 256:264] = marks_ref[x].astype(F32)
    diagonal = jnp.where(iota((64, 64), 0) == iota((64, 64), 1), 1.0, 0.0)
    rows = []
    for k in range(CLASSES):
        block = blocks_ref[k]
        diag = jnp.sum(block * diagonal, axis=0, keepdims=True)
        rows.append(jnp.concatenate([diag, jnp.sum(block, axis=0, keepdims=True)], axis=1))
    parts = split(jnp.concatenate(rows, axis=0))
    table = jnp.concatenate(list(parts) + [jnp.zeros((80, 128), F32)], axis=0).T
    table_ref[...] = table[:, 0:48].astype(jnp.bfloat16)

    parts = cell_parts(own_ref, table_ref, weights_ref, shift_ref)
    shape = (128, 128)
    source, target = iota(shape, 0), iota(shape, 1)
    hit = (source < 64) & (((source >> 2) & 1) == (target >> 6)) & ((source >> 4) == ((target >> 4) & 3))
    cells = dot(parts, jnp.where(hit, 1.0, 0.0))
    lane = iota((1, 128), 1)
    b, gy, gy0 = (lane >> 4) & 3, lane & 15, place_ref[1]
    row = jnp.where(gy == gy0, cells[0:1], jnp.where(gy == gy0 + 1, cells[1:2], 0.0))
    row = row + jnp.where(gy == gy0 - 1, cells[2:3], 0.0)
    row = row + jnp.where(gy == ((gy0 + 8) & 15), cells[3:4], 0.0)
    row = row + jnp.where(gy == ((gy0 + 4) & 15), roll(cells[4:5], 64, 1), 0.0)
    far = gy == ((gy0 + 12) & 15)
    row = row + jnp.where(far & (b == 0), roll(cells[5:6], -48, 1), 0.0)
    payload_ref[...] = row + jnp.where(far & (b == 3), roll(cells[5:6], 48, 1), 0.0)


def rotate(values, step):
    gy = iota(values.shape, 1) & 15
    return jnp.where(gy + step < 16, roll(values, -step, 1), roll(values, 16 - step, 1))


def join_parts(gathered_ref):
    lane, sub = iota((8, 128), 1), iota((8, 128), 0)
    a, b = lane >> 6, (lane >> 4) & 3
    result = []
    for gx in range(8):
        value = gathered_ref[gx, :, 0:128]
        if gx > 0:
            value = value + jnp.where(a == 0, rotate(gathered_ref[gx - 1, :, 256:384], 4), 0.0)
        if gx < 7:
            value = value + jnp.where(a == 1, rotate(gathered_ref[gx + 1, :, 256:384], 4), 0.0)
        z = rotate(gathered_ref[gx, :, 384:512], 12)
        value = value + jnp.where((b == 0) & (sub > 0), roll(z, 1, 0), 0.0)
        value = value + jnp.where((b == 3) & (sub < 7), roll(z, -1, 0), 0.0)
        result.append(value)
    return result


def pack_kernel(blocks_ref, packed_ref):
    low = iota((64, 128), 1) < 64
    for k in range(CLASSES):
        block = blocks_ref[k]
        first, second, third = split(jnp.concatenate([block, block], axis=1))
        at = slice(64 * k, 64 * k + 64)
        packed_ref[at, 0:128] = first.astype(jnp.bfloat16)
        packed_ref[at, 128:256] = jnp.where(low, first, second).astype(jnp.bfloat16)
        packed_ref[at, 256:384] = jnp.where(low, second, third).astype(jnp.bfloat16)


def coefficient_kernel(place_ref, below_ref, here_ref, above_ref, table_ref, class_ref, inverse_ref, sums_ref):
    marks = jnp.concatenate([below_ref[4:24, 0:128], here_ref[:, 0:128], above_ref[0:20, 0:128]], axis=0)
    marks = jnp.concatenate([marks, marks], axis=0).T[0:16].astype(jnp.int32)
    low = iota((1, 128), 1) < 64
    class_ref[...] = jnp.zeros((8, 128), jnp.int32)
    x, yd, _, half = packed_places((1, 128))
    for j in range(6):
        class_ref[j : j + 1, :] = jnp.where(low, marks[2 + j : 3 + j], marks[8 + j : 9 + j])
    for j in (0, 2, 4):
        both = coefficients([class_ref[j : j + 1, :], class_ref[j + 1 : j + 2, :]], table_ref)
        for part in range(2):
            columns = slice(128 * part, 128 * part + 128)
            relax = relaxation(x, yd, 2 + j + part + 6 * half, place_ref)
            inverse_ref[j + part] = relax / both[:64, columns]
            sums_ref[j + part] = both[64:, columns]


def local_kernel(
    place_ref, weights_ref, below_ref, here_ref, above_ref, table_ref, packed_ref,
    smooth_ref, inverse_ref, keep_ref,
    field_ref, iterate_ref, class_ref,
):
    def turned(block):
        columns = slice(128 * block, 128 * block + 128)
        middle = [ref[:, columns] for ref in (below_ref, here_ref, above_ref)]
        return jnp.concatenate([jnp.zeros((24, 128), F32)] + middle + [jnp.zeros((32, 128), F32)], axis=0).T

    class_ref[...] = turned(0)[0:16].astype(jnp.int32)
    x, yd, _ = lane_places((1, 128))
    for pair in range(SLABS // 2):
        block = turned(pair + 1)
        both = coefficients([class_ref[2 * pair + i : 2 * pair + i + 1, :] for i in (0, 1)], table_ref)
        for part in range(2):
            s = 2 * pair + part
            columns = slice(128 * part, 128 * part + 128)
            values = block[64 * part : 64 * part + 64]
            inverse = relaxation(x, yd, s, place_ref) / both[:64, columns]
            field_ref[s] = values
            inverse_ref[s] = inverse
            keep_ref[s] = 1.0 - inverse * both[64:, columns]
            iterate_ref[s] = inverse * values
    for s in (0, 15):
        smooth_ref[s] = jnp.zeros((64, 128), F32)
    for s in range(1, 14, 2):
        planes = [iterate_ref[s + i] for i in (-1, 0, 1, 2)]
        marks = [class_ref[s + i : s + i + 1, :] for i in (0, 1)]
        chosen = dense(jnp.concatenate(planes[1:3], axis=1), marks, packed_ref)
        for part in range(2):
            faces = coupling(groups(planes[part]), Full(planes[part + 1]), groups(planes[part + 2]), weights_ref)
            for g in range(8):
                at = (s + part, slice(8 * g, 8 * g + 8))
                value = chosen[part][g] - faces[g]
                smooth_ref[at] = iterate_ref[at] + inverse_ref[at] * (field_ref[at] - value)


def first_kernel(
    place_ref, weights_ref, gathered_ref, local_ref, inverse_ref, keep_ref, class_ref, near_inverse_ref, sums_ref,
    packed_ref, right_ref,
    image_ref, edge_ref, own_direction_ref, own_image_ref, payload_ref,
    smooth_ref, pad_ref, rows_ref, shift_ref, all_ref, cells_ref,
):
    coarse = coarse_cycle(join_parts(gathered_ref), [rotate(gathered_ref[g, :, 128:256], 8) for g in range(8)])
    place_correction(coarse, place_ref, pad_ref, rows_ref, shift_ref)
    _, _, yi = lane_places((8, 128))
    for s in range(1, 15):
        here = shift_ref[s : s + 1, :]
        faces = constant_coupling(shift_ref[s - 1 : s, :], here, shift_ref[s + 1 : s + 2, :], yi, weights_ref)
        here = jnp.broadcast_to(here, (8, 128))
        for g in range(8):
            at = (s, slice(8 * g, 8 * g + 8))
            smooth_ref[at] = local_ref[at] + (keep_ref[at] * here + inverse_ref[at] * faces[g])

    lane = iota((64, 128), 1)

    def block(j):
        return jnp.where(lane < 64, roll(smooth_ref[2 + j], -28, 1), roll(smooth_ref[8 + j], 36, 1))

    blocks = [block(j) for j in range(-1, 7)]
    for j in (0, 2, 4):
        marks = [class_ref[j + i : j + i + 1, :] for i in (0, 1)]
        chosen = dense(jnp.concatenate([blocks[j + 1], blocks[j + 2]], axis=1), marks, packed_ref)
        for part in range(2):
            at = j + part
            view = Pack(smooth_ref[2 + at], smooth_ref[8 + at])
            faces = coupling(groups(blocks[at]), view, groups(blocks[at + 2]), weights_ref)
            for g in range(8):
                image_ref[at, 8 * g : 8 * g + 8] = chosen[part][g] - faces[g]
    own = (lane & 63) >= 20
    own = own & ((lane & 63) < 44)
    for j in range(3):
        edge_ref[j] = jnp.where(own, image_ref[j], roll(image_ref[j + 3], 32, 1))
    restrict(image_ref, near_inverse_ref, sums_ref, weights_ref, all_ref, cells_ref)
    row = payload(cells_ref[...], place_ref, 1.0 / NODES)
    own_z = gather_own([(smooth_ref[z + 4], 56) for z in range(8)])
    own_rows(own_z, own_of_packed(image_ref), own_direction_ref, own_image_ref)
    direction = own_direction_ref[...]
    lane = iota((1, 128), 1)
    gamma, delta = total(own_right(right_ref) * direction), total(direction * own_image_ref[...])
    far = (lane & 15) == ((place_ref[1] + 8) & 15)
    row = row + jnp.where(far & ((lane >> 4) == 0), gamma, 0.0)
    payload_ref[...] = row + jnp.where(far & ((lane >> 4) == 1), delta, 0.0)


def near_kernel(
    weights_ref, own_ref, below_ref, above_ref, class_ref, inverse_ref, packed_ref,
    smooth_ref,
    iterate_ref, image_ref,
):
    lane = iota((64, 128), 1) & 63
    for j in range(6):
        below = roll(below_ref[j % 3], -24 if j < 3 else -56, 1)
        above = roll(above_ref[j % 3], 24 if j < 3 else -8, 1)
        image_ref[j] = jnp.where(lane < 20, below, jnp.where(lane < 44, own_ref[j], above))
        iterate_ref[j] = inverse_ref[j] * image_ref[j]
    for j in (0, 2, 4):
        marks = [class_ref[j + i : j + i + 1, :] for i in (0, 1)]
        chosen = dense(jnp.concatenate([iterate_ref[j], iterate_ref[j + 1]], axis=1), marks, packed_ref)
        for part in range(2):
            at = j + part
            before, after = groups(block_before(iterate_ref, at)), groups(block_after(iterate_ref, at))
            faces = coupling(before, Block(iterate_ref[at]), after, weights_ref)
            for g in range(8):
                place = (at, slice(8 * g, 8 * g + 8))
                value = chosen[part][g] - faces[g]
                smooth_ref[place] = iterate_ref[place] + inverse_ref[place] * (image_ref[place] - value)


def second_kernel(
    place_ref, weights_ref, gathered_ref, shifts_ref, local_ref, class_ref, inverse_ref, sums_ref, packed_ref,
    right_ref, own_direction_ref, own_image_ref,
    residual_ref, smoothed_ref, applied_ref, known_ref, payload_ref,
    smooth_ref, pad_ref, rows_ref, shift_ref, turned_ref, image_ref, near_ref,
):
    coarse = coarse_cycle(
        [gathered_ref[g, :, 0:128] for g in range(8)], [rotate(shifts_ref[g, :, 128:256], 8) for g in range(8)]
    )
    place_correction(coarse, place_ref, pad_ref, rows_ref, shift_ref)
    lane = iota((8, 128), 1)
    near_ref[...] = jnp.where(lane < 64, roll(shift_ref[2:10, :], -28, 1), roll(shift_ref[8:16, :], 36, 1))
    _, _, yi, _ = packed_places((8, 128))

    def row(j):
        return near_ref[j : j + 1, :]

    for j in range(6):
        before = row(j - 1) if j > 0 else roll(row(5), 64, 1)
        after = row(j + 1) if j < 5 else roll(row(0), 64, 1)
        faces = constant_coupling(before, row(j), after, yi, weights_ref)
        here = jnp.broadcast_to(row(j), (8, 128))
        for g in range(8):
            at = (j, slice(8 * g, 8 * g + 8))
            inverse = inverse_ref[at]
            smooth_ref[at] = local_ref[at] + (here + inverse * (faces[g] - sums_ref[at] * here))

    own_y = own_of_packed(smooth_ref)
    own_marks = gather_own(
        [(jnp.broadcast_to(class_ref[j : j + 1, :].astype(F32), (64, 128)), first)
         for j, first in [(2, 28), (3, 28), (4, 28), (5, 28), (0, 92), (1, 92), (2, 92), (3, 92)]]
    )
    chosen = dense(own_y, [own_marks[0:1].astype(jnp.int32)], packed_ref)[0]
    for j in range(6):
        before, after = groups(block_before(smooth_ref, j)), groups(block_after(smooth_ref, j))
        faces = coupling(before, Block(smooth_ref[j]), after, weights_ref)
        for g in range(8):
            image_ref[j, 8 * g : 8 * g + 8] = faces[g]
    own_v = jnp.concatenate(chosen, axis=0) - own_of_packed(image_ref)

    sums = gathered_ref[0, :, 128:256]
    for g in range(1, 8):
        sums = sums + gathered_ref[g, :, 128:256]
    sums = jnp.sum(sums, axis=0, keepdims=True)
    slot = iota((1, 128), 1) >> 4
    gamma, delta = total(jnp.where(slot == 0, sums, 0.0)), total(jnp.where(slot == 1, sums, 0.0))
    lane = iota((1, 128), 1)
    known_ref[...] = jnp.where(lane == 0, gamma, jnp.where(lane == 1, delta, 0.0))
    step = gamma / delta
    own_rows(own_y, own_v, smoothed_ref, turned_ref)
    smoothed = own_direction_ref[...] - step * smoothed_ref[...]
    smoothed_ref[...] = smoothed
    applied = own_image_ref[...] - step * turned_ref[...]
    applied_ref[...] = applied
    residual = own_right(right_ref) - step * own_image_ref[...]
    residual_ref[...] = residual
    lane = iota((1, 128), 1)
    cross = own_direction_ref[...] * applied + own_image_ref[...] * smoothed
    values = jnp.where(lane == 0, total(residual * smoothed), 0.0)
    values = jnp.where(lane == 1, total(smoothed * applied), values)
    payload_ref[...] = jnp.where(lane == 2, total(cross), values)


def last_kernel(
    parts_ref, known_ref, direction_ref, own_image_ref, smoothed_ref, applied_ref, residual_ref, field_ref, out_ref
):
    totals = parts_ref[0]
    for gx in range(1, 8):
        totals = totals + parts_ref[gx]
    gamma, delta = known_ref[:, 0:1], known_ref[:, 1:2]
    beta = totals[:, 0:1] / gamma
    step = totals[:, 0:1] / (totals[:, 1:2] + beta * (totals[:, 2:3] + beta * delta))
    direction = direction_ref[...]
    field = (gamma / delta) * direction + step * (smoothed_ref[...] + beta * direction)
    residual = residual_ref[...] - step * (applied_ref[...] + beta * own_image_ref[...])
    for x in range(4):
        field_ref[x] = field[2 * x : 2 * x + 2]
        out_ref[x] = residual[2 * x : 2 * x + 2]


VMEM = pl.BlockSpec(memory_space=pltpu.VMEM)
SMEM = pl.BlockSpec(memory_space=pltpu.SMEM)


def call(body, scalars, out_shape, scratch, *args, flops=10**7):
    specs = [SMEM] * scalars + [VMEM] * (len(args) - scalars)
    shapes = [jax.ShapeDtypeStruct(shape, dtype) for shape, dtype in out_shape]
    return pl.pallas_call(
        body,
        out_shape=shapes,
        in_specs=specs,
        out_specs=[VMEM] * len(shapes),
        scratch_shapes=[pltpu.VMEM(shape, dtype) for shape, dtype in scratch],
        cost_estimate=pl.CostEstimate(flops=flops, bytes_accessed=10**6, transcendentals=0),
        compiler_params=pltpu.CompilerParams(vmem_limit_bytes=16 * 1024 * 1024),
    )(*args)


FIELD = ((SLABS, NODES, 128), F32)
BLOCKS = ((6, NODES, 128), F32)
MARKS = ((8, 128), jnp.int32)
OWN = ((8, 512), F32)
CELLS = ((8, 128), F32)
ROW = ((1, 128), F32)
COARSE_SCRATCH = [((10, 24, 128), F32), ((16, 128), F32), ((16, 128), F32)]
SUM_SCRATCH = [((6, 8, 128), F32), ((24, 128), F32)]
EDGE = ((3, NODES, 128), F32)
PAIR_FLOPS = 2 * 1024 * 384 * 256


def front_call(*args):
    return call(front_kernel, 3, [((8, 640), F32), ((128, 48), jnp.bfloat16), ROW], [], *args)


def pack_call(blocks):
    return call(pack_kernel, 0, [((CLASSES * NODES, 384), jnp.bfloat16)], [], blocks)[0]


def coefficient_call(*args):
    return call(coefficient_kernel, 1, [MARKS, BLOCKS, BLOCKS], [], *args)


def local_call(*args):
    scratch = [FIELD, FIELD, ((SLABS, 128), jnp.int32)]
    return call(local_kernel, 2, [FIELD, FIELD, FIELD], scratch, *args, flops=7 * PAIR_FLOPS)


def first_call(*args):
    scratch = [FIELD] + COARSE_SCRATCH + SUM_SCRATCH
    return call(first_kernel, 2, [BLOCKS, EDGE, OWN, OWN, ROW], scratch, *args, flops=3 * PAIR_FLOPS)


def near_call(*args):
    return call(near_kernel, 1, [BLOCKS], [BLOCKS, BLOCKS], *args, flops=3 * PAIR_FLOPS)[0]


def second_call(*args):
    scratch = [BLOCKS] + COARSE_SCRATCH + [OWN, BLOCKS, CELLS]
    return call(second_kernel, 2, [OWN, OWN, OWN, ROW, ROW], scratch, *args, flops=PAIR_FLOPS)


def shifted(x, axis, step):
    size = lax.axis_size(axis)
    pairs = [(i, i + step) for i in range(size) if 0 <= i + step < size]
    return lax.ppermute(x, axis, pairs)


def extend_xz(own):
    wide = jnp.concatenate([shifted(own, "gx", 1), own, shifted(own, "gx", -1)], axis=0)
    low = shifted(wide[:, 256:640], "gz", 1)
    high = shifted(wide[:, 0:384], "gz", -1)
    nothing = jnp.zeros((24, 112), F32)
    pieces = [low[:, 4:8], wide[:, 256:264], high[:, 256:260], nothing]
    return jnp.concatenate(pieces + [low[:, 128:384], wide[:, 0:256], wide[:, 384:640], high[:, 0:256]], axis=1)


def gather_cells(row, *offsets):
    parts = lax.all_to_all(jnp.broadcast_to(row[None], (128, 1, 128)), ("gy", "gz"), 0, 0, tiled=True)
    parts = parts.reshape(16, 8, 128)
    offset = (iota(parts.shape, 2) - iota(parts.shape, 0)) & 15
    near = (offset == 0) | (offset == 1) | (offset == 15)
    keeps = [near] + [offset == value for value in offsets]
    plane = jnp.concatenate([jnp.where(keep, parts, 0.0).sum(axis=0) for keep in keeps], axis=1)
    shape = (8,) + plane.shape
    return lax.all_to_all(jnp.broadcast_to(plane[None], shape), "gx", 0, 0, tiled=True)


def gather_sum(row):
    parts = lax.all_to_all(jnp.broadcast_to(row[None], (128, 1, 128)), ("gy", "gz"), 0, 0, tiled=True)
    part = parts.reshape(128, 128).sum(axis=0)
    return lax.all_to_all(jnp.broadcast_to(part[None, None], (8, 1, 128)), "gx", 0, 0, tiled=True)


def per_device(right_side, element_class, class_blocks, class_shift, face_weights):
    place = jnp.stack([lax.axis_index(axis) for axis in AXES]).astype(jnp.int32)
    own, table, row = front_call(place, face_weights, class_shift, right_side, element_class, class_blocks)
    gathered = gather_cells(row, 8, 4, 12)
    packed = pack_call(class_blocks)
    here = extend_xz(own)
    below, above = shifted(here, "gy", 1), shifted(here, "gy", -1)
    marks, near_inverse, sums = coefficient_call(place, below, here, above, table)
    local, inverse, keep = local_call(place, face_weights, below, here, above, table, packed)
    image, edge, direction, own_image, row = first_call(
        place, face_weights, gathered, local, inverse, keep, marks, near_inverse, sums, packed, own
    )
    again = gather_cells(row, 8)
    from_below, from_above = shifted(edge, "gy", 1), shifted(edge, "gy", -1)
    near = near_call(face_weights, image, from_below, from_above, marks, near_inverse, packed)
    residual, smoothed, applied, known, row = second_call(
        place, face_weights, again, gathered, near, marks, near_inverse, sums, packed, own, direction, own_image
    )
    parts = gather_sum(row)
    shapes = [(right_side.shape, F32)] * 2
    return tuple(call(last_kernel, 0, shapes, [], parts, known, direction, own_image, smoothed, applied, residual))


def solution(mesh):
    in_specs = (P("gx", "gy", "gz"), P("gx", "gy", "gz"), P(), P(), P())
    out_specs = (P("gx", "gy", "gz"), P("gx", "gy", "gz"))
    return jax.shard_map(
        per_device, mesh=mesh, in_specs=in_specs, out_specs=out_specs, check_vma=False
    )
```

```python
import jax
import jax.numpy as jnp
from jax import lax
from jax.experimental import pallas as pl
from jax.experimental.pallas import tpu as pltpu
from jax.sharding import PartitionSpec as P

NODES = 64
CLASSES = 16
SLABS = 16
RELAX = 0.6
F32 = jnp.float32
HIGHEST = lax.Precision.HIGHEST
AXES = ("gx", "gy", "gz")


def dot(left, right):
    return jnp.dot(left, right, precision=HIGHEST, preferred_element_type=F32)


def iota(shape, dim):
    return lax.broadcasted_iota(jnp.int32, shape, dim)


def roll(values, shift, axis):
    return pltpu.roll(values, shift % values.shape[axis], axis)


def lane_places(shape):
    lane = iota(shape, len(shape) - 1)
    yd = (lane * 171) >> 12
    rest = lane - 24 * yd
    return rest >> 1, yd, rest & 1


def beside_1(v, lane, sub):
    a, b, gy = lane >> 6, (lane >> 4) & 3, lane & 15
    swapped = [roll(x, 64, 1) for x in v]
    result = []
    for gx in range(8):
        x = v[gx]
        total = swapped[gx] + jnp.where((gy & 1) == 0, roll(x, -1, 1), roll(x, 1, 1))
        if gx % 2 == 0:
            total = total + jnp.where(a == 1, swapped[gx + 1], 0.0)
        else:
            total = total + jnp.where(a == 0, swapped[gx - 1], 0.0)
        after = jnp.where((sub & 1) == 0, roll(roll(x, -1, 0), 48, 1), 0.0)
        before = jnp.where((sub & 1) == 1, roll(roll(x, 1, 0), -48, 1), 0.0)
        total = total + jnp.where(b < 3, roll(x, -16, 1), after)
        total = total + jnp.where(b > 0, roll(x, 16, 1), before)
        result.append(total)
    return result


def beside_2(v, lane, sub):
    b, gy = (lane >> 4) & 3, lane & 15
    result = []
    for gx in range(8):
        x = v[gx]
        total = jnp.where((gy & 2) == 0, roll(x, -2, 1), roll(x, 2, 1))
        if gx % 4 < 3:
            total = total + v[gx + 1]
        if gx % 4 > 0:
            total = total + v[gx - 1]
        after = jnp.where((sub & 3) < 3, roll(roll(x, -1, 0), 32, 1), 0.0)
        before = jnp.where((sub & 3) > 0, roll(roll(x, 1, 0), -32, 1), 0.0)
        total = total + jnp.where(b < 2, roll(x, -32, 1), after)
        total = total + jnp.where(b >= 2, roll(x, 32, 1), before)
        result.append(total)
    return result


def beside_3(v, lane, sub):
    gy = lane & 15
    result = []
    for gx in range(8):
        x = v[gx]
        total = jnp.where((gy & 4) == 0, roll(x, -4, 1), roll(x, 4, 1))
        if gx + 2 < 8:
            total = total + v[gx + 2]
        if gx - 2 >= 0:
            total = total + v[gx - 2]
        total = total + jnp.where(sub < 7, roll(x, -1, 0), 0.0)
        total = total + jnp.where(sub > 0, roll(x, 1, 0), 0.0)
        result.append(total)
    return result


def coarsen_1(v, lane):
    b, gy = (lane >> 4) & 3, lane & 15
    result = []
    for x in v:
        x = x + roll(x, 64, 1)
        x = x + jnp.where((b & 1) == 0, roll(x, -16, 1), roll(x, 16, 1))
        x = x + jnp.where((gy & 1) == 0, roll(x, -1, 1), roll(x, 1, 1))
        result.append(x)
    return result


def coarsen_2(v, lane):
    b, gy = (lane >> 4) & 3, lane & 15
    result = []
    for gx in range(8):
        x = v[gx] + v[gx ^ 1]
        x = x + jnp.where(b < 2, roll(x, -32, 1), roll(x, 32, 1))
        x = x + jnp.where((gy & 2) == 0, roll(x, -2, 1), roll(x, 2, 1))
        result.append(x)
    return result


def coarse_cycle(source, shift):
    lane, sub = iota((8, 128), 1), iota((8, 128), 0)
    eight = range(8)

    def remainder(beside, q, d, x):
        around = beside(x, lane, sub)
        return [q[i] - (d[i] * x[i] - around[i]) for i in eight]

    d1 = [6.0 + s for s in shift]
    shift2 = [0.125 * s for s in coarsen_1(shift, lane)]
    d2 = [6.0 + s for s in shift2]
    d3 = [6.0 + 0.125 * s for s in coarsen_2(shift2, lane)]
    w1 = [RELAX / d for d in d1]
    w2 = [RELAX / d for d in d2]
    w3 = [RELAX / d for d in d3]
    x1 = [w1[i] * source[i] for i in eight]
    q2 = [0.25 * t for t in coarsen_1(remainder(beside_1, source, d1, x1), lane)]
    x2 = [w2[i] * q2[i] for i in eight]
    q3 = [0.25 * t for t in coarsen_2(remainder(beside_2, q2, d2, x2), lane)]
    x3 = [w3[i] * q3[i] for i in eight]
    for _ in range(3):
        t3 = remainder(beside_3, q3, d3, x3)
        x3 = [x3[i] + w3[i] * t3[i] for i in eight]
    x2 = [x2[i] + x3[i] for i in eight]
    t2 = remainder(beside_2, q2, d2, x2)
    x2 = [x2[i] + w2[i] * t2[i] for i in eight]
    x1 = [x1[i] + x2[i] for i in eight]
    t1 = remainder(beside_1, source, d1, x1)
    return [x1[i] + w1[i] * t1[i] for i in eight]


def place_correction(coarse, place_ref, pad_ref, rows_ref, out_ref):
    gx0, gy0, gz0 = place_ref[0], place_ref[1], place_ref[2]
    pad_ref[...] = jnp.zeros_like(pad_ref)
    for gx in range(8):
        pad_ref[gx + 1, 8:16, :] = coarse[gx]
    rows_ref[...] = jnp.zeros_like(rows_ref)
    for e in range(3):
        for d in range(3):
            rows_ref[3 * e + d : 3 * e + d + 1, :] = pad_ref[gx0 + d, pl.ds(gz0 + 7 + e, 1), :]
    shape = (128, 512)
    source = iota(shape, 0)
    column = iota(shape, 1)
    target = column & 127
    yd = (target * 171) >> 12
    x = (target - 24 * yd) >> 1
    hit = ((source >> 4) & 3) == (column >> 7)
    hit = hit & ((source >> 6) == ((x >> 1) & 1))
    hit = hit & ((source & 15) == gy0 - 2 + yd) & (target < 120)
    spread = dot(rows_ref[...], jnp.where(hit, 1.0, 0.0))
    lane_x, _, _ = lane_places((1, 128))
    part = lane_x >> 2
    for t in range(8):
        e, b = (t + 2) // 4, (t + 2) % 4
        pieces = [spread[3 * e + d : 3 * e + d + 1, 128 * b : 128 * b + 128] for d in range(3)]
        row = jnp.where(part == 0, pieces[0], jnp.where(part == 1, pieces[1], pieces[2]))
        out_ref[2 * t : 2 * t + 1, :] = row
        out_ref[2 * t + 1 : 2 * t + 2, :] = row


def groups(values):
    return [values[8 * g : 8 * g + 8] for g in range(8)]


def packed_places(shape):
    lane = iota(shape, len(shape) - 1)
    rest = (lane & 63) + 4
    yd = 1 + ((rest * 171) >> 12)
    rest = rest - 24 * (yd - 1)
    return rest >> 1, yd, rest & 1, lane >> 6


def dense(values, marks, packed_ref):
    first = values.astype(jnp.bfloat16)
    rest = values - first.astype(F32)
    second = rest.astype(jnp.bfloat16)
    third = (rest - second.astype(F32)).astype(jnp.bfloat16)
    stack = jnp.concatenate([first, second, third, first, second, first], axis=0)
    products = jnp.dot(packed_ref[...], stack, preferred_element_type=F32)
    result = []
    for part, row in enumerate(marks):
        row = jnp.broadcast_to(row, (8, 128))
        columns = slice(128 * part, 128 * part + 128)
        chosen = [products[8 * g : 8 * g + 8, columns] for g in range(8)]
        for k in range(1, CLASSES):
            hit = row == k
            for g in range(8):
                at = 64 * k + 8 * g
                chosen[g] = jnp.where(hit, products[at : at + 8, columns], chosen[g])
        result.append(chosen)
    return result


class Full:
    def __init__(self, slab):
        self.parts = groups(slab)
        self.yi = lane_places((8, 128))[2]

    def here(self, g):
        return self.parts[g]

    def shift(self, g, step):
        return roll(self.parts[g], -step, 1)


class Pack:
    def __init__(self, low, high):
        self.low, self.high = groups(low), groups(high)
        self.yi = packed_places((8, 128))[2]

    def here(self, g):
        return self.shift(g, 0)

    def shift(self, g, step):
        lane = iota((8, 128), 1)
        return jnp.where(lane < 64, roll(self.low[g], -28 - step, 1), roll(self.high[g], 36 - step, 1))


class Block(Full):
    def __init__(self, block):
        self.parts = groups(block)
        self.yi = packed_places((8, 128))[2]


def upward_y(view, g):
    return jnp.where(view.yi == 0, view.shift(g, 1), view.shift(g, 23))


def downward_y(view, g):
    return jnp.where(view.yi == 1, view.shift(g, -1), view.shift(g, -23))


def face_weights_of(weights_ref):
    sub = iota((8, 128), 0)
    wx, wy, wz = weights_ref[0], weights_ref[1], weights_ref[2]
    top = jnp.where((sub & 3) == 3, wz, 0.0), jnp.where(sub >= 4, wy, 0.0)
    bottom = jnp.where((sub & 3) == 0, wz, 0.0), jnp.where(sub < 4, wy, 0.0)
    return wx, top, bottom


def coupling(before, view, after, weights_ref):
    wx, (wz_top, wy_top), (wz_bottom, wy_bottom) = face_weights_of(weights_ref)
    result = []
    for g in range(8):
        term = wz_top * roll(after[g], 3, 0) + wz_bottom * roll(before[g], -3, 0)
        if g % 2 == 1:
            term = term + wy_top * roll(upward_y(view, g - 1), 4, 0)
        else:
            term = term + wy_bottom * roll(downward_y(view, g + 1), 4, 0)
        if g >= 6:
            term = term + wx * view.shift(g - 6, 2)
        if g < 2:
            term = term + wx * view.shift(g + 6, -2)
        result.append(term)
    return result


def constant_coupling(before, here, after, yi, weights_ref):
    wx, (wz_top, wy_top), (wz_bottom, wy_bottom) = face_weights_of(weights_ref)

    def wide(row):
        return jnp.broadcast_to(row, (8, 128))

    here = wide(here)
    up = jnp.where(yi == 0, roll(here, -1, 1), roll(here, -23, 1))
    down = jnp.where(yi == 1, roll(here, 1, 1), roll(here, 23, 1))
    along = wz_top * wide(after) + wz_bottom * wide(before)
    even, odd = along + wy_bottom * down, along + wy_top * up
    result = [even if g % 2 == 0 else odd for g in range(8)]
    for g in (0, 1):
        result[g] = result[g] + wx * roll(here, 2, 1)
    for g in (6, 7):
        result[g] = result[g] + wx * roll(here, -2, 1)
    return result


def block_before(ref, j):
    return ref[j - 1] if j > 0 else roll(ref[5], 64, 1)


def block_after(ref, j):
    return ref[j + 1] if j < 5 else roll(ref[0], 64, 1)


def restrict(source_ref, inverse_ref, sums_ref, weights_ref, all_ref, out_ref):
    wx, (wz_top, wy_top), (wz_bottom, wy_bottom) = face_weights_of(weights_ref)
    _, _, yi, _ = packed_places((8, 128))
    totals = []
    out_ref[...] = jnp.zeros_like(out_ref)
    for j in range(6):
        r = source_ref[j]
        x = inverse_ref[j] * r
        d = groups(r - sums_ref[j] * x)
        xs = groups(x)
        even = (xs[0] + xs[2]) + (xs[4] + xs[6])
        odd = (xs[1] + xs[3]) + (xs[5] + xs[7])
        local = ((d[0] + d[1]) + (d[2] + d[3])) + ((d[4] + d[5]) + (d[6] + d[7]))
        local = local + wx * (roll(xs[0] + xs[1], -2, 1) + roll(xs[6] + xs[7], 2, 1))
        upper, lower = wy_top * odd, wy_bottom * even
        totals.append(local + jnp.where(yi == 0, roll(lower, -1, 1), roll(upper, 1, 1)))
        all_ref[j] = even + odd
        out_ref[8 + j : 9 + j, :] = jnp.sum(jnp.where(yi == 1, upper, 0.0), axis=0, keepdims=True)
        out_ref[16 + j : 17 + j, :] = jnp.sum(jnp.where(yi == 0, lower, 0.0), axis=0, keepdims=True)
    for j in range(6):
        value = totals[j] + wz_bottom * block_after(all_ref, j) + wz_top * block_before(all_ref, j)
        out_ref[j : j + 1, :] = jnp.sum(value, axis=0, keepdims=True)


def payload(cells, place_ref, scale):
    shape = (128, 256)
    source, column = iota(shape, 0), iota(shape, 1)
    own = (source & 63) - 28
    hit = (own >= 0) & (own < 8) & ((source >> 6) == (column >> 7)) & ((own >> 2) == ((column & 127) >> 6))
    spread = dot(cells, jnp.where(hit, scale, 0.0))
    block, column = iota((8, 256), 0), iota((8, 256), 1)
    z = block - 2 + 6 * (column >> 7)
    keep = (block < 6) & (z >= 0) & (z < 8) & ((z >> 1) == ((column >> 4) & 3))
    gy, gy0 = column & 15, place_ref[1]
    value = jnp.where(gy == gy0, spread[0:8], jnp.where(gy == gy0 + 1, spread[8:16], 0.0))
    value = value + jnp.where(gy == gy0 - 1, spread[16:24], 0.0)
    row = jnp.sum(jnp.where(keep, value, 0.0), axis=0, keepdims=True)
    return row[:, 0:128] + row[:, 128:256]


def gather_own(planes):
    lane = iota((64, 128), 1)
    result = jnp.zeros((64, 128), F32)
    for z, (plane, first) in enumerate(planes):
        result = jnp.where((lane >> 3) == z, roll(plane, 8 * z - first, 1), result)
    return result


def own_of_packed(blocks):
    return gather_own([(blocks[z + 2], 28) if z < 4 else (blocks[z - 4], 92) for z in range(8)])


def own_rows(first, second, first_ref, second_ref):
    turned = jnp.concatenate([first, second], axis=0).T
    low = iota((8, 128), 1) < 64
    for pair in range(4):
        even = turned[16 * pair : 16 * pair + 8]
        odd = turned[16 * pair + 8 : 16 * pair + 16]
        columns = slice(128 * pair, 128 * pair + 128)
        first_ref[:, columns] = jnp.where(low, even, roll(odd, 64, 1))
        second_ref[:, columns] = jnp.where(low, roll(even, 64, 1), odd)


def coefficients(rows, table_ref):
    halves = []
    for row in rows:
        wide = jnp.broadcast_to(row, (CLASSES, 128))
        halves.append(jnp.where(wide == iota((CLASSES, 128), 0), 1.0, 0.0))
    onehot = jnp.concatenate(halves, axis=1)
    onehot = jnp.concatenate([onehot] * 3, axis=0).astype(jnp.bfloat16)
    return jnp.dot(table_ref[...], onehot, preferred_element_type=F32)


def relaxation(x, yd, slab, place_ref):
    gx, gy = place_ref[0] - 1 + (x >> 2), place_ref[1] - 2 + yd
    gz = place_ref[2] - 1 + ((slab + 4) >> 3)
    inside = (gx >= 0) & (gx < 8) & (gy >= 0) & (gy < 16) & (gz >= 0) & (gz < 8) & (yd < 5)
    return jnp.where(inside, RELAX, 0.0)


def total(values):
    return jnp.sum(jnp.sum(values, axis=0, keepdims=True), axis=1, keepdims=True)


def own_right(own_ref):
    return jnp.concatenate([own_ref[:, 0:256], own_ref[:, 384:640]], axis=1)


def split(values):
    first = values.astype(jnp.bfloat16).astype(F32)
    rest = values - first
    second = rest.astype(jnp.bfloat16).astype(F32)
    return first, second, rest - second


def cell_parts(own_ref, table, weights_ref, shift_ref):
    pieces = []
    for pair in range(4):
        start = 128 * pair if pair < 2 else 128 * pair + 128
        values = own_ref[:, start : start + 128]
        pieces += [values, roll(values, 64, 1)]
    b = jnp.concatenate(pieces + [jnp.zeros((64, 128), F32)], axis=0).T[0:64]
    turned = jnp.concatenate([own_ref[:, 256:384], jnp.zeros((120, 128), F32)], axis=0).T
    lane = iota((1, 128), 1)
    marks = jnp.zeros((1, 128), F32)
    for z in range(8):
        marks = jnp.where((lane >> 3) == z, roll(turned[z : z + 1], 8 * z, 1), marks)
    marks = marks.astype(jnp.int32)
    both = coefficients([marks], table)
    x0 = (RELAX / both[:64]) * b
    d, xs = groups(b - both[64:] * x0), groups(x0)
    wx, wy, wz = weights_ref[0], weights_ref[1], weights_ref[2]
    sub = iota((8, 128), 0)
    even = (xs[0] + xs[2]) + (xs[4] + xs[6])
    odd = (xs[1] + xs[3]) + (xs[5] + xs[7])
    every = even + odd

    def along(values):
        return jnp.sum(values, axis=0, keepdims=True)

    local = along(((d[0] + d[1]) + (d[2] + d[3])) + ((d[4] + d[5]) + (d[6] + d[7])))
    x_low, x_high = wx * along(xs[0] + xs[1]), wx * along(xs[6] + xs[7])
    y_low, y_high = wy * along(jnp.where(sub < 4, even, 0.0)), wy * along(jnp.where(sub >= 4, odd, 0.0))
    z_low = wz * along(jnp.where((sub & 3) == 0, every, 0.0))
    z_high = wz * along(jnp.where((sub & 3) == 3, every, 0.0))
    x, yi, z = (lane >> 1) & 3, lane & 1, lane >> 3
    local = local + jnp.where(x > 0, roll(x_high, 2, 1), 0.0) + jnp.where(x < 3, roll(x_low, -2, 1), 0.0)
    local = local + jnp.where(yi == 1, roll(y_high, 1, 1), roll(y_low, -1, 1))
    local = local + jnp.where(z > 0, roll(z_high, 8, 1), 0.0) + jnp.where(z < 7, roll(z_low, -8, 1), 0.0)
    shifts = jnp.zeros((1, 128), F32)
    for k in range(CLASSES):
        shifts = jnp.where(marks == k, shift_ref[k], shifts)
    scale = 1.0 / NODES
    return jnp.concatenate(
        [
            scale * local,
            scale * jnp.where(yi == 1, y_high, 0.0),
            scale * jnp.where(yi == 0, y_low, 0.0),
            0.125 * shifts,
            scale * jnp.where(x == 3, x_high, jnp.where(x == 0, x_low, 0.0)),
            scale * jnp.where(z == 7, z_high, jnp.where(z == 0, z_low, 0.0)),
            jnp.zeros((2, 128), F32),
        ],
        axis=0,
    )


def front_kernel(
    place_ref, weights_ref, shift_ref, right_ref, marks_ref, blocks_ref,
    own_ref, table_ref, payload_ref,
):
    own_ref[:, 256:384] = jnp.zeros((8, 128), F32)
    for x in range(4):
        rows = slice(2 * x, 2 * x + 2)
        values = right_ref[x]
        own_ref[rows, 0:256] = values[:, 0:256]
        own_ref[rows, 384:640] = values[:, 256:512]
        own_ref[rows, 256:264] = marks_ref[x].astype(F32)
    diagonal = jnp.where(iota((64, 64), 0) == iota((64, 64), 1), 1.0, 0.0)
    rows = []
    for k in range(CLASSES):
        block = blocks_ref[k]
        diag = jnp.sum(block * diagonal, axis=0, keepdims=True)
        rows.append(jnp.concatenate([diag, jnp.sum(block, axis=0, keepdims=True)], axis=1))
    parts = split(jnp.concatenate(rows, axis=0))
    table = jnp.concatenate(list(parts) + [jnp.zeros((80, 128), F32)], axis=0).T
    table_ref[...] = table[:, 0:48].astype(jnp.bfloat16)

    parts = cell_parts(own_ref, table_ref, weights_ref, shift_ref)
    shape = (128, 128)
    source, target = iota(shape, 0), iota(shape, 1)
    hit = (source < 64) & (((source >> 2) & 1) == (target >> 6)) & ((source >> 4) == ((target >> 4) & 3))
    cells = dot(parts, jnp.where(hit, 1.0, 0.0))
    lane = iota((1, 128), 1)
    b, gy, gy0 = (lane >> 4) & 3, lane & 15, place_ref[1]
    row = jnp.where(gy == gy0, cells[0:1], jnp.where(gy == gy0 + 1, cells[1:2], 0.0))
    row = row + jnp.where(gy == gy0 - 1, cells[2:3], 0.0)
    row = row + jnp.where(gy == ((gy0 + 8) & 15), cells[3:4], 0.0)
    row = row + jnp.where(gy == ((gy0 + 4) & 15), roll(cells[4:5], 64, 1), 0.0)
    far = gy == ((gy0 + 12) & 15)
    row = row + jnp.where(far & (b == 0), roll(cells[5:6], -48, 1), 0.0)
    payload_ref[...] = row + jnp.where(far & (b == 3), roll(cells[5:6], 48, 1), 0.0)


def rotate(values, step):
    gy = iota(values.shape, 1) & 15
    return jnp.where(gy + step < 16, roll(values, -step, 1), roll(values, 16 - step, 1))


def join_parts(gathered_ref):
    lane, sub = iota((8, 128), 1), iota((8, 128), 0)
    a, b = lane >> 6, (lane >> 4) & 3
    result = []
    for gx in range(8):
        value = gathered_ref[gx, :, 0:128]
        if gx > 0:
            value = value + jnp.where(a == 0, rotate(gathered_ref[gx - 1, :, 256:384], 4), 0.0)
        if gx < 7:
            value = value + jnp.where(a == 1, rotate(gathered_ref[gx + 1, :, 256:384], 4), 0.0)
        z = rotate(gathered_ref[gx, :, 384:512], 12)
        value = value + jnp.where((b == 0) & (sub > 0), roll(z, 1, 0), 0.0)
        value = value + jnp.where((b == 3) & (sub < 7), roll(z, -1, 0), 0.0)
        result.append(value)
    return result


def pack_kernel(blocks_ref, packed_ref):
    low = iota((64, 128), 1) < 64
    for k in range(CLASSES):
        block = blocks_ref[k]
        first, second, third = split(jnp.concatenate([block, block], axis=1))
        at = slice(64 * k, 64 * k + 64)
        packed_ref[at, 0:128] = first.astype(jnp.bfloat16)
        packed_ref[at, 128:256] = jnp.where(low, first, second).astype(jnp.bfloat16)
        packed_ref[at, 256:384] = jnp.where(low, second, third).astype(jnp.bfloat16)


def coefficient_kernel(place_ref, below_ref, here_ref, above_ref, table_ref, class_ref, inverse_ref, sums_ref):
    marks = jnp.concatenate([below_ref[4:24, 0:128], here_ref[:, 0:128], above_ref[0:20, 0:128]], axis=0)
    marks = jnp.concatenate([marks, marks], axis=0).T[0:16].astype(jnp.int32)
    low = iota((1, 128), 1) < 64
    class_ref[...] = jnp.zeros((8, 128), jnp.int32)
    x, yd, _, half = packed_places((1, 128))
    for j in range(6):
        class_ref[j : j + 1, :] = jnp.where(low, marks[2 + j : 3 + j], marks[8 + j : 9 + j])
    for j in (0, 2, 4):
        both = coefficients([class_ref[j : j + 1, :], class_ref[j + 1 : j + 2, :]], table_ref)
        for part in range(2):
            columns = slice(128 * part, 128 * part + 128)
            relax = relaxation(x, yd, 2 + j + part + 6 * half, place_ref)
            inverse_ref[j + part] = relax / both[:64, columns]
            sums_ref[j + part] = both[64:, columns]


def local_kernel(
    place_ref, weights_ref, below_ref, here_ref, above_ref, table_ref, packed_ref,
    smooth_ref, inverse_ref, keep_ref,
    field_ref, iterate_ref, class_ref,
):
    def turned(block):
        columns = slice(128 * block, 128 * block + 128)
        middle = [ref[:, columns] for ref in (below_ref, here_ref, above_ref)]
        return jnp.concatenate([jnp.zeros((24, 128), F32)] + middle + [jnp.zeros((32, 128), F32)], axis=0).T

    class_ref[...] = turned(0)[0:16].astype(jnp.int32)
    x, yd, _ = lane_places((1, 128))
    for pair in range(SLABS // 2):
        block = turned(pair + 1)
        both = coefficients([class_ref[2 * pair + i : 2 * pair + i + 1, :] for i in (0, 1)], table_ref)
        for part in range(2):
            s = 2 * pair + part
            columns = slice(128 * part, 128 * part + 128)
            values = block[64 * part : 64 * part + 64]
            inverse = relaxation(x, yd, s, place_ref) / both[:64, columns]
            field_ref[s] = values
            inverse_ref[s] = inverse
            keep_ref[s] = 1.0 - inverse * both[64:, columns]
            iterate_ref[s] = inverse * values
    for s in (0, 15):
        smooth_ref[s] = jnp.zeros((64, 128), F32)
    for s in range(1, 14, 2):
        planes = [iterate_ref[s + i] for i in (-1, 0, 1, 2)]
        marks = [class_ref[s + i : s + i + 1, :] for i in (0, 1)]
        chosen = dense(jnp.concatenate(planes[1:3], axis=1), marks, packed_ref)
        for part in range(2):
            faces = coupling(groups(planes[part]), Full(planes[part + 1]), groups(planes[part + 2]), weights_ref)
            for g in range(8):
                at = (s + part, slice(8 * g, 8 * g + 8))
                value = chosen[part][g] - faces[g]
                smooth_ref[at] = iterate_ref[at] + inverse_ref[at] * (field_ref[at] - value)


def first_kernel(
    place_ref, weights_ref, gathered_ref, local_ref, inverse_ref, keep_ref, class_ref, near_inverse_ref, sums_ref,
    packed_ref, right_ref,
    image_ref, edge_ref, own_direction_ref, own_image_ref, payload_ref,
    smooth_ref, pad_ref, rows_ref, shift_ref, all_ref, cells_ref,
):
    coarse = coarse_cycle(join_parts(gathered_ref), [rotate(gathered_ref[g, :, 128:256], 8) for g in range(8)])
    place_correction(coarse, place_ref, pad_ref, rows_ref, shift_ref)
    _, _, yi = lane_places((8, 128))
    for s in range(1, 15):
        here = shift_ref[s : s + 1, :]
        faces = constant_coupling(shift_ref[s - 1 : s, :], here, shift_ref[s + 1 : s + 2, :], yi, weights_ref)
        here = jnp.broadcast_to(here, (8, 128))
        for g in range(8):
            at = (s, slice(8 * g, 8 * g + 8))
            smooth_ref[at] = local_ref[at] + (keep_ref[at] * here + inverse_ref[at] * faces[g])

    lane = iota((64, 128), 1)

    def block(j):
        return jnp.where(lane < 64, roll(smooth_ref[2 + j], -28, 1), roll(smooth_ref[8 + j], 36, 1))

    blocks = [block(j) for j in range(-1, 7)]
    for j in (0, 2, 4):
        marks = [class_ref[j + i : j + i + 1, :] for i in (0, 1)]
        chosen = dense(jnp.concatenate([blocks[j + 1], blocks[j + 2]], axis=1), marks, packed_ref)
        for part in range(2):
            at = j + part
            view = Pack(smooth_ref[2 + at], smooth_ref[8 + at])
            faces = coupling(groups(blocks[at]), view, groups(blocks[at + 2]), weights_ref)
            for g in range(8):
                image_ref[at, 8 * g : 8 * g + 8] = chosen[part][g] - faces[g]
    edge = jnp.zeros((64, 128), F32)
    for i in range(10):
        j, half = (i + 1) % 6, (i + 1) // 6
        taken = (lane >= 12 * i) & (lane < 12 * i + 12)
        edge = jnp.where(taken, roll(image_ref[j], 12 * i - 26 - 64 * half, 1), edge)
    edge_ref[...] = edge
    restrict(image_ref, near_inverse_ref, sums_ref, weights_ref, all_ref, cells_ref)
    row = payload(cells_ref[...], place_ref, 1.0 / NODES)
    own_z = gather_own([(smooth_ref[z + 4], 56) for z in range(8)])
    own_rows(own_z, own_of_packed(image_ref), own_direction_ref, own_image_ref)
    direction = own_direction_ref[...]
    lane = iota((1, 128), 1)
    gamma, delta = total(own_right(right_ref) * direction), total(direction * own_image_ref[...])
    far = (lane & 15) == ((place_ref[1] + 8) & 15)
    row = row + jnp.where(far & ((lane >> 4) == 0), gamma, 0.0)
    payload_ref[...] = row + jnp.where(far & ((lane >> 4) == 1), delta, 0.0)


def from_edge(edge_ref, j, first):
    lane = iota((64, 128), 1)
    result = jnp.zeros((64, 128), F32)
    for half in range(2):
        i, start = j - 1 + 6 * half, first + 64 * half
        if 0 <= i < 10:
            taken = (lane >= start) & (lane < start + 12)
            result = jnp.where(taken, roll(edge_ref[...], start - 12 * i, 1), result)
    return result


def near_kernel(
    weights_ref, own_ref, below_ref, above_ref, class_ref, inverse_ref, packed_ref,
    smooth_ref,
    iterate_ref, image_ref,
):
    lane = iota((64, 128), 1) & 63
    for j in range(6):
        below, above = from_edge(below_ref, j, 2), from_edge(above_ref, j, 50)
        image_ref[j] = jnp.where(lane < 20, below, jnp.where(lane < 44, own_ref[j], above))
        iterate_ref[j] = inverse_ref[j] * image_ref[j]
    for j in (0, 2, 4):
        marks = [class_ref[j + i : j + i + 1, :] for i in (0, 1)]
        chosen = dense(jnp.concatenate([iterate_ref[j], iterate_ref[j + 1]], axis=1), marks, packed_ref)
        for part in range(2):
            at = j + part
            before, after = groups(block_before(iterate_ref, at)), groups(block_after(iterate_ref, at))
            faces = coupling(before, Block(iterate_ref[at]), after, weights_ref)
            for g in range(8):
                place = (at, slice(8 * g, 8 * g + 8))
                value = chosen[part][g] - faces[g]
                smooth_ref[place] = iterate_ref[place] + inverse_ref[place] * (image_ref[place] - value)


def second_kernel(
    place_ref, weights_ref, gathered_ref, shifts_ref, local_ref, class_ref, inverse_ref, sums_ref, packed_ref,
    right_ref, own_direction_ref, own_image_ref,
    residual_ref, smoothed_ref, applied_ref, known_ref, payload_ref,
    smooth_ref, pad_ref, rows_ref, shift_ref, turned_ref, image_ref, near_ref,
):
    coarse = coarse_cycle(
        [gathered_ref[g, :, 0:128] for g in range(8)], [rotate(shifts_ref[g, :, 128:256], 8) for g in range(8)]
    )
    place_correction(coarse, place_ref, pad_ref, rows_ref, shift_ref)
    lane = iota((8, 128), 1)
    near_ref[...] = jnp.where(lane < 64, roll(shift_ref[2:10, :], -28, 1), roll(shift_ref[8:16, :], 36, 1))
    _, _, yi, _ = packed_places((8, 128))

    def row(j):
        return near_ref[j : j + 1, :]

    for j in range(6):
        before = row(j - 1) if j > 0 else roll(row(5), 64, 1)
        after = row(j + 1) if j < 5 else roll(row(0), 64, 1)
        faces = constant_coupling(before, row(j), after, yi, weights_ref)
        here = jnp.broadcast_to(row(j), (8, 128))
        for g in range(8):
            at = (j, slice(8 * g, 8 * g + 8))
            inverse = inverse_ref[at]
            smooth_ref[at] = local_ref[at] + (here + inverse * (faces[g] - sums_ref[at] * here))

    own_y = own_of_packed(smooth_ref)
    own_marks = gather_own(
        [(jnp.broadcast_to(class_ref[j : j + 1, :].astype(F32), (64, 128)), first)
         for j, first in [(2, 28), (3, 28), (4, 28), (5, 28), (0, 92), (1, 92), (2, 92), (3, 92)]]
    )
    chosen = dense(own_y, [own_marks[0:1].astype(jnp.int32)], packed_ref)[0]
    for j in range(6):
        before, after = groups(block_before(smooth_ref, j)), groups(block_after(smooth_ref, j))
        faces = coupling(before, Block(smooth_ref[j]), after, weights_ref)
        for g in range(8):
            image_ref[j, 8 * g : 8 * g + 8] = faces[g]
    own_v = jnp.concatenate(chosen, axis=0) - own_of_packed(image_ref)

    sums = gathered_ref[0, :, 128:256]
    for g in range(1, 8):
        sums = sums + gathered_ref[g, :, 128:256]
    sums = jnp.sum(sums, axis=0, keepdims=True)
    slot = iota((1, 128), 1) >> 4
    gamma, delta = total(jnp.where(slot == 0, sums, 0.0)), total(jnp.where(slot == 1, sums, 0.0))
    lane = iota((1, 128), 1)
    known_ref[...] = jnp.where(lane == 0, gamma, jnp.where(lane == 1, delta, 0.0))
    step = gamma / delta
    own_rows(own_y, own_v, smoothed_ref, turned_ref)
    smoothed = own_direction_ref[...] - step * smoothed_ref[...]
    smoothed_ref[...] = smoothed
    applied = own_image_ref[...] - step * turned_ref[...]
    applied_ref[...] = applied
    residual = own_right(right_ref) - step * own_image_ref[...]
    residual_ref[...] = residual
    lane = iota((1, 128), 1)
    cross = own_direction_ref[...] * applied + own_image_ref[...] * smoothed
    values = jnp.where(lane == 0, total(residual * smoothed), 0.0)
    values = jnp.where(lane == 1, total(smoothed * applied), values)
    payload_ref[...] = jnp.where(lane == 2, total(cross), values)


def last_kernel(
    parts_ref, known_ref, direction_ref, own_image_ref, smoothed_ref, applied_ref, residual_ref, field_ref, out_ref
):
    totals = parts_ref[0]
    for gx in range(1, 8):
        totals = totals + parts_ref[gx]
    gamma, delta = known_ref[:, 0:1], known_ref[:, 1:2]
    beta = totals[:, 0:1] / gamma
    step = totals[:, 0:1] / (totals[:, 1:2] + beta * (totals[:, 2:3] + beta * delta))
    direction = direction_ref[...]
    field = (gamma / delta) * direction + step * (smoothed_ref[...] + beta * direction)
    residual = residual_ref[...] - step * (applied_ref[...] + beta * own_image_ref[...])
    for x in range(4):
        field_ref[x] = field[2 * x : 2 * x + 2]
        out_ref[x] = residual[2 * x : 2 * x + 2]


VMEM = pl.BlockSpec(memory_space=pltpu.VMEM)
SMEM = pl.BlockSpec(memory_space=pltpu.SMEM)


def call(body, scalars, out_shape, scratch, *args, flops=10**7):
    specs = [SMEM] * scalars + [VMEM] * (len(args) - scalars)
    shapes = [jax.ShapeDtypeStruct(shape, dtype) for shape, dtype in out_shape]
    return pl.pallas_call(
        body,
        out_shape=shapes,
        in_specs=specs,
        out_specs=[VMEM] * len(shapes),
        scratch_shapes=[pltpu.VMEM(shape, dtype) for shape, dtype in scratch],
        cost_estimate=pl.CostEstimate(flops=flops, bytes_accessed=10**6, transcendentals=0),
        compiler_params=pltpu.CompilerParams(vmem_limit_bytes=16 * 1024 * 1024),
    )(*args)


FIELD = ((SLABS, NODES, 128), F32)
BLOCKS = ((6, NODES, 128), F32)
MARKS = ((8, 128), jnp.int32)
OWN = ((8, 512), F32)
CELLS = ((8, 128), F32)
ROW = ((1, 128), F32)
COARSE_SCRATCH = [((10, 24, 128), F32), ((16, 128), F32), ((16, 128), F32)]
SUM_SCRATCH = [((6, 8, 128), F32), ((24, 128), F32)]
EDGE = ((NODES, 128), F32)
PAIR_FLOPS = 2 * 1024 * 384 * 256


def front_call(*args):
    return call(front_kernel, 3, [((8, 640), F32), ((128, 48), jnp.bfloat16), ROW], [], *args)


def pack_call(blocks):
    return call(pack_kernel, 0, [((CLASSES * NODES, 384), jnp.bfloat16)], [], blocks)[0]


def coefficient_call(*args):
    return call(coefficient_kernel, 1, [MARKS, BLOCKS, BLOCKS], [], *args)


def local_call(*args):
    scratch = [FIELD, FIELD, ((SLABS, 128), jnp.int32)]
    return call(local_kernel, 2, [FIELD, FIELD, FIELD], scratch, *args, flops=7 * PAIR_FLOPS)


def first_call(*args):
    scratch = [FIELD] + COARSE_SCRATCH + SUM_SCRATCH
    return call(first_kernel, 2, [BLOCKS, EDGE, OWN, OWN, ROW], scratch, *args, flops=3 * PAIR_FLOPS)


def near_call(*args):
    return call(near_kernel, 1, [BLOCKS], [BLOCKS, BLOCKS], *args, flops=3 * PAIR_FLOPS)[0]


def second_call(*args):
    scratch = [BLOCKS] + COARSE_SCRATCH + [OWN, BLOCKS, CELLS]
    return call(second_kernel, 2, [OWN, OWN, OWN, ROW, ROW], scratch, *args, flops=PAIR_FLOPS)


def shifted(x, axis, step):
    size = lax.axis_size(axis)
    pairs = [(i, i + step) for i in range(size) if 0 <= i + step < size]
    return lax.ppermute(x, axis, pairs)


def extend_xz(own):
    wide = jnp.concatenate([shifted(own, "gx", 1), own, shifted(own, "gx", -1)], axis=0)
    low = shifted(wide[:, 256:640], "gz", 1)
    high = shifted(wide[:, 0:384], "gz", -1)
    nothing = jnp.zeros((24, 112), F32)
    pieces = [low[:, 4:8], wide[:, 256:264], high[:, 256:260], nothing]
    return jnp.concatenate(pieces + [low[:, 128:384], wide[:, 0:256], wide[:, 384:640], high[:, 0:256]], axis=1)


def gather_cells(row, *offsets):
    parts = lax.all_to_all(jnp.broadcast_to(row[None], (128, 1, 128)), ("gy", "gz"), 0, 0, tiled=True)
    parts = parts.reshape(16, 8, 128)
    offset = (iota(parts.shape, 2) - iota(parts.shape, 0)) & 15
    near = (offset == 0) | (offset == 1) | (offset == 15)
    keeps = [near] + [offset == value for value in offsets]
    plane = jnp.concatenate([jnp.where(keep, parts, 0.0).sum(axis=0) for keep in keeps], axis=1)
    shape = (8,) + plane.shape
    return lax.all_to_all(jnp.broadcast_to(plane[None], shape), "gx", 0, 0, tiled=True)


def gather_sum(row):
    parts = lax.all_to_all(jnp.broadcast_to(row[None], (128, 1, 128)), ("gy", "gz"), 0, 0, tiled=True)
    part = parts.reshape(128, 128).sum(axis=0)
    return lax.all_to_all(jnp.broadcast_to(part[None, None], (8, 1, 128)), "gx", 0, 0, tiled=True)


def per_device(right_side, element_class, class_blocks, class_shift, face_weights):
    place = jnp.stack([lax.axis_index(axis) for axis in AXES]).astype(jnp.int32)
    own, table, row = front_call(place, face_weights, class_shift, right_side, element_class, class_blocks)
    gathered = gather_cells(row, 8, 4, 12)
    packed = pack_call(class_blocks)
    here = extend_xz(own)
    below, above = shifted(here, "gy", 1), shifted(here, "gy", -1)
    marks, near_inverse, sums = coefficient_call(place, below, here, above, table)
    local, inverse, keep = local_call(place, face_weights, below, here, above, table, packed)
    image, edge, direction, own_image, row = first_call(
        place, face_weights, gathered, local, inverse, keep, marks, near_inverse, sums, packed, own
    )
    again = gather_cells(row, 8)
    from_below, from_above = shifted(edge, "gy", 1), shifted(edge, "gy", -1)
    near = near_call(face_weights, image, from_below, from_above, marks, near_inverse, packed)
    residual, smoothed, applied, known, row = second_call(
        place, face_weights, again, gathered, near, marks, near_inverse, sums, packed, own, direction, own_image
    )
    parts = gather_sum(row)
    shapes = [(right_side.shape, F32)] * 2
    return tuple(call(last_kernel, 0, shapes, [], parts, known, direction, own_image, smoothed, applied, residual))


def solution(mesh):
    in_specs = (P("gx", "gy", "gz"), P("gx", "gy", "gz"), P(), P(), P())
    out_specs = (P("gx", "gy", "gz"), P("gx", "gy", "gz"))
    return jax.shard_map(
        per_device, mesh=mesh, in_specs=in_specs, out_specs=out_specs, check_vma=False
    )
```
